32 devices in a mesh: gx: 4 (over y, x), gy: 8 (over z, core).
Axes of the slice: x: 2, y: 2, z: 4, core: 2. Of those that a mesh axis runs over, the one named last changes fastest.
Arguments:
- spatial_factor: float32 [16, 128, 32, 64], P('gx', 'gy'), may hold values from -60 to 60
- coupling: float32 [64, 64], replicated, may hold values from -1 to 5
- orient_factor: float32 [2048, 64], replicated, may hold values from -6 to 6
- directions: float32 [3, 2048], replicated, may hold values from -1 to 1, as said below
Outputs:
- new_spatial: float32 [16, 128, 32, 64], P('gx', 'gy')
- new_coupling: float32 [64, 64], replicated
- new_orient: float32 [2048, 64], replicated
The draws below stay inside these ranges and needn't reach their ends.
Inputs may be any that keep to these rules, and one draw needn't show every extreme that they name: `directions`: each column is a unit vector.
All inputs are finite; a program needn't handle non-finite values.
Results may differ from the reference program's by a relative error of at most 0.0003.
Values sent between devices are 32-bit elements; how exact they have to be, the bound alone decides.
No kernel may reach another device: no remote copies, remote signals or barrier semaphores. Data moves between devices by JAX's collectives and lax.ppermute only.
A program may use at most 64 MiB of HBM per device.

```python
import math
import jax
import jax.numpy as jnp
from jax import lax

R = 64
NO = 2048
STEPS = 2
NX = 16
NY = 128
NZ = 32


def draw_spatial_factor(key, part):
    across = jnp.arange(NX, dtype=jnp.float32)[:, None, None, None] / NX
    along = jnp.arange(NY, dtype=jnp.float32)[None, :, None, None] / NY
    base = jnp.clip(jax.random.normal(key, (NX, NY, NZ, R), jnp.float32), -6.0, 6.0)
    growth = across + along
    return base * jnp.exp(math.log(3.0) * growth)


def draw_coupling(key, part):
    first_key, second_key = jax.random.split(jax.random.fold_in(key, 11))
    diagonal = jnp.exp(jax.random.uniform(first_key, (R,), jnp.float32, math.log(2.0), math.log(4.0)))
    others = jnp.clip(jax.random.normal(second_key, (R, R), jnp.float32), -3.0, 3.0)
    identity = jnp.eye(R, dtype=jnp.float32)
    return others * (0.7 / math.sqrt(R)) * (1.0 - identity) + identity * diagonal[None, :]


def draw_directions(key, part):
    first_key, second_key = jax.random.split(jax.random.fold_in(key, 23))
    height = jax.random.uniform(first_key, (NO,), jnp.float32, -1.0, 1.0)
    azimuth = jax.random.uniform(second_key, (NO,), jnp.float32, -math.pi, math.pi)
    radius = jnp.sqrt(jnp.maximum(1.0 - height * height, 0.0))
    return jnp.stack([radius * jnp.cos(azimuth), radius * jnp.sin(azimuth), height])


def centred(stream_key, shape, width, limit, kind=jnp.bfloat16):
    array = jax.random.normal(stream_key, shape, jnp.float32) * width
    return jnp.minimum(jnp.maximum(array, -limit), limit).astype(kind)


def setup_inputs(seed: int = 0) -> dict:
    splits = jax.random.split(jax.random.key(seed), 5)
    spatial_factor = draw_spatial_factor(jax.random.fold_in(splits[4], 71), 0)
    coupling = draw_coupling(jax.random.fold_in(splits[4], 71), 0)
    orient_factor = centred(splits[2], (NO, R), 1.0, 6.0, jnp.float32)
    directions = draw_directions(jax.random.fold_in(splits[4], 71), 0)
    return {"spatial_factor": spatial_factor, "coupling": coupling, "orient_factor": orient_factor, "directions": directions}


courant = 0.3
tumble = 0.2
highest = lax.Precision.HIGHEST

def matmul(left, right):
    return jnp.matmul(left, right, precision=highest)

def motility(density):
    return 1.0 / (1.0 + density * density)

def orient_tables(orient, directions):
    e_plus = jnp.maximum(directions, 0.0)
    e_minus = jnp.maximum(-directions, 0.0)
    orient_count = orient.shape[0]
    c_plus = [matmul((orient * e_plus[dim_index][:, None]).T, orient) / orient_count for dim_index in range(3)]
    c_minus = [matmul((orient * e_minus[dim_index][:, None]).T, orient) / orient_count for dim_index in range(3)]
    mean_row = jnp.mean(orient, axis=0)
    return (e_plus, e_minus, c_plus, c_minus, mean_row)

def differences(padded):
    center = padded[1:-1, 1:-1]
    backward = [center - padded[:-2, 1:-1], center - padded[1:-1, :-2], center - jnp.roll(center, 1, 2)]
    forward = [padded[2:, 1:-1] - center, padded[1:-1, 2:] - center, jnp.roll(center, -1, 2) - center]
    return (backward, forward)

def drift_term(flux_ext, c_plus, c_minus):
    backward, forward = differences(flux_ext)
    summed = jnp.zeros(backward[0].shape, jnp.float32)
    for dim_index in range(3):
        summed = summed + matmul(backward[dim_index], c_plus[dim_index]) - matmul(forward[dim_index], c_minus[dim_index])
    return summed

def k_update(k_center, rho_center, flux_ext, c_plus, c_minus, mean_row):
    return k_center - courant * drift_term(flux_ext, c_plus, c_minus) + tumble * (rho_center[..., None] * mean_row - k_center)

def projections(base, speed_ext):
    rank_width = base.shape[-1]
    rows_flat = base.reshape(-1, rank_width)
    backward, forward = differences(speed_ext)
    return jnp.stack([matmul(rows_flat.T, member.reshape(-1, rank_width)) for member in backward + forward])

def orient_update(start_coupling, orient, galerkin, e_plus, e_minus, c_plus, c_minus, mean_row):
    mid_coupling = start_coupling - tumble * (jnp.outer(matmul(start_coupling, mean_row), mean_row) - start_coupling)
    for dim_index in range(3):
        mid_coupling = mid_coupling + courant * (matmul(matmul(galerkin[dim_index], start_coupling), c_plus[dim_index]) - matmul(matmul(galerkin[dim_index + 3], start_coupling), c_minus[dim_index]))
    l_matrix = matmul(orient, mid_coupling.T)
    l_next = l_matrix + tumble * (jnp.mean(l_matrix, axis=0)[None, :] - l_matrix)
    for dim_index in range(3):
        l_next = l_next - courant * (e_plus[dim_index][:, None] * matmul(l_matrix, galerkin[dim_index].T) - e_minus[dim_index][:, None] * matmul(l_matrix, galerkin[dim_index + 3].T))
    chol_lower = jnp.linalg.cholesky(matmul(l_next.T, l_next) / l_next.shape[0])
    new_orient = lax.linalg.triangular_solve(chol_lower, l_next, left_side=False, lower=True, transpose_a=True)
    return (chol_lower, new_orient)

def wrap_pad(field):
    return jnp.pad(field, ((1, 1), (1, 1), (0, 0), (0, 0)), mode='wrap')

def reference(spatial_factor, coupling, orient_factor, directions):
    spatial = spatial_factor
    orient = orient_factor
    rank_width = spatial.shape[-1]
    cell_count = NX * NY * NZ
    for step_index in range(STEPS):
        e_plus, e_minus, c_plus, c_minus, mean_row = orient_tables(orient, directions)
        k_matrix = matmul(spatial, coupling)
        density = matmul(k_matrix, mean_row)
        flux_ext = wrap_pad(motility(density)[..., None] * k_matrix)
        k_next = k_update(k_matrix, density, flux_ext, c_plus, c_minus, mean_row)
        rows_flat = k_next.reshape(-1, rank_width)
        chol_lower = jnp.linalg.cholesky(matmul(rows_flat.T, rows_flat) / cell_count)
        new_spatial = lax.linalg.triangular_solve(chol_lower, rows_flat, left_side=False, lower=True, transpose_a=True).reshape(k_next.shape)
        speed_ext = wrap_pad(motility(matmul(k_next, mean_row))[..., None] * new_spatial)
        galerkin = projections(new_spatial, speed_ext) / cell_count
        coupling, orient = orient_update(chol_lower.T, orient, galerkin, e_plus, e_minus, c_plus, c_minus, mean_row)
        spatial = new_spatial
    return (spatial, coupling, orient)
```

```python
import jax
import jax.numpy as jnp
from jax import lax
from jax.sharding import PartitionSpec as P

STEPS = 2

courant = 0.3
tumble = 0.2
highest = lax.Precision.HIGHEST


def mm(left, right, contract=(1, 0)):
    return lax.dot_general(
        left, right, (((contract[0],), (contract[1],)), ((), ())),
        precision=highest, preferred_element_type=jnp.float32,
    )


def shifted(axis, up):
    count = lax.axis_size(axis)
    step = 1 if up else count - 1
    return [(i, (i + step) % count) for i in range(count)]


def all_sum(part):
    count = lax.axis_size("gx") * lax.axis_size("gy")
    flat = part.reshape(-1, part.shape[-1])
    rows = flat.shape[0]
    padded = -(-rows // count) * count
    if padded != rows:
        flat = jnp.pad(flat, ((0, padded - rows), (0, 0)))
    split = flat.reshape(count, padded // count, flat.shape[-1])
    mine = lax.all_to_all(split, ("gx", "gy"), 0, 0).sum(axis=0)
    every = lax.all_to_all(jnp.broadcast_to(mine[None], split.shape), ("gx", "gy"), 0, 0)
    return every.reshape(padded, -1)[:rows].reshape(part.shape)


def y_layer(field, dims, index):
    lx, ly, lz = dims
    return field.reshape(-1, lx, ly, lz)[:, :, index].reshape(-1, lx * lz)


def halo(field, dims, both):
    lx, ly, lz = dims
    slab = ly * lz
    x_ahead = lax.ppermute(field[:, :slab], "gx", shifted("gx", False))
    y_ahead = lax.ppermute(y_layer(field, dims, 0), "gy", shifted("gy", False))
    x_behind = lax.ppermute(field[:, -slab:], "gx", shifted("gx", True))
    y_behind = lax.ppermute(y_layer(field, dims, ly - 1), "gy", shifted("gy", True))
    return x_behind, x_ahead, y_behind, y_ahead


def ahead(field, dims, x_ahead, y_ahead):
    lx, ly, lz = dims
    cube = field.reshape(-1, lx, ly, lz)
    over_x = jnp.concatenate([cube[:, 1:], x_ahead.reshape(-1, 1, ly, lz)], axis=1)
    over_y = jnp.concatenate([cube[:, :, 1:], y_ahead.reshape(-1, lx, 1, lz)], axis=2)
    over_z = jnp.roll(cube, -1, 3)
    return [m.reshape(field.shape) for m in (over_x, over_y, over_z)]


def behind(field, dims, x_behind, y_behind):
    lx, ly, lz = dims
    cube = field.reshape(-1, lx, ly, lz)
    over_x = jnp.concatenate([x_behind.reshape(-1, 1, ly, lz), cube[:, :-1]], axis=1)
    over_y = jnp.concatenate([y_behind.reshape(-1, lx, 1, lz), cube[:, :, :-1]], axis=2)
    over_z = jnp.roll(cube, 1, 3)
    return [m.reshape(field.shape) for m in (over_x, over_y, over_z)]


def motility(density):
    return 1.0 / (1.0 + density * density)


def tables(orient, e_plus, e_minus):
    count = orient.shape[1]
    plus = [mm(orient * e_plus[d][None], orient, (1, 1)) / count for d in range(3)]
    minus = [mm(orient * e_minus[d][None], orient, (1, 1)) / count for d in range(3)]
    return plus, minus, jnp.sum(orient, axis=1, keepdims=True) / count


def stage_weights(plus, minus, mean, into):
    rank = mean.shape[0]
    total = plus[0] + plus[1] + plus[2] + minus[0] + minus[1] + minus[2]
    first = (1.0 - tumble) * jnp.eye(rank, dtype=jnp.float32) + tumble * mean * mean.T
    blocks = [first, -courant * total]
    for d in range(3):
        blocks += [courant * plus[d], courant * minus[d]]
    weights = mm(jnp.concatenate(blocks, axis=0), into)
    weights = jnp.concatenate(jnp.split(weights, 8, axis=0), axis=1)
    return weights, mm(mean, into, (0, 0))


def k_stage(field, halos, dims, weights, density_row):
    x_behind, x_ahead, y_behind, y_ahead = [motility(mm(density_row, h)) * h for h in halos]
    flux = motility(mm(density_row, field)) * field
    later = ahead(flux, dims, x_ahead, y_ahead)
    before = behind(flux, dims, x_behind, y_behind)
    stack = [field, flux]
    for d in range(3):
        stack += [before[d], later[d]]
    return mm(weights, jnp.concatenate(stack, axis=0))


def galerkin(k_next, dims, x_ahead, y_ahead, mean):
    speed = motility(mm(mean, k_next, (0, 0)))
    q = speed * k_next
    later = ahead(k_next, dims, x_ahead, y_ahead)
    parts = [mm(k_next, jnp.concatenate([k_next, q], axis=0), (1, 1))]
    for moved in later:
        moved_speed = motility(mm(mean, moved, (0, 0)))
        parts.append(mm(moved, jnp.concatenate([moved_speed * k_next, q], axis=0), (1, 1)))
    return jnp.stack(parts)


def factor(gram):
    lower = jnp.linalg.cholesky(gram)
    inverse = lax.linalg.triangular_solve(
        lower, jnp.eye(gram.shape[0], dtype=jnp.float32), left_side=True, lower=True
    )
    return lower, inverse


def orient_stage(sums, cells, orient, plus, minus, mean, e_plus, e_minus):
    rank, count = orient.shape
    sums = sums / cells
    gram, d_sum = sums[0, :, :rank], sums[0, :, rank:]
    lower, inverse = factor(gram)
    upper = lower.T
    drift = jnp.zeros_like(gram)
    back, fore = [], []
    for d in range(3):
        back.append(d_sum - sums[1 + d, :, rank:])
        fore.append(sums[1 + d, :, :rank].T - d_sum)
        drift = drift + mm(back[d], plus[d]) - mm(fore[d], minus[d])
    mid = (1.0 + tumble) * upper - tumble * mm(upper, mean) * mean.T + courant * mm(inverse, drift)
    solved = mm(inverse, mid, (0, 0))
    rows = [(1.0 - tumble) * mid]
    for d in range(3):
        rows += [-courant * mm(inverse, mm(back[d], solved)), courant * mm(inverse, mm(fore[d], solved))]
    moved = mm(jnp.concatenate(rows, axis=0), orient).reshape(7, rank, count)
    new = moved[0] + tumble * mm(mid, mean)
    for d in range(3):
        new = new + e_plus[d][None] * moved[1 + 2 * d] + e_minus[d][None] * moved[2 + 2 * d]
    lower_v, inverse_v = factor(mm(new, new, (1, 1)) / count)
    return inverse, lower_v, mm(inverse_v, new)


def shards(spatial_factor, coupling, orient_factor, directions):
    dims = spatial_factor.shape[:3]
    rank = spatial_factor.shape[-1]
    cells = dims[0] * dims[1] * dims[2] * lax.axis_size("gx") * lax.axis_size("gy")
    field = spatial_factor.reshape(-1, rank).T
    orient = orient_factor.T
    e_plus = jnp.maximum(directions, 0.0)
    e_minus = jnp.maximum(-directions, 0.0)
    into = coupling.T
    halos = halo(field, dims, True)
    for step in range(STEPS):
        plus, minus, mean = tables(orient, e_plus, e_minus)
        weights, density_row = stage_weights(plus, minus, mean, into)
        field = k_stage(field, halos, dims, weights, density_row)
        halos = halo(field, dims, step < STEPS - 1)
        sums = all_sum(galerkin(field, dims, halos[1], halos[3], mean))
        inverse, lower_v, orient = orient_stage(sums, cells, orient, plus, minus, mean, e_plus, e_minus)
        into = mm(lower_v, inverse, (0, 0))
    new_spatial = mm(field, inverse, (0, 1)).reshape(spatial_factor.shape)
    return new_spatial, lower_v, orient.T


def solution(mesh):
    return jax.shard_map(
        shards,
        mesh=mesh,
        in_specs=(P("gx", "gy", None, None), P(), P(), P()),
        out_specs=(P("gx", "gy", None, None), P(), P()),
        check_vma=False,
    )
```

```python
import functools

import jax
import jax.numpy as jnp
from jax import lax
from jax.experimental import pallas as pl
from jax.experimental.pallas import tpu as pltpu
from jax.sharding import PartitionSpec as P

STEPS = 2

courant = 0.3
tumble = 0.2
highest = lax.Precision.HIGHEST
half = jnp.bfloat16
LANES = 128
VMEM_BYTES = 32 * 1024 * 1024


def mm(left, right, contract=(1, 0)):
    return lax.dot_general(
        left, right, (((contract[0],), (contract[1],)), ((), ())),
        precision=highest, preferred_element_type=jnp.float32,
    )


def dot(left, right, contract=(1, 0)):
    return lax.dot_general(
        left, right, (((contract[0],), (contract[1],)), ((), ())),
        preferred_element_type=jnp.float32,
    )


def halves(value):
    high = value.astype(half)
    return high, (value - high.astype(jnp.float32)).astype(half)


def three(left, right, contract):
    left_high, left_low = halves(left)
    right_high, right_low = halves(right)
    rows = left.shape[0]
    both = dot(jnp.concatenate([left_high, left_low], axis=0), right_high, contract)
    return both[:rows] + both[rows:] + dot(left_high, right_low, contract)


def lane_index(width):
    return lax.broadcasted_iota(jnp.int32, (1, width), 1)


def roll(value, shift):
    width = value.shape[1]
    shift = shift % width
    return value if shift == 0 else pltpu.roll(value, shift, axis=1)


def slabs_of(value, dims):
    slab = dims[1] * dims[2]
    return [value[:, x * slab:(x + 1) * slab] for x in range(dims[0])]


def y_layers(slabs, dims):
    lx, ly, lz = dims
    width = lx * lz
    owner = lane_index(width) // lz
    first = last = None
    for x in range(lx):
        head = roll(slabs[x][:, :width], lz * x)
        tail = roll(slabs[x][:, -width:], lz * (x + 1))
        first = head if first is None else jnp.where(owner == x, head, first)
        last = tail if last is None else jnp.where(owner == x, tail, last)
    return first, last


def y_ahead(slab, layer, x, dims):
    lz, width = dims[2], layer.shape[1]
    moved = roll(slab, -lz)
    edge = jnp.where(lane_index(width) >= width - lz, roll(layer, -lz * (x + 1)), moved[:, -width:])
    return jnp.concatenate([moved[:, :-width], edge], axis=1)


def y_behind(slab, layer, x, dims):
    lz, width = dims[2], layer.shape[1]
    moved = roll(slab, lz)
    edge = jnp.where(lane_index(width) < lz, roll(layer, -lz * x), moved[:, :width])
    return jnp.concatenate([edge, moved[:, width:]], axis=1)


def z_ahead(slab, dims):
    lz = dims[2]
    place = lane_index(slab.shape[1]) % lz
    return jnp.where(place == lz - 1, roll(slab, lz - 1), roll(slab, -1))


def z_behind(slab, dims):
    lz = dims[2]
    place = lane_index(slab.shape[1]) % lz
    return jnp.where(place == 0, roll(slab, 1 - lz), roll(slab, 1))


def motility(density):
    return 1.0 / (1.0 + density * density)


def speed_of(column, value):
    return motility(jnp.sum(column * value, axis=0, keepdims=True))


def signs(directions):
    return jnp.maximum(directions, 0.0), jnp.maximum(-directions, 0.0)


def tables(orient, directions):
    rank, count = orient.shape
    plus, minus = signs(directions)
    high, low = halves(orient)
    both = jnp.concatenate([high, low], axis=0)
    stack = [orient * part[d:d + 1] for d in range(3) for part in (plus, minus)]
    stack_high, stack_low = halves(jnp.concatenate(stack, axis=0))
    wide = dot(stack_high, both, (1, 1))
    summed = (wide[:, :rank] + wide[:, rank:] + dot(stack_low, high, (1, 1))) * (1.0 / count)
    return summed, jnp.sum(orient, axis=1, keepdims=True) * (1.0 / count)


def unit(rank):
    row = lax.broadcasted_iota(jnp.int32, (rank, rank), 0)
    col = lax.broadcasted_iota(jnp.int32, (rank, rank), 1)
    return jnp.where(row == col, 1.0, 0.0).astype(jnp.float32)


def stage_weights(table, mean, into):
    rank = mean.shape[0]
    blocks = [table[d * rank:(d + 1) * rank] for d in range(6)]
    total = blocks[0] + blocks[1] + blocks[2] + blocks[3] + blocks[4] + blocks[5]
    spread = jnp.broadcast_to(mean, (rank, rank))
    first = (1.0 - tumble) * unit(rank) + tumble * spread * spread.T
    stack = jnp.concatenate([first, -courant * total, courant * table], axis=0)
    column = mm(into, spread, (0, 0))[:, :1]
    return mm(stack, into), column


def factor(gram):
    rank = gram.shape[0]
    wide = jnp.concatenate([gram, unit(rank)], axis=1)
    group = 8
    rows = [wide[b * group:(b + 1) * group] for b in range(rank // group)]
    place = lax.broadcasted_iota(jnp.int32, (group, 1), 0)
    lane = lax.broadcasted_iota(jnp.int32, (group, 2 * rank), 1)
    for k in range(rank):
        b, i = divmod(k, group)
        row = rows[b][i:i + 1]
        scaled = row * (1.0 / row[:, k:k + 1])
        for c in range(b, rank // group):
            col = rows[c][:, k:k + 1]
            if c == b:
                col = jnp.where(place > i, col, 0.0)
            rows[c] = rows[c] - col * scaled
    done = []
    for b, block in enumerate(rows):
        pivot = jnp.sum(jnp.where(lane == place + b * group, block, 0.0), axis=1, keepdims=True)
        done.append(block * lax.rsqrt(pivot))
    done = jnp.concatenate(done, axis=0)
    return done[:, :rank], done[:, rank:]


def flat_weights(weights):
    rank = weights.shape[1]
    return jnp.concatenate([weights[b * rank:(b + 1) * rank] for b in range(weights.shape[0] // rank)], axis=1)


def call(body, outs, *args):
    return pl.pallas_call(
        body,
        out_shape=[jax.ShapeDtypeStruct(shape, jnp.float32) for shape in outs],
        in_specs=[pl.BlockSpec(memory_space=pltpu.VMEM)] * len(args),
        out_specs=[pl.BlockSpec(memory_space=pltpu.VMEM)] * len(outs),
        compiler_params=pltpu.CompilerParams(vmem_limit_bytes=VMEM_BYTES),
    )(*args)


def layer_shapes(rank, dims):
    lx, ly, lz = dims
    return [(rank, ly * lz)] * 2 + [(rank, lx * lz)] * 2


def write_layers(slabs, dims, refs):
    refs[0][...] = slabs[0]
    refs[1][...] = slabs[-1]
    refs[2][...], refs[3][...] = y_layers(slabs, dims)


def enter_kernel(dims, x_ref, field_ref, *layer_refs):
    field = x_ref[...].T
    field_ref[...] = field
    write_layers(slabs_of(field, dims), dims, layer_refs)


def table_kernel(v_ref, e_ref, s_ref, orient_ref, table_ref, mean_ref, weight_ref, column_ref):
    orient = v_ref[...].T
    orient_ref[...] = orient
    table, mean = tables(orient, e_ref[...])
    table_ref[...] = table
    mean_ref[...] = mean
    weights, column_ref[...] = stage_weights(table, mean, s_ref[...].T)
    weight_ref[...] = flat_weights(weights)


def k_kernel(dims, field_ref, xb_ref, xa_ref, yb_ref, ya_ref, weight_ref, column_ref, out_ref, *layer_refs):
    lx, ly, lz = dims
    slab = ly * lz
    column = column_ref[...]
    rank = column.shape[0]

    def flux_of(value):
        return speed_of(column, value) * value

    fields = slabs_of(field_ref[...], dims)
    flux = [flux_of(f) for f in fields]
    before, after = flux_of(xb_ref[...]), flux_of(xa_ref[...])
    layer_before, layer_after = flux_of(yb_ref[...]), flux_of(ya_ref[...])
    w_high, w_low = halves(weight_ref[...])
    w_both = jnp.concatenate([w_high, w_low], axis=0)
    results = []
    for x in range(lx):
        g = flux[x]
        stack = [
            fields[x],
            g,
            flux[x - 1] if x > 0 else before,
            flux[x + 1] if x < lx - 1 else after,
            y_behind(g, layer_before, x, dims),
            y_ahead(g, layer_after, x, dims),
            z_behind(g, dims),
            z_ahead(g, dims),
        ]
        high, low = halves(jnp.concatenate(stack, axis=0))
        wide = dot(w_both, high)
        result = wide[:rank] + wide[rank:] + dot(w_high, low)
        out_ref[:, x * slab:(x + 1) * slab] = result
        results.append(result)
    write_layers(results, dims, layer_refs)


def galerkin_kernel(dims, k_ref, xa_ref, ya_ref, mean_ref, out_ref):
    lx, ly, lz = dims
    mean = mean_ref[...]
    rank = mean.shape[0]
    fields = slabs_of(k_ref[...], dims)
    after, layer = xa_ref[...], ya_ref[...]
    speeds = [speed_of(mean, f) for f in fields] + [speed_of(mean, after)]
    sums = [jnp.zeros((rank, 2 * rank), jnp.float32) for _ in range(4)]
    for x in range(lx):
        k = fields[x]
        q = speeds[x] * k
        pairs = [(k, k)]
        moved = fields[x + 1] if x < lx - 1 else after
        pairs.append((moved, speeds[x + 1] * k))
        for moved in (y_ahead(k, layer, x, dims), z_ahead(k, dims)):
            pairs.append((moved, speed_of(mean, moved) * k))
        for n, (left, right) in enumerate(pairs):
            sums[n] = sums[n] + three(left, jnp.concatenate([right, q], axis=0), (1, 1))
    for n in range(4):
        out_ref[n * rank:(n + 1) * rank] = sums[n]


def orient_stage(cells, sums, orient, table, mean, directions):
    rank, count = orient.shape
    plus, minus = signs(directions)
    blocks = [sums[n * rank:(n + 1) * rank] * (1.0 / cells) for n in range(4)]
    table = [table[d * rank:(d + 1) * rank] for d in range(6)]
    upper, inverse = factor(blocks[0][:, :rank])
    d_sum = blocks[0][:, rank:]
    back = [d_sum - blocks[1 + d][:, rank:] for d in range(3)]
    fore = [blocks[1 + d][:, :rank].T - d_sum for d in range(3)]
    drift = jnp.zeros((rank, rank), jnp.float32)
    for d in range(3):
        drift = drift + mm(back[d], table[2 * d]) - mm(fore[d], table[2 * d + 1])
    spread = jnp.broadcast_to(mean, (rank, rank))
    mid = (1.0 + tumble) * upper - tumble * mm(upper, spread) * spread.T + courant * mm(inverse, drift)
    solved = mm(inverse, mid, (0, 0))
    inner = jnp.concatenate([m for d in range(3) for m in (-back[d], fore[d])], axis=0)
    inner = mm(inner, solved)
    rows = [(1.0 - tumble) * mid]
    for n in range(6):
        rows.append(courant * mm(inverse, inner[n * rank:(n + 1) * rank]))
    rows_high, rows_low = halves(jnp.concatenate(rows, axis=0))
    high, low = halves(orient)
    moved = dot(
        jnp.concatenate([rows_high, rows_high, rows_low], axis=1),
        jnp.concatenate([high, low, high], axis=0),
    )
    new = moved[:rank] + tumble * mm(mid, spread)[:, :1]
    for d in range(3):
        new = new + plus[d:d + 1] * moved[(1 + 2 * d) * rank:(2 + 2 * d) * rank]
        new = new + minus[d:d + 1] * moved[(2 + 2 * d) * rank:(3 + 2 * d) * rank]
    upper_v, inverse_v = factor(three(new, new, (1, 1)) * (1.0 / count))
    return inverse, upper_v, three(inverse_v, new, (1, 0))


def turn_kernel(cells, sums_ref, orient_ref, table_ref, mean_ref, e_ref, orient_out, table_out, mean_out, weight_ref, column_ref):
    directions = e_ref[...]
    inverse, upper_v, orient = orient_stage(cells, sums_ref[...], orient_ref[...], table_ref[...], mean_ref[...], directions)
    orient_out[...] = orient
    table, mean = tables(orient, directions)
    table_out[...] = table
    mean_out[...] = mean
    weights, column_ref[...] = stage_weights(table, mean, mm(upper_v, inverse))
    weight_ref[...] = flat_weights(weights)


def last_kernel(cells, sums_ref, orient_ref, table_ref, mean_ref, e_ref, field_ref, x_ref, s_ref, v_ref):
    inverse, upper_v, orient = orient_stage(cells, sums_ref[...], orient_ref[...], table_ref[...], mean_ref[...], e_ref[...])
    x_ref[...] = three(inverse, field_ref[...], (1, 0)).T
    s_ref[...] = upper_v.T
    v_ref[...] = orient.T


def shifted(axis, up):
    count = lax.axis_size(axis)
    step = 1 if up else count - 1
    return [(i, (i + step) % count) for i in range(count)]


def all_sum(part):
    count = lax.axis_size("gx") * lax.axis_size("gy")
    rows, width = part.shape
    padded = -(-rows // count) * count
    if padded != rows:
        part = jnp.pad(part, ((0, padded - rows), (0, 0)))
    split = part.reshape(count, padded // count, width)
    mine = lax.all_to_all(split, ("gx", "gy"), 0, 0).sum(axis=0)
    every = lax.all_to_all(jnp.broadcast_to(mine[None], split.shape), ("gx", "gy"), 0, 0)
    return every.reshape(padded, width)[:rows]


def ahead(layers):
    return (
        lax.ppermute(layers[0], "gx", shifted("gx", False)),
        lax.ppermute(layers[2], "gy", shifted("gy", False)),
    )


def behind(layers):
    return (
        lax.ppermute(layers[1], "gx", shifted("gx", True)),
        lax.ppermute(layers[3], "gy", shifted("gy", True)),
    )


def shards(spatial_factor, coupling, orient_factor, directions):
    dims = spatial_factor.shape[:3]
    rank = spatial_factor.shape[-1]
    sites = dims[0] * dims[1] * dims[2]
    count = orient_factor.shape[0]
    cells = sites * lax.axis_size("gx") * lax.axis_size("gy")
    layers = layer_shapes(rank, dims)
    stage = [(rank, count), (6 * rank, rank), (rank, 1), (rank, 8 * rank), (rank, 1)]
    field, *edges = call(
        functools.partial(enter_kernel, dims), [(rank, sites)] + layers, spatial_factor.reshape(sites, rank)
    )
    x_after, y_after = ahead(edges)
    x_before, y_before = behind(edges)
    orient, table, mean, weights, column = call(table_kernel, stage, orient_factor, directions, coupling)
    for step in range(STEPS):
        field, *edges = call(
            functools.partial(k_kernel, dims), [(rank, sites)] + layers,
            field, x_before, x_after, y_before, y_after, weights, column,
        )
        x_after, y_after = ahead(edges)
        if step < STEPS - 1:
            x_before, y_before = behind(edges)
        (part,) = call(
            functools.partial(galerkin_kernel, dims), [(4 * rank, 2 * rank)], field, x_after, y_after, mean
        )
        sums = all_sum(part)
        if step < STEPS - 1:
            orient, table, mean, weights, column = call(
                functools.partial(turn_kernel, cells), stage, sums, orient, table, mean, directions
            )
    new_spatial, new_coupling, new_orient = call(
        functools.partial(last_kernel, cells), [(sites, rank), (rank, rank), (count, rank)],
        sums, orient, table, mean, directions, field,
    )
    return new_spatial.reshape(spatial_factor.shape), new_coupling, new_orient


def solution(mesh):
    return jax.shard_map(
        shards,
        mesh=mesh,
        in_specs=(P("gx", "gy", None, None), P(), P(), P()),
        out_specs=(P("gx", "gy", None, None), P(), P()),
        check_vma=False,
    )
```

```python
import functools

import jax
import jax.numpy as jnp
from jax import lax
from jax.experimental import pallas as pl
from jax.experimental.pallas import tpu as pltpu
from jax.sharding import PartitionSpec as P

courant = 0.3
tumble = 0.2
highest = lax.Precision.HIGHEST
half = jnp.bfloat16
LANES = 128
VMEM_BYTES = 32 * 1024 * 1024


def mm(left, right, contract=(1, 0)):
    return lax.dot_general(
        left, right, (((contract[0],), (contract[1],)), ((), ())),
        precision=highest, preferred_element_type=jnp.float32,
    )


def dot(left, right, contract=(1, 0)):
    return lax.dot_general(
        left, right, (((contract[0],), (contract[1],)), ((), ())),
        preferred_element_type=jnp.float32,
    )


def halves(value):
    high = value.astype(half)
    return high, (value - high.astype(jnp.float32)).astype(half)


def three(left, right, contract):
    left_high, left_low = halves(left)
    right_high, right_low = halves(right)
    rows = left.shape[0]
    both = dot(jnp.concatenate([left_high, left_low], axis=0), right_high, contract)
    return both[:rows] + both[rows:] + dot(left_high, right_low, contract)


def lane_index(width):
    return lax.broadcasted_iota(jnp.int32, (1, width), 1)


def roll(value, shift):
    width = value.shape[1]
    shift = shift % width
    return value if shift == 0 else pltpu.roll(value, shift, axis=1)


def slabs_of(value, dims):
    slab = dims[1] * dims[2]
    return [value[:, x * slab:(x + 1) * slab] for x in range(dims[0])]


def y_layer(slabs, dims, index):
    lx, ly, lz = dims
    width = lx * lz
    start = index * lz // width * width
    owner = lane_index(width) // lz
    layer = None
    for x in range(lx):
        line = roll(slabs[x][:, start:start + width], lz * x - (index * lz - start))
        layer = line if layer is None else jnp.where(owner == x, line, layer)
    return layer


def y_ahead(slab, edge, dims):
    lz, width = dims[2], edge.shape[1]
    moved = roll(slab, -lz)
    last = jnp.where(lane_index(width) >= width - lz, edge, moved[:, -width:])
    return jnp.concatenate([moved[:, :-width], last], axis=1)


def y_behind(slab, edge, dims):
    lz, width = dims[2], edge.shape[1]
    moved = roll(slab, lz)
    first = jnp.where(lane_index(width) < lz, edge, moved[:, :width])
    return jnp.concatenate([first, moved[:, width:]], axis=1)


def z_ahead(slab, dims):
    lz = dims[2]
    place = lane_index(slab.shape[1]) % lz
    return jnp.where(place == lz - 1, roll(slab, lz - 1), roll(slab, -1))


def z_behind(slab, dims):
    lz = dims[2]
    place = lane_index(slab.shape[1]) % lz
    return jnp.where(place == 0, roll(slab, 1 - lz), roll(slab, 1))


def motility(density):
    return 1.0 / (1.0 + density * density)


def speed_of(column, value):
    return motility(jnp.sum(column * value, axis=0, keepdims=True))


def signs(directions):
    return jnp.maximum(directions, 0.0), jnp.maximum(-directions, 0.0)


def tables(orient, directions):
    rank, count = orient.shape
    plus, minus = signs(directions)
    high, low = halves(orient)
    both = jnp.concatenate([high, low], axis=0)
    stack = [orient * part[d:d + 1] for d in range(3) for part in (plus, minus)]
    stack_high, stack_low = halves(jnp.concatenate(stack, axis=0))
    wide = dot(stack_high, both, (1, 1))
    summed = (wide[:, :rank] + wide[:, rank:] + dot(stack_low, high, (1, 1))) * (1.0 / count)
    return summed, jnp.sum(orient, axis=1, keepdims=True) * (1.0 / count)


def unit(rank):
    row = lax.broadcasted_iota(jnp.int32, (rank, rank), 0)
    col = lax.broadcasted_iota(jnp.int32, (rank, rank), 1)
    return jnp.where(row == col, 1.0, 0.0).astype(jnp.float32)


def stage_weights(table, mean, into):
    rank = mean.shape[0]
    blocks = [table[d * rank:(d + 1) * rank] for d in range(6)]
    total = blocks[0] + blocks[1] + blocks[2] + blocks[3] + blocks[4] + blocks[5]
    spread = jnp.broadcast_to(mean, (rank, rank))
    first = (1.0 - tumble) * unit(rank) + tumble * spread * spread.T
    stack = jnp.concatenate([first, -courant * total, courant * table], axis=0)
    column = mm(into, spread, (0, 0))[:, :1]
    return mm(stack, into), column


def factor(gram):
    rank = gram.shape[0]
    group = 8
    shape = (group, 2 * rank)
    eye = unit(rank)
    diag_row = jnp.sum(eye * gram, axis=0, keepdims=True)
    diag_column = jnp.sum(eye * gram, axis=1, keepdims=True)
    scale = lax.rsqrt(diag_row)
    wide = jnp.concatenate([gram * lax.rsqrt(diag_column) * scale, eye], axis=1)
    blocks = rank // group
    rows = [wide[b * group:(b + 1) * group] for b in range(blocks)]
    place = lax.broadcasted_iota(jnp.int32, shape, 0)
    lane = lax.broadcasted_iota(jnp.int32, shape, 1)

    def spread(value, i):
        return jnp.broadcast_to(value[i:i + 1], shape)

    for b in range(blocks):
        start = b * group
        cols = {
            c: [jnp.broadcast_to(rows[c][:, start + j:start + j + 1], shape) for j in range(group)]
            for c in range(b, blocks)
        }
        for j in range(0, group, 2):
            first, second = cols[b][j], cols[b][j + 1]
            p, o, q = spread(first, j), spread(second, j), spread(second, j + 1)
            over = 1.0 / (p * q - o * o)
            p, o, q = p * over, o * over, q * over

            def solve(value):
                upper, lower = spread(value, j), spread(value, j + 1)
                return q * upper - o * lower, p * lower - o * upper

            later = [solve(cols[b][n]) for n in range(j + 2, group)]
            row_first, row_second = solve(rows[b])
            for c in range(b, blocks):
                left, right = cols[c][j], cols[c][j + 1]
                if c == b:
                    if j == group - 2:
                        continue
                    left, right = jnp.where(place > j + 1, left, 0.0), jnp.where(place > j + 1, right, 0.0)
                for n, (up, low) in enumerate(later):
                    cols[c][j + 2 + n] = cols[c][j + 2 + n] - left * up - right * low
                rows[c] = rows[c] - left * row_first - right * row_second
    done = []
    for b, block in enumerate(rows):
        at = place + b * group
        pivot = jnp.sum(jnp.where(lane == at, block, 0.0), axis=1, keepdims=True)
        beside = jnp.sum(jnp.where((lane == at - 1) & (place % 2 == 1), block, 0.0), axis=1, keepdims=True)
        pivot = jnp.broadcast_to(pivot, shape)
        part = beside / pltpu.roll(pivot, 1, axis=0)
        block = block - part * pltpu.roll(block, 1, axis=0)
        done.append(block * lax.rsqrt(pivot - part * beside))
    done = jnp.concatenate(done, axis=0) * jnp.concatenate([diag_row * scale, scale], axis=1)
    return done[:, :rank], done[:, rank:]


def flat_weights(weights):
    rank = weights.shape[1]
    return jnp.concatenate([weights[b * rank:(b + 1) * rank] for b in range(weights.shape[0] // rank)], axis=1)


def call(body, outs, *args):
    return pl.pallas_call(
        body,
        out_shape=[jax.ShapeDtypeStruct(shape, jnp.float32) for shape in outs],
        in_specs=[pl.BlockSpec(memory_space=pltpu.VMEM)] * len(args),
        out_specs=[pl.BlockSpec(memory_space=pltpu.VMEM)] * len(outs),
        compiler_params=pltpu.CompilerParams(vmem_limit_bytes=VMEM_BYTES),
    )(*args)


def enter_kernel(dims, x_ref, field_ref, first_ref, last_ref, y_first_ref, y_last_ref):
    field = x_ref[...].T
    field_ref[...] = field
    slabs = slabs_of(field, dims)
    first_ref[...], last_ref[...] = slabs[0], slabs[-1]
    y_first_ref[...], y_last_ref[...] = y_layer(slabs, dims, 0), y_layer(slabs, dims, dims[1] - 1)


def table_kernel(v_ref, e_ref, s_ref, orient_ref, table_ref, mean_ref, weight_ref, column_ref):
    orient = v_ref[...].T
    orient_ref[...] = orient
    table, mean = tables(orient, e_ref[...])
    table_ref[...] = table
    mean_ref[...] = mean
    weights, column_ref[...] = stage_weights(table, mean, s_ref[...].T)
    weight_ref[...] = flat_weights(weights)


def weighted(weights, rank):
    w_high, w_low = halves(weights)
    w_both = jnp.concatenate([w_high, w_low], axis=0)

    def product(stack):
        high, low = halves(jnp.concatenate(stack, axis=0))
        wide = dot(w_both, high)
        return wide[:rank] + wide[rank:] + dot(w_high, low)

    return product


def k_stage(dims, field, weights, column, xb, xa, yb, ya, further=None):
    lx, ly, lz = dims
    slab, width = ly * lz, lx * lz

    def flux_of(value):
        return speed_of(column, value) * value

    product = weighted(weights, column.shape[0])
    fields = slabs_of(field, dims) + [xa]
    flux = [flux_of(f) for f in fields]
    before, layer, layer_before = flux_of(xb), flux_of(ya), flux_of(yb)
    if further is not None:
        second, corner_before, layer_next = [flux_of(f) for f in further]
        corners = second[:, slab:]
        corner_after = roll(corners, -2 * lz)
        flux.append(second[:, :slab])
    flux.append(before)
    results = []
    for x in range(lx if further is None else lx + 1):
        g = flux[x]
        line_before = roll(layer_before, -lz * x) if x < lx else corners
        line_after = roll(layer, -lz * (x + 1)) if x < lx else corner_after
        results.append(product([
            fields[x], g, flux[x - 1], flux[x + 1],
            y_behind(g, line_before, dims), y_ahead(g, line_after, dims), z_behind(g, dims), z_ahead(g, dims),
        ]))
    if further is None:
        return results
    lane = lane_index(width)
    side = product([
        ya, layer,
        jnp.where(lane < lz, roll(corner_before, lz), roll(layer, lz)),
        jnp.where(lane >= width - lz, corner_after, roll(layer, -lz)),
        y_layer(flux[:lx], dims, ly - 1), layer_next, z_behind(layer, dims), z_ahead(layer, dims),
    ])
    return results, side


def galerkin(dims, fields, layer, mean):
    lx, ly, lz = dims
    rank = mean.shape[0]
    speeds = [speed_of(mean, f) for f in fields]
    sums = [jnp.zeros((rank, 2 * rank), jnp.float32) for _ in range(4)]
    for x in range(lx):
        k = fields[x]
        q = speeds[x] * k
        pairs = [(k, k), (fields[x + 1], speeds[x + 1] * k)]
        for moved in (y_ahead(k, roll(layer, -lz * (x + 1)), dims), z_ahead(k, dims)):
            pairs.append((moved, speed_of(mean, moved) * k))
        for n, (left, right) in enumerate(pairs):
            sums[n] = sums[n] + three(left, jnp.concatenate([right, q], axis=0), (1, 1))
    return jnp.concatenate(sums, axis=0)


def write_slabs(ref, slabs):
    slab = slabs[0].shape[1]
    for x, value in enumerate(slabs):
        ref[:, x * slab:(x + 1) * slab] = value


def first_kernel(
    dims, field_ref, xb, xa, yb, ya, weight_ref, column_ref, out_ref, first_ref, y_first_ref, y_last_ref
):
    slabs = k_stage(
        dims, field_ref[...], weight_ref[...], column_ref[...], xb[...], xa[...], yb[...], ya[...]
    )
    write_slabs(out_ref, slabs)
    first_ref[...] = slabs[0]
    y_first_ref[...], y_last_ref[...] = y_layer(slabs, dims, 0), y_layer(slabs, dims, dims[1] - 1)


def galerkin_kernel(dims, field_ref, xa, ya, yb, mean_ref, sums_ref, down_ref, up_ref, next_ref):
    lx, ly, lz = dims
    slab, width = ly * lz, lx * lz
    slabs = slabs_of(field_ref[...], dims)
    layer = ya[...]
    sums_ref[...] = galerkin(dims, slabs + [xa[...]], layer, mean_ref[...])
    down_ref[:, :slab] = slabs[1]
    down_ref[:, slab:] = jnp.where(lane_index(width) < lz, yb[...], roll(layer, lz))
    up_ref[:, :slab] = slabs[-1]
    up_ref[:, slab:] = layer
    next_ref[...] = y_layer(slabs, dims, 1)


def orient_stage(cells, sums, orient, table, mean, directions):
    rank, count = orient.shape
    plus, minus = signs(directions)
    blocks = [sums[n * rank:(n + 1) * rank] * (1.0 / cells) for n in range(4)]
    table = [table[d * rank:(d + 1) * rank] for d in range(6)]
    upper, inverse = factor(blocks[0][:, :rank])
    d_sum = blocks[0][:, rank:]
    back = [d_sum - blocks[1 + d][:, rank:] for d in range(3)]
    fore = [blocks[1 + d][:, :rank].T - d_sum for d in range(3)]
    drift = jnp.zeros((rank, rank), jnp.float32)
    for d in range(3):
        drift = drift + mm(back[d], table[2 * d]) - mm(fore[d], table[2 * d + 1])
    spread = jnp.broadcast_to(mean, (rank, rank))
    mid = (1.0 + tumble) * upper - tumble * mm(upper, spread) * spread.T + courant * mm(inverse, drift)
    solved = mm(inverse, mid, (0, 0))
    inner = jnp.concatenate([m for d in range(3) for m in (-back[d], fore[d])], axis=0)
    inner = mm(inner, solved)
    rows = [(1.0 - tumble) * mid]
    for n in range(6):
        rows.append(courant * mm(inverse, inner[n * rank:(n + 1) * rank]))
    rows_high, rows_low = halves(jnp.concatenate(rows, axis=0))
    high, low = halves(orient)
    moved = dot(
        jnp.concatenate([rows_high, rows_high, rows_low], axis=1),
        jnp.concatenate([high, low, high], axis=0),
    )
    new = moved[:rank] + tumble * mm(mid, spread)[:, :1]
    for d in range(3):
        new = new + plus[d:d + 1] * moved[(1 + 2 * d) * rank:(2 + 2 * d) * rank]
        new = new + minus[d:d + 1] * moved[(2 + 2 * d) * rank:(3 + 2 * d) * rank]
    upper_v, inverse_v = factor(three(new, new, (1, 1)) * (1.0 / count))
    return inverse, upper_v, three(inverse_v, new, (1, 0))


def turn_kernel(
    cells, sums_ref, orient_ref, table_ref, mean_ref, e_ref, orient_out, table_out, mean_out, weight_ref, column_ref
):
    directions = e_ref[...]
    inverse, upper_v, orient = orient_stage(cells, sums_ref[...], orient_ref[...], table_ref[...], mean_ref[...], directions)
    orient_out[...] = orient
    table, mean = tables(orient, directions)
    table_out[...] = table
    mean_out[...] = mean
    weights, column_ref[...] = stage_weights(table, mean, mm(upper_v, inverse))
    weight_ref[...] = flat_weights(weights)


def second_kernel(
    dims, field_ref, xa, ya, yb, second, behind, after, weight_ref, column_ref, mean_ref, field_out, sums_out
):
    slab = dims[1] * dims[2]
    slabs, side = k_stage(
        dims, field_ref[...], weight_ref[...], column_ref[...], behind[:, :slab], xa[...], yb[...], ya[...],
        (second[...], behind[:, slab:], after[...]),
    )
    write_slabs(field_out, slabs[:-1])
    sums_out[...] = galerkin(dims, slabs, side, mean_ref[...])


def last_kernel(cells, sums_ref, orient_ref, table_ref, mean_ref, e_ref, field_ref, x_ref, s_ref, v_ref):
    inverse, upper_v, orient = orient_stage(cells, sums_ref[...], orient_ref[...], table_ref[...], mean_ref[...], e_ref[...])
    x_ref[...] = three(inverse, field_ref[...], (1, 0)).T
    s_ref[...] = upper_v.T
    v_ref[...] = orient.T


def shifted(axis, up):
    count = lax.axis_size(axis)
    step = 1 if up else count - 1
    return [(i, (i + step) % count) for i in range(count)]


def all_sum(part):
    count = lax.axis_size("gx") * lax.axis_size("gy")
    rows, width = part.shape
    padded = -(-rows // count) * count
    if padded != rows:
        part = jnp.pad(part, ((0, padded - rows), (0, 0)))
    split = part.reshape(count, padded // count, width)
    mine = lax.all_to_all(split, ("gx", "gy"), 0, 0).sum(axis=0)
    every = lax.all_to_all(jnp.broadcast_to(mine[None], split.shape), ("gx", "gy"), 0, 0)
    return every.reshape(padded, width)[:rows]


def up(value, axis):
    return lax.ppermute(value, axis, shifted(axis, True))


def down(value, axis):
    return lax.ppermute(value, axis, shifted(axis, False))


def shards(spatial_factor, coupling, orient_factor, directions):
    dims = spatial_factor.shape[:3]
    lx, ly, lz = dims
    rank = spatial_factor.shape[-1]
    sites = lx * ly * lz
    count = orient_factor.shape[0]
    cells = sites * lax.axis_size("gx") * lax.axis_size("gy")
    whole, slab, layer = (rank, sites), (rank, ly * lz), (rank, lx * lz)
    more = (rank, ly * lz + lx * lz)
    summed = (4 * rank, 2 * rank)
    basis = [(rank, count), (6 * rank, rank), (rank, 1)]
    field, first, last, y_first, y_last = call(
        functools.partial(enter_kernel, dims), [whole, slab, slab, layer, layer], spatial_factor.reshape(sites, rank)
    )
    xb, xa, yb, ya = up(last, "gx"), down(first, "gx"), up(y_last, "gy"), down(y_first, "gy")
    stage = basis + [(rank, 8 * rank), (rank, 1)]
    orient, table, mean, weights, column = call(table_kernel, stage, orient_factor, directions, coupling)
    field, first, y_first, y_last = call(
        functools.partial(first_kernel, dims), [whole, slab, layer, layer], field, xb, xa, yb, ya, weights, column
    )
    xa, ya, yb = down(first, "gx"), down(y_first, "gy"), up(y_last, "gy")
    part, second, behind, after = call(
        functools.partial(galerkin_kernel, dims), [summed, more, more, layer], field, xa, ya, yb, mean
    )
    second, behind, after = down(second, "gx"), up(behind, "gx"), down(after, "gy")
    orient, table, mean, weights, column = call(
        functools.partial(turn_kernel, cells), stage, all_sum(part), orient, table, mean, directions
    )
    field, part = call(
        functools.partial(second_kernel, dims), [whole, summed],
        field, xa, ya, yb, second, behind, after, weights, column, mean,
    )
    new_spatial, new_coupling, new_orient = call(
        functools.partial(last_kernel, cells), [(sites, rank), (rank, rank), (count, rank)],
        all_sum(part), orient, table, mean, directions, field,
    )
    return new_spatial.reshape(spatial_factor.shape), new_coupling, new_orient


def solution(mesh):
    return jax.shard_map(
        shards,
        mesh=mesh,
        in_specs=(P("gx", "gy", None, None), P(), P(), P()),
        out_specs=(P("gx", "gy", None, None), P(), P()),
        check_vma=False,
    )
```

```python
import functools

import jax
import jax.numpy as jnp
from jax import lax
from jax.experimental import pallas as pl
from jax.experimental.pallas import tpu as pltpu
from jax.sharding import PartitionSpec as P

courant = 0.3
tumble = 0.2
highest = lax.Precision.HIGHEST
half = jnp.bfloat16
LANES = 128
VMEM_BYTES = 32 * 1024 * 1024


def mm(left, right, contract=(1, 0)):
    return lax.dot_general(
        left, right, (((contract[0],), (contract[1],)), ((), ())),
        precision=highest, preferred_element_type=jnp.float32,
    )


def dot(left, right, contract=(1, 0)):
    return lax.dot_general(
        left, right, (((contract[0],), (contract[1],)), ((), ())),
        preferred_element_type=jnp.float32,
    )


def halves(value):
    high = value.astype(half)
    return high, (value - high.astype(jnp.float32)).astype(half)


def three(left, right, contract):
    left_high, left_low = halves(left)
    right_high, right_low = halves(right)
    rows = left.shape[0]
    both = dot(jnp.concatenate([left_high, left_low], axis=0), right_high, contract)
    return both[:rows] + both[rows:] + dot(left_high, right_low, contract)


def lane_index(width):
    return lax.broadcasted_iota(jnp.int32, (1, width), 1)


def roll(value, shift):
    width = value.shape[1]
    shift = shift % width
    return value if shift == 0 else pltpu.roll(value, shift, axis=1)


def slabs_of(value, dims):
    slab = dims[1] * dims[2]
    return [value[:, x * slab:(x + 1) * slab] for x in range(dims[0])]


def y_layer(slabs, dims, index):
    lx, ly, lz = dims
    width = lx * lz
    start = index * lz // width * width
    owner = lane_index(width) // lz
    layer = None
    for x in range(lx):
        line = roll(slabs[x][:, start:start + width], lz * x - (index * lz - start))
        layer = line if layer is None else jnp.where(owner == x, line, layer)
    return layer


def y_ahead(slab, edge, dims):
    lz, width = dims[2], edge.shape[1]
    moved = roll(slab, -lz)
    last = jnp.where(lane_index(width) >= width - lz, edge, moved[:, -width:])
    return jnp.concatenate([moved[:, :-width], last], axis=1)


def y_behind(slab, edge, dims):
    lz, width = dims[2], edge.shape[1]
    moved = roll(slab, lz)
    first = jnp.where(lane_index(width) < lz, edge, moved[:, :width])
    return jnp.concatenate([first, moved[:, width:]], axis=1)


def z_ahead(slab, dims):
    lz = dims[2]
    place = lane_index(slab.shape[1]) % lz
    return jnp.where(place == lz - 1, roll(slab, lz - 1), roll(slab, -1))


def z_behind(slab, dims):
    lz = dims[2]
    place = lane_index(slab.shape[1]) % lz
    return jnp.where(place == 0, roll(slab, 1 - lz), roll(slab, 1))


def motility(density):
    return 1.0 / (1.0 + density * density)


def speed_of(column, value):
    return motility(jnp.sum(column * value, axis=0, keepdims=True))


def signs(directions):
    return jnp.maximum(directions, 0.0), jnp.maximum(-directions, 0.0)


def tables(orient, directions):
    rank, count = orient.shape
    plus, minus = signs(directions)
    high, low = halves(orient)
    both = jnp.concatenate([high, low], axis=0)
    stack = [orient * part[d:d + 1] for d in range(3) for part in (plus, minus)]
    stack_high, stack_low = halves(jnp.concatenate(stack, axis=0))
    scale = 1.0 / count

    def product(left_high, left_low):
        wide = dot(left_high, both, (1, 1))
        return (wide[:, :rank] + wide[:, rank:] + dot(left_low, high, (1, 1))) * scale

    return product(high, low), product(stack_high, stack_low), jnp.sum(orient, axis=1, keepdims=True) * scale


def unit(rank):
    row = lax.broadcasted_iota(jnp.int32, (rank, rank), 0)
    col = lax.broadcasted_iota(jnp.int32, (rank, rank), 1)
    return jnp.where(row == col, 1.0, 0.0).astype(jnp.float32)


def stage_weights(gram, table, mean, into):
    rank = mean.shape[0]
    blocks = [table[d * rank:(d + 1) * rank] for d in range(6)]
    total = blocks[0] + blocks[1] + blocks[2] + blocks[3] + blocks[4] + blocks[5]
    spread = jnp.broadcast_to(mean, (rank, rank))
    first = (1.0 - tumble) * gram + tumble * spread * spread.T
    weights = mm(jnp.concatenate([first, -courant * total, courant * table], axis=0), into)
    weights = jnp.concatenate([weights[b * rank:(b + 1) * rank] for b in range(8)], axis=1)
    return weights, mm(into, spread, (0, 0))[:, :1]


def factor(gram, beside=None, meanwhile=()):
    rank = gram.shape[0]
    group = 8
    shape = (group, 2 * rank)
    eye = unit(rank)
    diag_row = jnp.sum(eye * gram, axis=0, keepdims=True)
    diag_column = jnp.sum(eye * gram, axis=1, keepdims=True)
    scale = lax.rsqrt(diag_row)
    scale_column = lax.rsqrt(diag_column)
    wide = jnp.concatenate([gram * scale_column * scale, eye], axis=1)
    blocks = rank // group
    fields = [wide] if beside is None else [wide, beside * scale_column]
    fields = [[f[b * group:(b + 1) * group] for b in range(blocks)] for f in fields]
    rows = fields[0]
    place = lax.broadcasted_iota(jnp.int32, shape, 0)
    lane = lax.broadcasted_iota(jnp.int32, shape, 1)

    def spread(value, i):
        return jnp.broadcast_to(value[i:i + 1], value.shape)

    for b in range(blocks):
        start = b * group
        cols = {
            c: [jnp.broadcast_to(rows[c][:, start + j:start + j + 1], shape) for j in range(group)]
            for c in range(b, blocks)
        }
        for j in range(0, group, 2):
            first, second = cols[b][j], cols[b][j + 1]
            p, o, q = spread(first, j), spread(second, j), spread(second, j + 1)
            over = 1.0 / (p * q - o * o)
            p, o, q = p * over, o * over, q * over

            def solve(value):
                width = value.shape[1]
                upper, lower = spread(value, j), spread(value, j + 1)
                return (
                    q[:, :width] * upper - o[:, :width] * lower,
                    p[:, :width] * lower - o[:, :width] * upper,
                )

            later = [solve(cols[b][n]) for n in range(j + 2, group)]
            pivots = [solve(f[b]) for f in fields]
            for c in range(b, blocks):
                left, right = cols[c][j], cols[c][j + 1]
                if c == b:
                    if j == group - 2:
                        continue
                    left, right = jnp.where(place > j + 1, left, 0.0), jnp.where(place > j + 1, right, 0.0)
                for n, (up, low) in enumerate(later):
                    cols[c][j + 2 + n] = cols[c][j + 2 + n] - left * up - right * low
                for f, (up, low) in zip(fields, pivots):
                    width = up.shape[1]
                    f[c] = f[c] - left[:, :width] * up - right[:, :width] * low
        if b < len(meanwhile):
            meanwhile[b]()
    done = [[] for _ in fields]
    for b, block in enumerate(rows):
        at = place + b * group
        pivot = jnp.sum(jnp.where(lane == at, block, 0.0), axis=1, keepdims=True)
        under = jnp.sum(jnp.where((lane == at - 1) & (place % 2 == 1), block, 0.0), axis=1, keepdims=True)
        pivot = jnp.broadcast_to(pivot, shape)
        part = under / pltpu.roll(pivot, 1, axis=0)
        root = lax.rsqrt(pivot - part * under)
        for f, out in zip(fields, done):
            width = f[b].shape[1]
            out.append((f[b] - part[:, :width] * pltpu.roll(f[b], 1, axis=0)) * root[:, :width])
    done = [jnp.concatenate(d, axis=0) for d in done]
    both = done[0] * jnp.concatenate([diag_row * scale, scale], axis=1)
    return (both[:, :rank], both[:, rank:], *done[1:])


def call(body, outs, *args, far_out=(), scratch=()):
    def space(n, far):
        return pl.BlockSpec(memory_space=pltpu.HBM if n in far else pltpu.VMEM)

    return pl.pallas_call(
        body,
        out_shape=[jax.ShapeDtypeStruct(shape, jnp.float32) for shape in outs],
        in_specs=[pl.BlockSpec(memory_space=pltpu.VMEM)] * len(args),
        out_specs=[space(n, far_out) for n in range(len(outs))],
        scratch_shapes=list(scratch),
        compiler_params=pltpu.CompilerParams(vmem_limit_bytes=VMEM_BYTES),
    )(*args)


def enter_kernel(dims, x_ref, field_ref, first_ref, last_ref, y_first_ref, y_last_ref):
    field = x_ref[...].T
    field_ref[...] = field
    slabs = slabs_of(field, dims)
    first_ref[...], last_ref[...] = slabs[0], slabs[-1]
    y_first_ref[...], y_last_ref[...] = y_layer(slabs, dims, 0), y_layer(slabs, dims, dims[1] - 1)


def table_kernel(orient_ref, e_ref, s_ref, table_ref, mean_ref, weight_ref, column_ref):
    _, table, mean = tables(orient_ref[...], e_ref[...])
    table_ref[...] = table
    mean_ref[...] = mean
    weight_ref[...], column_ref[...] = stage_weights(unit(mean.shape[0]), table, mean, s_ref[...].T)


def weighted(weights, rank):
    w_high, w_low = halves(weights)
    w_both = jnp.concatenate([w_high, w_low], axis=0)

    def product(stack):
        high, low = halves(jnp.concatenate(stack, axis=0))
        wide = dot(w_both, high)
        return wide[:rank] + wide[rank:] + dot(w_high, low)

    return product


def k_stage(dims, field, weights, column, xb, xa, yb, ya, further=None):
    lx, ly, lz = dims
    slab, width = ly * lz, lx * lz

    def flux_of(value):
        return speed_of(column, value) * value

    product = weighted(weights, column.shape[0])
    fields = slabs_of(field, dims) + [xa]
    flux = [flux_of(f) for f in fields]
    before, layer, layer_before = flux_of(xb), flux_of(ya), flux_of(yb)
    if further is not None:
        second, corner_before, layer_next = [flux_of(f) for f in further]
        corners = second[:, slab:]
        corner_after = roll(corners, -2 * lz)
        flux.append(second[:, :slab])
    flux.append(before)
    results = []
    for x in range(lx if further is None else lx + 1):
        g = flux[x]
        line_before = roll(layer_before, -lz * x) if x < lx else corners
        line_after = roll(layer, -lz * (x + 1)) if x < lx else corner_after
        results.append(product([
            fields[x], g, flux[x - 1], flux[x + 1],
            y_behind(g, line_before, dims), y_ahead(g, line_after, dims), z_behind(g, dims), z_ahead(g, dims),
        ]))
    if further is None:
        return results
    lane = lane_index(width)
    side = product([
        ya, layer,
        jnp.where(lane < lz, roll(corner_before, lz), roll(layer, lz)),
        jnp.where(lane >= width - lz, corner_after, roll(layer, -lz)),
        y_layer(flux[:lx], dims, ly - 1), layer_next, z_behind(layer, dims), z_ahead(layer, dims),
    ])
    return results, side


def galerkin(dims, fields, layer, mean):
    lx, ly, lz = dims
    rank = mean.shape[0]
    speeds = [speed_of(mean, f) for f in fields]
    sums = [jnp.zeros((rank, 2 * rank), jnp.float32) for _ in range(4)]
    for x in range(lx):
        k = fields[x]
        q = speeds[x] * k
        pairs = [(k, k), (fields[x + 1], speeds[x + 1] * k)]
        for moved in (y_ahead(k, roll(layer, -lz * (x + 1)), dims), z_ahead(k, dims)):
            pairs.append((moved, speed_of(mean, moved) * k))
        for n, (left, right) in enumerate(pairs):
            sums[n] = sums[n] + three(left, jnp.concatenate([right, q], axis=0), (1, 1))
    return jnp.concatenate(sums, axis=0)


def write_slabs(ref, slabs):
    slab = slabs[0].shape[1]
    for x, value in enumerate(slabs):
        ref[:, x * slab:(x + 1) * slab] = value


def first_kernel(
    dims, field_ref, xb, xa, yb, ya, weight_ref, column_ref, out_ref, first_ref, y_first_ref, y_last_ref
):
    slabs = k_stage(
        dims, field_ref[...], weight_ref[...], column_ref[...], xb[...], xa[...], yb[...], ya[...]
    )
    write_slabs(out_ref, slabs)
    first_ref[...] = slabs[0]
    y_first_ref[...], y_last_ref[...] = y_layer(slabs, dims, 0), y_layer(slabs, dims, dims[1] - 1)


def galerkin_kernel(dims, field_ref, xa, ya, yb, mean_ref, sums_ref, down_ref, up_ref, next_ref):
    lx, ly, lz = dims
    slab, width = ly * lz, lx * lz
    slabs = slabs_of(field_ref[...], dims)
    layer = ya[...]
    sums_ref[...] = galerkin(dims, slabs + [xa[...]], layer, mean_ref[...])
    down_ref[:, :slab] = slabs[1]
    down_ref[:, slab:] = jnp.where(lane_index(width) < lz, yb[...], roll(layer, lz))
    up_ref[:, :slab] = slabs[-1]
    up_ref[:, slab:] = layer
    next_ref[...] = y_layer(slabs, dims, 1)


def apply(left, right):
    left_high, left_low = halves(left)
    high, low = halves(right)
    return dot(
        jnp.concatenate([left_high, left_high, left_low], axis=1), jnp.concatenate([high, low, high], axis=0)
    )


def orient_stage(cells, sums, orient, table, mean, directions, basis=None):
    rank = orient.shape[0]
    plus, minus = signs(directions)
    blocks = [sums[n * rank:(n + 1) * rank] * (1.0 / cells) for n in range(4)]
    gram, d_sum = blocks[0][:, :rank], blocks[0][:, rank:]
    inner = []
    for d in range(3):
        inner += [blocks[1 + d][:, rank:] - d_sum, blocks[1 + d][:, :rank].T - d_sum]
    drift = -mm(jnp.concatenate(inner, axis=1), table)
    upper, inverse, drift = factor(gram, drift)
    spread = jnp.broadcast_to(mean, (rank, rank))
    solved = (1.0 + tumble) * unit(rank) - tumble * spread * spread.T + courant * mm(inverse, drift, (0, 0))
    rows = [(1.0 - tumble) * upper] + [courant * mm(inverse, part) for part in inner]
    rows = mm(jnp.concatenate(rows, axis=0), solved)
    mid_mean = mm(rows[:rank], spread)[:, :1]
    moved = apply(rows if basis is None else mm(rows, basis), orient)
    new = moved[:rank] + mid_mean * (tumble / (1.0 - tumble))
    for d in range(3):
        new = new + plus[d:d + 1] * moved[(1 + 2 * d) * rank:(2 + 2 * d) * rank]
        new = new + minus[d:d + 1] * moved[(2 + 2 * d) * rank:(3 + 2 * d) * rank]
    return inverse, new


def turn_kernel(
    cells, sums_ref, orient_ref, table_ref, mean_ref, e_ref,
    weight_ref, column_ref, mean_out, new_ref, inverse_ref, table_out,
):
    directions = e_ref[...]
    rank = orient_ref.shape[0]
    inverse, new = orient_stage(cells, sums_ref[...], orient_ref[...], table_ref[...], mean_ref[...], directions)
    new_ref[...] = new
    gram, table, mean = tables(new, directions)
    weights, column_ref[...] = stage_weights(gram, table, mean, inverse)
    _, inverse_v = factor(gram)
    inverse_ref[...] = inverse_v
    weight_ref[...] = mm(inverse_v, weights)
    mean_out[...] = mm(inverse_v, jnp.broadcast_to(mean, (rank, rank)))[:, :1]
    right = mm(table, inverse_v, (1, 1))
    for n in range(6):
        table_out[n * rank:(n + 1) * rank] = mm(inverse_v, right[n * rank:(n + 1) * rank])


def second_kernel(
    dims, field_ref, xa, ya, yb, second, behind, after, weight_ref, column_ref, mean_ref, field_out, sums_out
):
    slab = dims[1] * dims[2]
    slabs, side = k_stage(
        dims, field_ref[...], weight_ref[...], column_ref[...], behind[:, :slab], xa[...], yb[...], ya[...],
        (second[...], behind[:, slab:], after[...]),
    )
    write_slabs(field_out, slabs[:-1])
    sums_out[...] = galerkin(dims, slabs, side, mean_ref[...])


def last_kernel(
    cells, sums_ref, orient_ref, basis_ref, table_ref, mean_ref, e_ref, field_ref, x_ref, s_ref, v_ref, x_buffer, sems
):
    inverse, new = orient_stage(
        cells, sums_ref[...], orient_ref[...], table_ref[...], mean_ref[...], e_ref[...], basis_ref[...]
    )
    count = new.shape[1]
    parts = sems.shape[0]
    chunk = field_ref.shape[1] // parts

    copies = [
        pltpu.make_async_copy(
            x_buffer.at[pl.ds(n * chunk, chunk)], x_ref.at[pl.ds(n * chunk, chunk)], sems.at[n]
        )
        for n in range(parts)
    ]

    def x_part(n):
        def work():
            x_buffer[n * chunk:(n + 1) * chunk] = apply(inverse, field_ref[:, n * chunk:(n + 1) * chunk]).T
            copies[n].start()
        return work

    upper_v, inverse_v = factor(
        three(new, new, (1, 1)) * (1.0 / count), meanwhile=[x_part(n) for n in range(parts)]
    )
    s_ref[...] = upper_v.T
    v_ref[...] = apply(inverse_v, new)
    for copy in copies:
        copy.wait()


def shifted(axis, up):
    count = lax.axis_size(axis)
    step = 1 if up else count - 1
    return [(i, (i + step) % count) for i in range(count)]


def all_sum(part):
    count = lax.axis_size("gx") * lax.axis_size("gy")
    rows, width = part.shape
    padded = -(-rows // count) * count
    if padded != rows:
        part = jnp.pad(part, ((0, padded - rows), (0, 0)))
    split = part.reshape(count, padded // count, width)
    mine = lax.all_to_all(split, ("gx", "gy"), 0, 0).sum(axis=0)
    every = lax.all_to_all(jnp.broadcast_to(mine[None], split.shape), ("gx", "gy"), 0, 0)
    return every.reshape(padded, width)[:rows]


def up(value, axis):
    return lax.ppermute(value, axis, shifted(axis, True))


def down(value, axis):
    return lax.ppermute(value, axis, shifted(axis, False))


def shards(spatial_factor, coupling, orient_factor, directions):
    dims = spatial_factor.shape[:3]
    lx, ly, lz = dims
    rank = spatial_factor.shape[-1]
    sites = lx * ly * lz
    count = orient_factor.shape[0]
    cells = sites * lax.axis_size("gx") * lax.axis_size("gy")
    whole, slab, layer = (rank, sites), (rank, ly * lz), (rank, lx * lz)
    more = (rank, ly * lz + lx * lz)
    summed = (4 * rank, 2 * rank)
    field, first, last, y_first, y_last = call(
        functools.partial(enter_kernel, dims), [whole, slab, slab, layer, layer], spatial_factor.reshape(sites, rank)
    )
    xb, xa, yb, ya = up(last, "gx"), down(first, "gx"), up(y_last, "gy"), down(y_first, "gy")
    basis = [(rank, count), (6 * rank, rank)]
    column_shape, weight_shape = (rank, 1), (rank, 8 * rank)
    orient = orient_factor.T
    table, mean, weights, column = call(
        table_kernel, [basis[1], column_shape, weight_shape, column_shape], orient, directions, coupling
    )
    field, first, y_first, y_last = call(
        functools.partial(first_kernel, dims), [whole, slab, layer, layer], field, xb, xa, yb, ya, weights, column
    )
    xa, ya, yb = down(first, "gx"), down(y_first, "gy"), up(y_last, "gy")
    part, second, behind, after = call(
        functools.partial(galerkin_kernel, dims), [summed, more, more, layer], field, xa, ya, yb, mean
    )
    second, behind, after = down(second, "gx"), up(behind, "gx"), down(after, "gy")
    weights, column, mean, new, inverse, table = call(
        functools.partial(turn_kernel, cells),
        [weight_shape, column_shape, column_shape, basis[0], (rank, rank), basis[1]],
        all_sum(part), orient, table, mean, directions,
    )
    field, part = call(
        functools.partial(second_kernel, dims), [whole, summed],
        field, xa, ya, yb, second, behind, after, weights, column, mean,
    )
    new_spatial, new_coupling, new_orient = call(
        functools.partial(last_kernel, cells), [(sites, rank), (rank, rank), (rank, count)],
        all_sum(part), new, inverse, table, mean, directions, field, far_out=(0,),
        scratch=(pltpu.VMEM((sites, rank), jnp.float32), pltpu.SemaphoreType.DMA((4,))),
    )
    return new_spatial.reshape(spatial_factor.shape), new_coupling, new_orient.T


def solution(mesh):
    return jax.shard_map(
        shards,
        mesh=mesh,
        in_specs=(P("gx", "gy", None, None), P(), P(), P()),
        out_specs=(P("gx", "gy", None, None), P(), P()),
        check_vma=False,
    )
```

```python
import functools

import jax
import jax.numpy as jnp
from jax import lax
from jax.experimental import pallas as pl
from jax.experimental.pallas import tpu as pltpu
from jax.sharding import PartitionSpec as P

courant = 0.3
tumble = 0.2
highest = lax.Precision.HIGHEST
half = jnp.bfloat16
LANES = 128
VMEM_BYTES = 32 * 1024 * 1024


def mm(left, right, contract=(1, 0)):
    return lax.dot_general(
        left, right, (((contract[0],), (contract[1],)), ((), ())),
        precision=highest, preferred_element_type=jnp.float32,
    )


def dot(left, right, contract=(1, 0)):
    return lax.dot_general(
        left, right, (((contract[0],), (contract[1],)), ((), ())),
        preferred_element_type=jnp.float32,
    )


def halves(value):
    high = value.astype(half)
    return high, (value - high.astype(jnp.float32)).astype(half)


def three(left, right, contract):
    left_high, left_low = halves(left)
    right_high, right_low = halves(right)
    rows = left.shape[0]
    both = dot(jnp.concatenate([left_high, left_low], axis=0), right_high, contract)
    return both[:rows] + both[rows:] + dot(left_high, right_low, contract)


def lane_index(width):
    return lax.broadcasted_iota(jnp.int32, (1, width), 1)


def roll(value, shift):
    width = value.shape[1]
    shift = shift % width
    return value if shift == 0 else pltpu.roll(value, shift, axis=1)


def slabs_of(value, dims):
    slab = dims[1] * dims[2]
    return [value[:, x * slab:(x + 1) * slab] for x in range(dims[0])]


def y_layer(slabs, dims, index):
    lx, ly, lz = dims
    width = lx * lz
    start = index * lz // width * width
    owner = lane_index(width) // lz
    layer = None
    for x in range(lx):
        line = roll(slabs[x][:, start:start + width], lz * x - (index * lz - start))
        layer = line if layer is None else jnp.where(owner == x, line, layer)
    return layer


def y_ahead(slab, edge, dims):
    lz, width = dims[2], edge.shape[1]
    moved = roll(slab, -lz)
    last = jnp.where(lane_index(width) >= width - lz, edge, moved[:, -width:])
    return jnp.concatenate([moved[:, :-width], last], axis=1)


def y_behind(slab, edge, dims):
    lz, width = dims[2], edge.shape[1]
    moved = roll(slab, lz)
    first = jnp.where(lane_index(width) < lz, edge, moved[:, :width])
    return jnp.concatenate([first, moved[:, width:]], axis=1)


def z_ahead(slab, dims):
    lz = dims[2]
    place = lane_index(slab.shape[1]) % lz
    return jnp.where(place == lz - 1, roll(slab, lz - 1), roll(slab, -1))


def z_behind(slab, dims):
    lz = dims[2]
    place = lane_index(slab.shape[1]) % lz
    return jnp.where(place == 0, roll(slab, 1 - lz), roll(slab, 1))


def motility(density):
    return 1.0 / (1.0 + density * density)


def speed_of(column, value):
    return motility(jnp.sum(column * value, axis=0, keepdims=True))


def signs(directions):
    return jnp.maximum(directions, 0.0), jnp.maximum(-directions, 0.0)


def tables(orient, directions):
    rank, count = orient.shape
    plus, minus = signs(directions)
    high, low = halves(orient)
    both = jnp.concatenate([high, low], axis=0)
    stack = [orient * part[d:d + 1] for d in range(3) for part in (plus, minus)]
    stack_high, stack_low = halves(jnp.concatenate(stack, axis=0))
    scale = 1.0 / count

    def product(left_high, left_low):
        wide = dot(left_high, both, (1, 1))
        return (wide[:, :rank] + wide[:, rank:] + dot(left_low, high, (1, 1))) * scale

    return product(high, low), product(stack_high, stack_low), jnp.sum(orient, axis=1, keepdims=True) * scale


def unit(rank):
    row = lax.broadcasted_iota(jnp.int32, (rank, rank), 0)
    col = lax.broadcasted_iota(jnp.int32, (rank, rank), 1)
    return jnp.where(row == col, 1.0, 0.0).astype(jnp.float32)


def stage_weights(gram, table, mean, into):
    rank = mean.shape[0]
    blocks = [table[d * rank:(d + 1) * rank] for d in range(6)]
    total = blocks[0] + blocks[1] + blocks[2] + blocks[3] + blocks[4] + blocks[5]
    spread = jnp.broadcast_to(mean, (rank, rank))
    first = (1.0 - tumble) * gram + tumble * spread * spread.T
    weights = mm(jnp.concatenate([first, -courant * total, courant * table], axis=0), into)
    weights = jnp.concatenate([weights[b * rank:(b + 1) * rank] for b in range(8)], axis=1)
    return weights, mm(into, spread, (0, 0))[:, :1]


def factor(gram, beside=None, meanwhile=()):
    rank = gram.shape[0]
    group = 8
    shape = (group, 2 * rank)
    eye = unit(rank)
    diag_row = jnp.sum(eye * gram, axis=0, keepdims=True)
    diag_column = jnp.sum(eye * gram, axis=1, keepdims=True)
    scale = lax.rsqrt(diag_row)
    scale_column = lax.rsqrt(diag_column)
    wide = jnp.concatenate([gram * scale_column * scale, eye], axis=1)
    blocks = rank // group
    fields = [wide] if beside is None else [wide, beside * scale_column]
    fields = [[f[b * group:(b + 1) * group] for b in range(blocks)] for f in fields]
    rows = fields[0]
    place = lax.broadcasted_iota(jnp.int32, shape, 0)
    lane = lax.broadcasted_iota(jnp.int32, shape, 1)

    def spread(value, i):
        return jnp.broadcast_to(value[i:i + 1], value.shape)

    for b in range(blocks):
        start = b * group
        cols = {
            c: [jnp.broadcast_to(rows[c][:, start + j:start + j + 1], shape) for j in range(group)]
            for c in range(b, blocks)
        }
        for j in range(0, group, 2):
            first, second = cols[b][j], cols[b][j + 1]
            p, o, q = spread(first, j), spread(second, j), spread(second, j + 1)
            over = 1.0 / (p * q - o * o)
            p, o, q = p * over, o * over, q * over

            def solve(value):
                width = value.shape[1]
                upper, lower = spread(value, j), spread(value, j + 1)
                return (
                    q[:, :width] * upper - o[:, :width] * lower,
                    p[:, :width] * lower - o[:, :width] * upper,
                )

            later = [solve(cols[b][n]) for n in range(j + 2, group)]
            pivots = [solve(f[b]) for f in fields]
            for c in range(b, blocks):
                left, right = cols[c][j], cols[c][j + 1]
                if c == b:
                    if j == group - 2:
                        continue
                    left, right = jnp.where(place > j + 1, left, 0.0), jnp.where(place > j + 1, right, 0.0)
                for n, (up, low) in enumerate(later):
                    cols[c][j + 2 + n] = cols[c][j + 2 + n] - left * up - right * low
                for f, (up, low) in zip(fields, pivots):
                    width = up.shape[1]
                    f[c] = f[c] - left[:, :width] * up - right[:, :width] * low
        if b < len(meanwhile):
            meanwhile[b]()
    done = [[] for _ in fields]
    for b, block in enumerate(rows):
        at = place + b * group
        pivot = jnp.sum(jnp.where(lane == at, block, 0.0), axis=1, keepdims=True)
        under = jnp.sum(jnp.where((lane == at - 1) & (place % 2 == 1), block, 0.0), axis=1, keepdims=True)
        pivot = jnp.broadcast_to(pivot, shape)
        part = under / pltpu.roll(pivot, 1, axis=0)
        root = lax.rsqrt(pivot - part * under)
        for f, out in zip(fields, done):
            width = f[b].shape[1]
            out.append((f[b] - part[:, :width] * pltpu.roll(f[b], 1, axis=0)) * root[:, :width])
    done = [jnp.concatenate(d, axis=0) for d in done]
    both = done[0] * jnp.concatenate([diag_row * scale, scale], axis=1)
    return (both[:, :rank], both[:, rank:], *done[1:])


def call(body, outs, *args, far_out=(), scratch=(), cost=None):
    def space(n, far):
        return pl.BlockSpec(memory_space=pltpu.HBM if n in far else pltpu.VMEM)

    return pl.pallas_call(
        body,
        out_shape=[jax.ShapeDtypeStruct(shape, jnp.float32) for shape in outs],
        in_specs=[pl.BlockSpec(memory_space=pltpu.VMEM)] * len(args),
        out_specs=[space(n, far_out) for n in range(len(outs))],
        scratch_shapes=list(scratch),
        cost_estimate=cost,
        compiler_params=pltpu.CompilerParams(vmem_limit_bytes=VMEM_BYTES),
    )(*args)


def enter_kernel(dims, x_ref, field_ref, first_ref, last_ref, y_first_ref, y_last_ref):
    field = x_ref[...].T
    field_ref[...] = field
    slabs = slabs_of(field, dims)
    first_ref[...], last_ref[...] = slabs[0], slabs[-1]
    y_first_ref[...], y_last_ref[...] = y_layer(slabs, dims, 0), y_layer(slabs, dims, dims[1] - 1)


def table_kernel(orient_ref, e_ref, s_ref, table_ref, mean_ref, weight_ref, column_ref):
    _, table, mean = tables(orient_ref[...], e_ref[...])
    table_ref[...] = table
    mean_ref[...] = mean
    weight_ref[...], column_ref[...] = stage_weights(unit(mean.shape[0]), table, mean, s_ref[...].T)


def weighted(weights, rank):
    w_high, w_low = halves(weights)
    w_both = jnp.concatenate([w_high, w_low], axis=0)

    def product(stack):
        high, low = halves(jnp.concatenate(stack, axis=0))
        wide = dot(w_both, high)
        return wide[:rank] + wide[rank:] + dot(w_high, low)

    return product


def k_stage(dims, field, weights, column, xb, xa, yb, ya, further=None):
    lx, ly, lz = dims
    slab, width = ly * lz, lx * lz

    def flux_of(value):
        return speed_of(column, value) * value

    product = weighted(weights, column.shape[0])
    fields = slabs_of(field, dims) + [xa]
    flux = [flux_of(f) for f in fields]
    before, layer, layer_before = flux_of(xb), flux_of(ya), flux_of(yb)
    if further is not None:
        second, corner_before, layer_next = [flux_of(f) for f in further]
        corners = second[:, slab:]
        corner_after = roll(corners, -2 * lz)
        flux.append(second[:, :slab])
    flux.append(before)
    results = []
    for x in range(lx if further is None else lx + 1):
        g = flux[x]
        line_before = roll(layer_before, -lz * x) if x < lx else corners
        line_after = roll(layer, -lz * (x + 1)) if x < lx else corner_after
        results.append(product([
            fields[x], g, flux[x - 1], flux[x + 1],
            y_behind(g, line_before, dims), y_ahead(g, line_after, dims), z_behind(g, dims), z_ahead(g, dims),
        ]))
    if further is None:
        return results
    lane = lane_index(width)
    side = product([
        ya, layer,
        jnp.where(lane < lz, roll(corner_before, lz), roll(layer, lz)),
        jnp.where(lane >= width - lz, corner_after, roll(layer, -lz)),
        y_layer(flux[:lx], dims, ly - 1), layer_next, z_behind(layer, dims), z_ahead(layer, dims),
    ])
    return results, side


def galerkin(dims, fields, layer, mean):
    lx, ly, lz = dims
    rank = mean.shape[0]
    speeds = [speed_of(mean, f) for f in fields]
    sums = [jnp.zeros((rank, 2 * rank), jnp.float32) for _ in range(4)]
    for x in range(lx):
        k = fields[x]
        q = speeds[x] * k
        pairs = [(k, k), (fields[x + 1], speeds[x + 1] * k)]
        for moved in (y_ahead(k, roll(layer, -lz * (x + 1)), dims), z_ahead(k, dims)):
            pairs.append((moved, speed_of(mean, moved) * k))
        for n, (left, right) in enumerate(pairs):
            sums[n] = sums[n] + three(left, jnp.concatenate([right, q], axis=0), (1, 1))
    low = lane_index(2 * rank) < rank
    centre = jnp.where(low, -roll(sums[0], rank), sums[0])
    gram = sums[0][:, :rank]
    rows = [jnp.concatenate([gram[:rank // 2], gram[rank // 2:]], axis=1)]
    for part in sums[1:]:
        rows.append(centre + jnp.where(low, part, -part))
    return jnp.concatenate(rows, axis=0)


def write_slabs(ref, slabs):
    slab = slabs[0].shape[1]
    for x, value in enumerate(slabs):
        ref[:, x * slab:(x + 1) * slab] = value


def first_kernel(dims, field_ref, xb, xa, yb, ya, weight_ref, column_ref, out_ref, first_ref, y_first_ref):
    width = dims[0] * dims[2]
    slabs = k_stage(
        dims, field_ref[...], weight_ref[...], column_ref[...], xb[...], xa[...], yb[...], ya[...]
    )
    write_slabs(out_ref, slabs)
    first_ref[...] = slabs[0]
    y_first_ref[:, :width], y_first_ref[:, width:] = y_layer(slabs, dims, 0), y_layer(slabs, dims, 1)


def galerkin_kernel(dims, field_ref, xa, ya, mean_ref, sums_ref, up_ref, y_last_ref):
    lx, ly, lz = dims
    slab, width = ly * lz, lx * lz
    slabs = slabs_of(field_ref[...], dims)
    layer = ya[:, :width]
    sums_ref[...] = galerkin(dims, slabs + [xa[...]], layer, mean_ref[...])
    up_ref[:, :slab] = slabs[-1]
    up_ref[:, slab:] = layer
    y_last_ref[...] = y_layer(slabs, dims, ly - 1)


def pack_kernel(dims, field_ref, ya, yb, down_ref):
    lx, ly, lz = dims
    slab, width = ly * lz, lx * lz
    down_ref[:, :slab] = field_ref[:, slab:2 * slab]
    down_ref[:, slab:] = jnp.where(lane_index(width) < lz, yb[...], roll(ya[:, :width], lz))


def apply(left, right):
    left_high, left_low = halves(left)
    high, low = halves(right)
    return dot(
        jnp.concatenate([left_high, left_high, left_low], axis=1), jnp.concatenate([high, low, high], axis=0)
    )


def orient_stage(cells, sums, orient, table, mean, directions, basis=None):
    rank = orient.shape[0]
    plus, minus = signs(directions)
    sums = sums * (1.0 / cells)
    gram = jnp.concatenate([sums[:rank // 2, :rank], sums[:rank // 2, rank:]], axis=0)
    inner = []
    for d in range(3):
        block = sums[rank // 2 + d * rank:rank // 2 + (d + 1) * rank]
        inner += [-block[:, rank:], block[:, :rank].T]
    drift = -mm(jnp.concatenate(inner, axis=1), table)
    upper, inverse, drift = factor(gram, drift)
    spread = jnp.broadcast_to(mean, (rank, rank))
    solved = (1.0 + tumble) * unit(rank) - tumble * spread * spread.T + courant * mm(inverse, drift, (0, 0))
    rows = [(1.0 - tumble) * upper] + [courant * mm(inverse, part) for part in inner]
    rows = mm(jnp.concatenate(rows, axis=0), solved)
    mid_mean = mm(rows[:rank], spread)[:, :1]
    moved = apply(rows if basis is None else mm(rows, basis), orient)
    new = moved[:rank] + mid_mean * (tumble / (1.0 - tumble))
    for d in range(3):
        new = new + plus[d:d + 1] * moved[(1 + 2 * d) * rank:(2 + 2 * d) * rank]
        new = new + minus[d:d + 1] * moved[(2 + 2 * d) * rank:(3 + 2 * d) * rank]
    return inverse, new


def turn_kernel(
    cells, sums_ref, orient_ref, table_ref, mean_ref, e_ref,
    weight_ref, column_ref, mean_out, new_ref, inverse_ref, table_out,
):
    directions = e_ref[...]
    rank = orient_ref.shape[0]
    inverse, new = orient_stage(cells, sums_ref[...], orient_ref[...], table_ref[...], mean_ref[...], directions)
    new_ref[...] = new
    gram, table, mean = tables(new, directions)
    weights, column_ref[...] = stage_weights(gram, table, mean, inverse)
    _, inverse_v = factor(gram)
    inverse_ref[...] = inverse_v
    weight_ref[...] = mm(inverse_v, weights)
    mean_out[...] = mm(inverse_v, jnp.broadcast_to(mean, (rank, rank)))[:, :1]
    right = mm(table, inverse_v, (1, 1))
    for n in range(6):
        table_out[n * rank:(n + 1) * rank] = mm(inverse_v, right[n * rank:(n + 1) * rank])


def second_kernel(
    dims, field_ref, xa, ya, yb, second, behind, weight_ref, column_ref, mean_ref, field_out, sums_out
):
    slab, width = dims[1] * dims[2], dims[0] * dims[2]
    slabs, side = k_stage(
        dims, field_ref[...], weight_ref[...], column_ref[...], behind[:, :slab], xa[...], yb[...], ya[:, :width],
        (second[...], behind[:, slab:], ya[:, width:]),
    )
    write_slabs(field_out, slabs[:-1])
    sums_out[...] = galerkin(dims, slabs, side, mean_ref[...])


def last_kernel(
    cells, sums_ref, orient_ref, basis_ref, table_ref, mean_ref, e_ref, field_ref, x_ref, s_ref, v_ref, x_buffer, sems
):
    inverse, new = orient_stage(
        cells, sums_ref[...], orient_ref[...], table_ref[...], mean_ref[...], e_ref[...], basis_ref[...]
    )
    count = new.shape[1]
    parts = sems.shape[0]
    chunk = field_ref.shape[1] // parts

    copies = [
        pltpu.make_async_copy(
            x_buffer.at[pl.ds(n * chunk, chunk)], x_ref.at[pl.ds(n * chunk, chunk)], sems.at[n]
        )
        for n in range(parts)
    ]

    def x_part(n):
        def work():
            x_buffer[n * chunk:(n + 1) * chunk] = apply(inverse, field_ref[:, n * chunk:(n + 1) * chunk]).T
            copies[n].start()
        return work

    upper_v, inverse_v = factor(
        three(new, new, (1, 1)) * (1.0 / count), meanwhile=[x_part(n) for n in range(parts)]
    )
    s_ref[...] = upper_v.T
    v_ref[...] = apply(inverse_v, new)
    for copy in copies:
        copy.wait()


def shifted(axis, up):
    count = lax.axis_size(axis)
    step = 1 if up else count - 1
    return [(i, (i + step) % count) for i in range(count)]


def scatter_gather_sum(part):
    count = lax.axis_size("gx") * lax.axis_size("gy")
    rows, width = part.shape
    padded = -(-rows // count) * count
    if padded != rows:
        part = jnp.pad(part, ((0, padded - rows), (0, 0)))
    split = part.reshape(count, padded // count, width)
    mine = lax.all_to_all(split, ("gx", "gy"), 0, 0).sum(axis=0)
    every = lax.all_to_all(jnp.broadcast_to(mine[None], split.shape), ("gx", "gy"), 0, 0)
    return every.reshape(padded, width)[:rows]


def swapped(value, bits):
    count = lax.axis_size("gx") * lax.axis_size("gy")
    return lax.ppermute(value, ("gx", "gy"), [(i, i ^ bits) for i in range(count)])


def sum_of_four(value, step):
    near, far, cross = [swapped(value, n * step) for n in (1, 2, 3)]
    return (value + near) + (far + cross)


def all_sum(part, meanwhile=(lambda value: value,) * 2):
    nx, ny = lax.axis_size("gx"), lax.axis_size("gy")
    rows = part.shape[0] // 2
    if nx != 4 or ny != 8 or rows % 8:
        for work in meanwhile:
            part = work(part)
        return scatter_gather_sum(part)
    first = lax.axis_index("gy") % 2 == 0
    total = part + swapped(part, 1)
    mine = jnp.where(first, total[:rows], total[rows:])
    for step, work in zip((ny, 2), meanwhile):
        mine = work(sum_of_four(mine, step))
    other = swapped(mine, 1)
    return jnp.concatenate([jnp.where(first, mine, other), jnp.where(first, other, mine)], axis=0)


def up(value, axis):
    return lax.ppermute(value, axis, shifted(axis, True))


def down(value, axis):
    return lax.ppermute(value, axis, shifted(axis, False))


def shards(spatial_factor, coupling, orient_factor, directions):
    dims = spatial_factor.shape[:3]
    lx, ly, lz = dims
    rank = spatial_factor.shape[-1]
    sites = lx * ly * lz
    count = orient_factor.shape[0]
    cells = sites * lax.axis_size("gx") * lax.axis_size("gy")
    whole, slab, layer = (rank, sites), (rank, ly * lz), (rank, lx * lz)
    two_layers, more = (rank, 2 * lx * lz), (rank, ly * lz + lx * lz)
    summed = (7 * rank // 2, 2 * rank)
    field, first, last, y_first, y_last = call(
        functools.partial(enter_kernel, dims), [whole, slab, slab, layer, layer], spatial_factor.reshape(sites, rank)
    )
    xb, xa, yb, ya = up(last, "gx"), down(first, "gx"), up(y_last, "gy"), down(y_first, "gy")
    basis = [(rank, count), (6 * rank, rank)]
    column_shape, weight_shape = (rank, 1), (rank, 8 * rank)
    orient = orient_factor.T
    table, mean, weights, column = call(
        table_kernel, [basis[1], column_shape, weight_shape, column_shape], orient, directions, coupling
    )
    field, first, y_first = call(
        functools.partial(first_kernel, dims), [whole, slab, two_layers], field, xb, xa, yb, ya, weights, column
    )
    xa, ya = down(first, "gx"), down(y_first, "gy")
    part, behind, y_last = call(
        functools.partial(galerkin_kernel, dims), [summed, more, layer], field, xa, ya, mean
    )
    yb, behind = up(y_last, "gy"), up(behind, "gx")
    halo = {"yb": yb, "behind": behind}

    def with_layer(value):
        value, halo["yb"] = lax.optimization_barrier((value, halo["yb"]))
        (packed,) = call(functools.partial(pack_kernel, dims), [more], field, ya, halo["yb"])
        halo["second"] = down(packed, "gx")
        return value

    sums = all_sum(part, (with_layer, lambda value: value))
    weights, column, mean, new, inverse, table = call(
        functools.partial(turn_kernel, cells),
        [weight_shape, column_shape, column_shape, basis[0], (rank, rank), basis[1]],
        sums, orient, table, mean, directions, cost=pl.CostEstimate(flops=1, bytes_accessed=1, transcendentals=0),
    )
    field, part = call(
        functools.partial(second_kernel, dims), [whole, summed],
        field, xa, ya, halo["yb"], halo["second"], halo["behind"], weights, column, mean,
    )
    new_spatial, new_coupling, new_orient = call(
        functools.partial(last_kernel, cells), [(sites, rank), (rank, rank), (rank, count)],
        all_sum(part), new, inverse, table, mean, directions, field, far_out=(0,),
        scratch=(pltpu.VMEM((sites, rank), jnp.float32), pltpu.SemaphoreType.DMA((4,))),
    )
    return new_spatial.reshape(spatial_factor.shape), new_coupling, new_orient.T


def solution(mesh):
    return jax.shard_map(
        shards,
        mesh=mesh,
        in_specs=(P("gx", "gy", None, None), P(), P(), P()),
        out_specs=(P("gx", "gy", None, None), P(), P()),
        check_vma=False,
    )
```

```python
import functools

import jax
import jax.numpy as jnp
from jax import lax
from jax.experimental import pallas as pl
from jax.experimental.pallas import tpu as pltpu
from jax.sharding import PartitionSpec as P

courant = 0.3
tumble = 0.2
highest = lax.Precision.HIGHEST
half = jnp.bfloat16
LANES = 128
VMEM_BYTES = 32 * 1024 * 1024


def mm(left, right, contract=(1, 0)):
    return lax.dot_general(
        left, right, (((contract[0],), (contract[1],)), ((), ())),
        precision=highest, preferred_element_type=jnp.float32,
    )


def dot(left, right, contract=(1, 0)):
    return lax.dot_general(
        left, right, (((contract[0],), (contract[1],)), ((), ())),
        preferred_element_type=jnp.float32,
    )


def halves(value):
    high = value.astype(half)
    return high, (value - high.astype(jnp.float32)).astype(half)


def stacked(pairs, axis=0):
    return tuple(jnp.concatenate(part, axis=axis) for part in zip(*pairs))


def three(left, right, contract):
    left_high, left_low = left
    right_high, right_low = right
    rows = left_high.shape[0]
    both = dot(jnp.concatenate(left, axis=0), right_high, contract)
    return both[:rows] + both[rows:] + dot(left_high, right_low, contract)


def lane_index(width):
    return lax.broadcasted_iota(jnp.int32, (1, width), 1)


def roll(value, shift):
    width = value.shape[1]
    shift = shift % width
    return value if shift == 0 else pltpu.roll(value, shift, axis=1)


def slabs_of(value, dims):
    slab = dims[1] * dims[2]
    return [value[:, x * slab:(x + 1) * slab] for x in range(dims[0])]


def y_layer(slabs, dims, index):
    lx, ly, lz = dims
    width = lx * lz
    start = index * lz // width * width
    owner = lane_index(width) // lz
    layer = None
    for x in range(lx):
        line = roll(slabs[x][:, start:start + width], lz * x - (index * lz - start))
        layer = line if layer is None else jnp.where(owner == x, line, layer)
    return layer


def y_ahead(slab, edge, dims):
    lz, width = dims[2], edge.shape[1]
    moved = roll(slab, -lz)
    last = jnp.where(lane_index(width) >= width - lz, edge, moved[:, -width:])
    return jnp.concatenate([moved[:, :-width], last], axis=1)


def y_behind(slab, edge, dims):
    lz, width = dims[2], edge.shape[1]
    moved = roll(slab, lz)
    first = jnp.where(lane_index(width) < lz, edge, moved[:, :width])
    return jnp.concatenate([first, moved[:, width:]], axis=1)


def z_ahead(slab, dims):
    lz = dims[2]
    place = lane_index(slab.shape[1]) % lz
    return jnp.where(place == lz - 1, roll(slab, lz - 1), roll(slab, -1))


def z_behind(slab, dims):
    lz = dims[2]
    place = lane_index(slab.shape[1]) % lz
    return jnp.where(place == 0, roll(slab, 1 - lz), roll(slab, 1))


def motility(density):
    return 1.0 / (1.0 + density * density)


def speed_of(column, value):
    return motility(jnp.sum(column * value, axis=0, keepdims=True))


def signs(directions):
    return jnp.maximum(directions, 0.0), jnp.maximum(-directions, 0.0)


def tables(orient, directions):
    rank, count = orient.shape
    plus, minus = signs(directions)
    high, low = halves(orient)
    both = jnp.concatenate([high, low], axis=0)
    stack = [orient * part[d:d + 1] for d in range(3) for part in (plus, minus)]
    stack_high, stack_low = halves(jnp.concatenate(stack, axis=0))
    scale = 1.0 / count

    def product(left_high, left_low):
        wide = dot(left_high, both, (1, 1))
        return (wide[:, :rank] + wide[:, rank:] + dot(left_low, high, (1, 1))) * scale

    return product(high, low), product(stack_high, stack_low), jnp.sum(orient, axis=1, keepdims=True) * scale


def unit(rank):
    row = lax.broadcasted_iota(jnp.int32, (rank, rank), 0)
    col = lax.broadcasted_iota(jnp.int32, (rank, rank), 1)
    return jnp.where(row == col, 1.0, 0.0).astype(jnp.float32)


def stage_weights(gram, table, mean, into):
    rank = mean.shape[0]
    blocks = [table[d * rank:(d + 1) * rank] for d in range(6)]
    total = blocks[0] + blocks[1] + blocks[2] + blocks[3] + blocks[4] + blocks[5]
    spread = jnp.broadcast_to(mean, (rank, rank))
    first = (1.0 - tumble) * gram + tumble * spread * spread.T
    weights = mm(jnp.concatenate([first, -courant * total, courant * table], axis=0), into)
    weights = jnp.concatenate([weights[b * rank:(b + 1) * rank] for b in range(8)], axis=1)
    return weights, mm(into, spread, (0, 0))[:, :1]


def factor(gram, beside=None, meanwhile=()):
    rank = gram.shape[0]
    group = 8
    shape = (group, 2 * rank)
    eye = unit(rank)
    diag_row = jnp.sum(eye * gram, axis=0, keepdims=True)
    diag_column = jnp.sum(eye * gram, axis=1, keepdims=True)
    scale = lax.rsqrt(diag_row)
    scale_column = lax.rsqrt(diag_column)
    wide = jnp.concatenate([gram * scale_column * scale, eye], axis=1)
    blocks = rank // group
    fields = [wide] if beside is None else [wide, beside * scale_column]
    fields = [[f[b * group:(b + 1) * group] for b in range(blocks)] for f in fields]
    rows = fields[0]
    done = [list(f) for f in fields]
    place = lax.broadcasted_iota(jnp.int32, shape, 0)

    def spread(value, i):
        return jnp.broadcast_to(value[i:i + 1], value.shape)

    for b in range(blocks):
        start = b * group
        cols = {
            c: [jnp.broadcast_to(rows[c][:, start + j:start + j + 1], shape) for j in range(group)]
            for c in range(b, blocks)
        }
        for j in range(0, group, 2):
            first, second = cols[b][j], cols[b][j + 1]
            p, o, q = spread(first, j), spread(second, j), spread(second, j + 1)
            root = lax.rsqrt(p)
            along = o * root
            root_next = lax.rsqrt(q - along * along)
            for f, out in zip(fields, done):
                width = f[b].shape[1]
                upper = spread(f[b], j) * root[:, :width]
                lower = (spread(f[b], j + 1) - along[:, :width] * upper) * root_next[:, :width]
                at = place[:, :width]
                out[b] = jnp.where(at == j, upper, jnp.where(at == j + 1, lower, out[b]))
            over = 1.0 / (p * q - o * o)
            p, o, q = p * over, o * over, q * over

            def solve(value):
                width = value.shape[1]
                upper, lower = spread(value, j), spread(value, j + 1)
                return (
                    q[:, :width] * upper - o[:, :width] * lower,
                    p[:, :width] * lower - o[:, :width] * upper,
                )

            later = [solve(cols[b][n]) for n in range(j + 2, group)]
            pivots = [solve(f[b]) for f in fields]
            for c in range(b, blocks):
                left, right = cols[c][j], cols[c][j + 1]
                if c == b:
                    if j == group - 2:
                        continue
                    left, right = jnp.where(place > j + 1, left, 0.0), jnp.where(place > j + 1, right, 0.0)
                for n, (up, low) in enumerate(later):
                    cols[c][j + 2 + n] = cols[c][j + 2 + n] - left * up - right * low
                for f, (up, low) in zip(fields, pivots):
                    width = up.shape[1]
                    f[c] = f[c] - left[:, :width] * up - right[:, :width] * low
        if b < len(meanwhile):
            meanwhile[b]()
    done = [jnp.concatenate(d, axis=0) for d in done]
    both = done[0] * jnp.concatenate([diag_row * scale, scale], axis=1)
    return (both[:, :rank], both[:, rank:], *done[1:])


def call(body, outs, *args, far_out=(), scratch=(), cost=None):
    def space(n, far):
        return pl.BlockSpec(memory_space=pltpu.HBM if n in far else pltpu.VMEM)

    return pl.pallas_call(
        body,
        out_shape=[jax.ShapeDtypeStruct(shape, jnp.float32) for shape in outs],
        in_specs=[pl.BlockSpec(memory_space=pltpu.VMEM)] * len(args),
        out_specs=[space(n, far_out) for n in range(len(outs))],
        scratch_shapes=list(scratch),
        cost_estimate=cost,
        compiler_params=pltpu.CompilerParams(vmem_limit_bytes=VMEM_BYTES),
    )(*args)


def enter_kernel(dims, x_ref, field_ref, first_ref, last_ref, y_first_ref, y_last_ref):
    field = x_ref[...].T
    field_ref[...] = field
    slabs = slabs_of(field, dims)
    first_ref[...], last_ref[...] = slabs[0], slabs[-1]
    y_first_ref[...], y_last_ref[...] = y_layer(slabs, dims, 0), y_layer(slabs, dims, dims[1] - 1)


def table_kernel(orient_ref, e_ref, s_ref, table_ref, mean_ref, weight_ref, column_ref):
    _, table, mean = tables(orient_ref[...], e_ref[...])
    table_ref[...] = table
    mean_ref[...] = mean
    weight_ref[...], column_ref[...] = stage_weights(unit(mean.shape[0]), table, mean, s_ref[...].T)


CENTRE, X_BEHIND, X_AHEAD, Y_BEHIND, Y_AHEAD, Z_BEHIND, Z_AHEAD = range(7)


def triple(value):
    high, low = halves(value)
    return jnp.concatenate([high, low, high], axis=0)


class Weights:
    def __init__(self, weights, column):
        self.column = column
        self.rank = rank = column.shape[0]
        blocks = [weights[:, n * rank:(n + 1) * rank] for n in range(8)]
        high, low = halves(jnp.concatenate(blocks, axis=0))
        self.left = jnp.concatenate([high, high, low], axis=1)

    def times(self, value, start=CENTRE, stop=Z_AHEAD + 1):
        rank = self.rank
        flux = triple(speed_of(self.column, value) * value)
        wide = dot(self.left[(1 + start) * rank:(1 + stop) * rank], flux)
        return {n: wide[(n - start) * rank:(n - start + 1) * rank] for n in range(start, stop)}

    def one(self, value, n):
        return self.times(value, n, n + 1)[n]

    def whole(self, value, part, dims):
        return (
            dot(self.left[:self.rank], triple(value)) + part[CENTRE]
            + z_behind(part[Z_BEHIND], dims) + z_ahead(part[Z_AHEAD], dims)
        )


def k_edges(dims, field, weights, column, xb, xa, yb, ya):
    lx, ly, lz = dims
    width = lx * lz
    w = Weights(weights, column)
    slabs = slabs_of(field, dims)
    from_behind, from_ahead = w.one(xb, X_BEHIND), w.one(xa, X_AHEAD)
    before = w.one(yb, Y_BEHIND)
    part = w.times(slabs[0])
    first = (
        w.whole(slabs[0], part, dims) + from_behind + w.one(slabs[1], X_AHEAD)
        + y_behind(part[Y_BEHIND], before, dims)
        + y_ahead(part[Y_AHEAD], roll(w.one(ya, Y_AHEAD), -lz), dims)
    )
    layers = jnp.concatenate([y_layer(slabs, dims, 0), y_layer(slabs, dims, 1)], axis=1)
    part = w.times(layers)
    after = w.one(y_layer(slabs, dims, 2), Y_AHEAD)
    lane = lane_index(width)
    over_y = [before + part[Y_AHEAD][:, width:], part[Y_BEHIND][:, :width] + after]
    over_x = []
    for n in range(2):
        here = slice(n * width, (n + 1) * width)
        over_x.append(
            jnp.where(lane < lz, roll(from_behind[:, :width], -n * lz), roll(part[X_BEHIND][:, here], lz))
            + jnp.where(
                lane >= width - lz, roll(from_ahead[:, :width], -(n + 1) * lz), roll(part[X_AHEAD][:, here], -lz)
            )
        )
    return first, w.whole(layers, part, dims) + jnp.concatenate([x + y for x, y in zip(over_x, over_y)], axis=1)


def k_stage(dims, field, weights, column, xb, xa, yb, ya, further=None):
    lx, ly, lz = dims
    slab, width = ly * lz, lx * lz
    w = Weights(weights, column)
    fields = slabs_of(field, dims)
    if further is not None:
        fields.append(xa)
        second, corner_before, layer_next = further
        last = w.one(second[:, :slab], X_AHEAD)
    else:
        last = w.one(xa, X_AHEAD)
    parts = [w.times(f) for f in fields]
    from_behind = [w.one(xb, X_BEHIND)] + [p[X_BEHIND] for p in parts[:-1]]
    from_ahead = [p[X_AHEAD] for p in parts[1:]] + [last]
    layer_before = w.one(yb, Y_BEHIND)
    if further is None:
        layer = {Y_AHEAD: w.one(ya, Y_AHEAD)}
    else:
        layer = w.times(ya)
        corners = w.times(second[:, slab:], X_AHEAD, Y_AHEAD + 1)

    results = []
    for x, value in enumerate(fields):
        line_before = roll(layer_before, -lz * x) if x < lx else corners[Y_BEHIND]
        line_after = roll(layer[Y_AHEAD], -lz * (x + 1)) if x < lx else roll(corners[Y_AHEAD], -2 * lz)
        results.append(
            w.whole(value, parts[x], dims) + from_behind[x] + from_ahead[x]
            + y_behind(parts[x][Y_BEHIND], line_before, dims) + y_ahead(parts[x][Y_AHEAD], line_after, dims)
        )
    if further is None:
        return results
    lane = lane_index(width)
    side = (
        w.whole(ya, layer, dims)
        + jnp.where(lane < lz, roll(w.one(corner_before, X_BEHIND), lz), roll(layer[X_BEHIND], lz))
        + jnp.where(lane >= width - lz, roll(corners[X_AHEAD], -2 * lz), roll(layer[X_AHEAD], -lz))
        + y_layer([p[Y_BEHIND] for p in parts[:lx]], dims, ly - 1) + w.one(layer_next, Y_AHEAD)
    )
    return results, side


def pair_sums(left, right, q):
    return three(halves(left), stacked([halves(right), q]), (1, 1))


def inner_sums(dims, fields, layer, mean):
    lx, ly, lz = dims
    rank = mean.shape[0]
    speeds = [speed_of(mean, f) for f in fields]
    split = [halves(f) for f in fields]
    sums = [jnp.zeros((rank, 2 * rank), jnp.float32) for _ in range(4)]
    for x in range(lx):
        k = fields[x]
        q = halves(speeds[x] * k)
        pairs = [(0, split[x], split[x])]
        if x + 1 < len(fields):
            pairs.append((1, split[x + 1], halves(speeds[x + 1] * k)))
        for n, moved in ((2, y_ahead(k, roll(layer, -lz * (x + 1)), dims)), (3, z_ahead(k, dims))):
            pairs.append((n, halves(moved), halves(speed_of(mean, moved) * k)))
        for n, left, right in pairs:
            sums[n] = sums[n] + three(left, stacked([right, q]), (1, 1))
    return sums


def packed_sums(sums):
    rank = sums[0].shape[0]
    low = lane_index(2 * rank) < rank
    centre = jnp.where(low, -roll(sums[0], rank), sums[0])
    gram = sums[0][:, :rank]
    rows = [jnp.concatenate([gram[:rank // 2], gram[rank // 2:]], axis=1)]
    for part in sums[1:]:
        rows.append(centre + jnp.where(low, part, -part))
    return jnp.concatenate(rows, axis=0)


def write_slabs(ref, slabs):
    slab = slabs[0].shape[1]
    for x, value in enumerate(slabs):
        ref[:, x * slab:(x + 1) * slab] = value


def edge_kernel(dims, field_ref, xb, xa, yb, ya, weight_ref, column_ref, first_ref, y_first_ref):
    first_ref[...], y_first_ref[...] = k_edges(
        dims, field_ref[...], weight_ref[...], column_ref[...], xb[...], xa[...], yb[...], ya[...]
    )


def first_kernel(
    dims, field_ref, xb, xa, yb, ya, weight_ref, column_ref, mean_ref, out_ref, sums_ref, last_ref, y_last_ref
):
    slabs = k_stage(
        dims, field_ref[...], weight_ref[...], column_ref[...], xb[...], xa[...], yb[...], ya[...]
    )
    write_slabs(out_ref, slabs)
    last_ref[...], y_last_ref[...] = slabs[-1], y_layer(slabs, dims, dims[1] - 1)
    none = jnp.zeros(y_last_ref.shape, jnp.float32)
    sums_ref[...] = jnp.concatenate(inner_sums(dims, slabs, none, mean_ref[...]), axis=0)


def face_kernel(dims, sums_ref, last_ref, y_last_ref, xa, ya, mean_ref, part_ref, up_ref):
    slab, width = dims[1] * dims[2], dims[0] * dims[2]
    mean = mean_ref[...]
    rank = mean.shape[0]
    layer = ya[:, :width]
    sums = [sums_ref[n * rank:(n + 1) * rank] for n in range(4)]
    for n, moved, k in ((1, xa[...], last_ref[...]), (2, layer, y_last_ref[...])):
        sums[n] = sums[n] + pair_sums(moved, speed_of(mean, moved) * k, halves(speed_of(mean, k) * k))
    part_ref[...] = packed_sums(sums)
    up_ref[:, :slab] = last_ref[...]
    up_ref[:, slab:] = layer


def pack_kernel(dims, field_ref, ya, yb, down_ref):
    lx, ly, lz = dims
    slab, width = ly * lz, lx * lz
    down_ref[:, :slab] = field_ref[:, slab:2 * slab]
    down_ref[:, slab:] = jnp.where(lane_index(width) < lz, yb[...], roll(ya[:, :width], lz))


def apply(left, right):
    left_high, left_low = halves(left)
    high, low = halves(right)
    return dot(
        jnp.concatenate([left_high, left_high, left_low], axis=1), jnp.concatenate([high, low, high], axis=0)
    )


def orient_stage(cells, sums, orient, table, mean, directions, basis=None):
    rank = orient.shape[0]
    plus, minus = signs(directions)
    sums = sums * (1.0 / cells)
    gram = jnp.concatenate([sums[:rank // 2, :rank], sums[:rank // 2, rank:]], axis=0)
    inner = []
    for d in range(3):
        block = sums[rank // 2 + d * rank:rank // 2 + (d + 1) * rank]
        inner += [-block[:, rank:], block[:, :rank].T]
    drift = -mm(jnp.concatenate(inner, axis=1), table)
    upper, inverse, drift = factor(gram, drift)
    spread = jnp.broadcast_to(mean, (rank, rank))
    solved = (1.0 + tumble) * unit(rank) - tumble * spread * spread.T + courant * mm(inverse, drift, (0, 0))
    rows = [(1.0 - tumble) * upper] + [courant * mm(inverse, part) for part in inner]
    rows = mm(jnp.concatenate(rows, axis=0), solved)
    mid_mean = mm(rows[:rank], spread)[:, :1]
    moved = apply(rows if basis is None else mm(rows, basis), orient)
    new = moved[:rank] + mid_mean * (tumble / (1.0 - tumble))
    for d in range(3):
        new = new + plus[d:d + 1] * moved[(1 + 2 * d) * rank:(2 + 2 * d) * rank]
        new = new + minus[d:d + 1] * moved[(2 + 2 * d) * rank:(3 + 2 * d) * rank]
    return inverse, new


def turn_kernel(
    cells, sums_ref, orient_ref, table_ref, mean_ref, e_ref,
    weight_ref, column_ref, mean_out, new_ref, inverse_ref, table_out,
):
    directions = e_ref[...]
    rank = orient_ref.shape[0]
    inverse, new = orient_stage(cells, sums_ref[...], orient_ref[...], table_ref[...], mean_ref[...], directions)
    new_ref[...] = new
    gram, table, mean = tables(new, directions)
    weights, column_ref[...] = stage_weights(gram, table, mean, inverse)
    _, inverse_v = factor(gram)
    inverse_ref[...] = inverse_v
    weight_ref[...] = mm(inverse_v, weights)
    mean_out[...] = mm(inverse_v, jnp.broadcast_to(mean, (rank, rank)))[:, :1]
    right = mm(table, inverse_v, (1, 1))
    for n in range(6):
        table_out[n * rank:(n + 1) * rank] = mm(inverse_v, right[n * rank:(n + 1) * rank])


def second_kernel(
    dims, field_ref, xa, ya, yb, second, behind, weight_ref, column_ref, mean_ref, field_out, sums_out
):
    slab, width = dims[1] * dims[2], dims[0] * dims[2]
    slabs, side = k_stage(
        dims, field_ref[...], weight_ref[...], column_ref[...], behind[:, :slab], xa[...], yb[...], ya[:, :width],
        (second[...], behind[:, slab:], ya[:, width:]),
    )
    write_slabs(field_out, slabs[:-1])
    sums_out[...] = packed_sums(inner_sums(dims, slabs, side, mean_ref[...]))


def last_kernel(
    cells, sums_ref, orient_ref, basis_ref, table_ref, mean_ref, e_ref, field_ref, x_ref, s_ref, v_ref, x_buffer, sems
):
    inverse, new = orient_stage(
        cells, sums_ref[...], orient_ref[...], table_ref[...], mean_ref[...], e_ref[...], basis_ref[...]
    )
    count = new.shape[1]
    parts = sems.shape[0]
    chunk = field_ref.shape[1] // parts

    copies = [
        pltpu.make_async_copy(
            x_buffer.at[pl.ds(n * chunk, chunk)], x_ref.at[pl.ds(n * chunk, chunk)], sems.at[n]
        )
        for n in range(parts)
    ]

    def x_part(n):
        def work():
            x_buffer[n * chunk:(n + 1) * chunk] = apply(inverse, field_ref[:, n * chunk:(n + 1) * chunk]).T
            copies[n].start()
        return work

    new_halves = halves(new)
    upper_v, inverse_v = factor(
        three(new_halves, new_halves, (1, 1)) * (1.0 / count), meanwhile=[x_part(n) for n in range(parts)]
    )
    s_ref[...] = upper_v.T
    v_ref[...] = apply(inverse_v, new)
    for copy in copies:
        copy.wait()


def shifted(axis, up):
    count = lax.axis_size(axis)
    step = 1 if up else count - 1
    return [(i, (i + step) % count) for i in range(count)]


def scatter_gather_sum(part):
    count = lax.axis_size("gx") * lax.axis_size("gy")
    rows, width = part.shape
    padded = -(-rows // count) * count
    if padded != rows:
        part = jnp.pad(part, ((0, padded - rows), (0, 0)))
    split = part.reshape(count, padded // count, width)
    mine = lax.all_to_all(split, ("gx", "gy"), 0, 0).sum(axis=0)
    every = lax.all_to_all(jnp.broadcast_to(mine[None], split.shape), ("gx", "gy"), 0, 0)
    return every.reshape(padded, width)[:rows]


def swapped(value, bits):
    count = lax.axis_size("gx") * lax.axis_size("gy")
    return lax.ppermute(value, ("gx", "gy"), [(i, i ^ bits) for i in range(count)])


def sum_of_four(value, step):
    near, far, cross = [swapped(value, n * step) for n in (1, 2, 3)]
    return (value + near) + (far + cross)


def all_sum(part, meanwhile=(lambda value: value,) * 2):
    nx, ny = lax.axis_size("gx"), lax.axis_size("gy")
    rows = part.shape[0] // 2
    if nx != 4 or ny != 8 or rows % 8:
        for work in meanwhile:
            part = work(part)
        return scatter_gather_sum(part)
    first = lax.axis_index("gy") % 2 == 0
    total = part + swapped(part, 1)
    mine = jnp.where(first, total[:rows], total[rows:])
    for step, work in zip((ny, 2), meanwhile):
        mine = work(sum_of_four(mine, step))
    other = swapped(mine, 1)
    return jnp.concatenate([jnp.where(first, mine, other), jnp.where(first, other, mine)], axis=0)


def up(value, axis):
    return lax.ppermute(value, axis, shifted(axis, True))


def down(value, axis):
    return lax.ppermute(value, axis, shifted(axis, False))


def shards(spatial_factor, coupling, orient_factor, directions):
    dims = spatial_factor.shape[:3]
    lx, ly, lz = dims
    rank = spatial_factor.shape[-1]
    sites = lx * ly * lz
    count = orient_factor.shape[0]
    cells = sites * lax.axis_size("gx") * lax.axis_size("gy")
    whole, slab, layer = (rank, sites), (rank, ly * lz), (rank, lx * lz)
    two_layers, more = (rank, 2 * lx * lz), (rank, ly * lz + lx * lz)
    summed = (7 * rank // 2, 2 * rank)
    field, first, last, y_first, y_last = call(
        functools.partial(enter_kernel, dims), [whole, slab, slab, layer, layer], spatial_factor.reshape(sites, rank)
    )
    xb, xa, yb, ya = up(last, "gx"), down(first, "gx"), up(y_last, "gy"), down(y_first, "gy")
    basis = [(rank, count), (6 * rank, rank)]
    column_shape, weight_shape = (rank, 1), (rank, 8 * rank)
    orient = orient_factor.T
    table, mean, weights, column = call(
        table_kernel, [basis[1], column_shape, weight_shape, column_shape], orient, directions, coupling
    )
    near = (field, xb, xa, yb, ya, weights, column)
    first, y_first = call(functools.partial(edge_kernel, dims), [slab, two_layers], *near)
    xa, ya = down(first, "gx"), down(y_first, "gy")
    field, part, last, y_last = call(
        functools.partial(first_kernel, dims), [whole, (4 * rank, 2 * rank), slab, layer], *near, mean,
        cost=pl.CostEstimate(flops=10**9, bytes_accessed=8 * 10**6, transcendentals=0),
    )
    part, behind = call(
        functools.partial(face_kernel, dims), [summed, more], part, last, y_last, xa, ya, mean
    )
    yb, behind = up(y_last, "gy"), up(behind, "gx")
    halo = {"yb": yb, "behind": behind}

    def with_layer(value):
        value, halo["yb"] = lax.optimization_barrier((value, halo["yb"]))
        (packed,) = call(functools.partial(pack_kernel, dims), [more], field, ya, halo["yb"])
        halo["second"] = down(packed, "gx")
        return value

    sums = all_sum(part, (with_layer, lambda value: value))
    weights, column, mean, new, inverse, table = call(
        functools.partial(turn_kernel, cells),
        [weight_shape, column_shape, column_shape, basis[0], (rank, rank), basis[1]],
        sums, orient, table, mean, directions, cost=pl.CostEstimate(flops=1, bytes_accessed=1, transcendentals=0),
    )
    field, part = call(
        functools.partial(second_kernel, dims), [whole, summed],
        field, xa, ya, halo["yb"], halo["second"], halo["behind"], weights, column, mean,
    )
    new_spatial, new_coupling, new_orient = call(
        functools.partial(last_kernel, cells), [(sites, rank), (rank, rank), (rank, count)],
        all_sum(part), new, inverse, table, mean, directions, field, far_out=(0,),
        scratch=(pltpu.VMEM((sites, rank), jnp.float32), pltpu.SemaphoreType.DMA((4,))),
    )
    return new_spatial.reshape(spatial_factor.shape), new_coupling, new_orient.T


def solution(mesh):
    return jax.shard_map(
        shards,
        mesh=mesh,
        in_specs=(P("gx", "gy", None, None), P(), P(), P()),
        out_specs=(P("gx", "gy", None, None), P(), P()),
        check_vma=False,
    )
```

```python
import functools

import jax
import jax.numpy as jnp
from jax import lax
from jax.experimental import pallas as pl
from jax.experimental.pallas import tpu as pltpu
from jax.sharding import PartitionSpec as P

courant = 0.3
tumble = 0.2
highest = lax.Precision.HIGHEST
half = jnp.bfloat16
LANES = 128
VMEM_BYTES = 32 * 1024 * 1024


def mm(left, right, contract=(1, 0)):
    return lax.dot_general(
        left, right, (((contract[0],), (contract[1],)), ((), ())),
        precision=highest, preferred_element_type=jnp.float32,
    )


def dot(left, right, contract=(1, 0)):
    return lax.dot_general(
        left, right, (((contract[0],), (contract[1],)), ((), ())),
        preferred_element_type=jnp.float32,
    )


def halves(value):
    high = value.astype(half)
    return high, (value - high.astype(jnp.float32)).astype(half)


def stacked(pairs, axis=0):
    return tuple(jnp.concatenate(part, axis=axis) for part in zip(*pairs))


def three(left, right, contract):
    left_high, left_low = left
    right_high, right_low = right
    rows = left_high.shape[0]
    both = dot(jnp.concatenate(left, axis=0), right_high, contract)
    return both[:rows] + both[rows:] + dot(left_high, right_low, contract)


def lane_index(width):
    return lax.broadcasted_iota(jnp.int32, (1, width), 1)


def roll(value, shift):
    width = value.shape[1]
    shift = shift % width
    return value if shift == 0 else pltpu.roll(value, shift, axis=1)


def slabs_of(value, dims):
    slab = dims[1] * dims[2]
    return [value[:, x * slab:(x + 1) * slab] for x in range(dims[0])]


def y_layer(slabs, dims, index):
    lx, ly, lz = dims
    width = lx * lz
    start = index * lz // width * width
    owner = lane_index(width) // lz
    layer = None
    for x in range(lx):
        line = roll(slabs[x][:, start:start + width], lz * x - (index * lz - start))
        layer = line if layer is None else jnp.where(owner == x, line, layer)
    return layer


def y_ahead(slab, edge, dims):
    lz, width = dims[2], edge.shape[1]
    moved = roll(slab, -lz)
    last = jnp.where(lane_index(width) >= width - lz, edge, moved[:, -width:])
    return jnp.concatenate([moved[:, :-width], last], axis=1)


def y_behind(slab, edge, dims):
    lz, width = dims[2], edge.shape[1]
    moved = roll(slab, lz)
    first = jnp.where(lane_index(width) < lz, edge, moved[:, :width])
    return jnp.concatenate([first, moved[:, width:]], axis=1)


def z_ahead(slab, dims):
    lz = dims[2]
    place = lane_index(slab.shape[1]) % lz
    return jnp.where(place == lz - 1, roll(slab, lz - 1), roll(slab, -1))


def z_behind(slab, dims):
    lz = dims[2]
    place = lane_index(slab.shape[1]) % lz
    return jnp.where(place == 0, roll(slab, 1 - lz), roll(slab, 1))


def motility(density):
    return 1.0 / (1.0 + density * density)


def speed_of(column, value):
    return motility(jnp.sum(column * value, axis=0, keepdims=True))


def signs(directions):
    return jnp.maximum(directions, 0.0), jnp.maximum(-directions, 0.0)


def tables(orient, directions):
    rank, count = orient.shape
    plus, minus = signs(directions)
    high, low = halves(orient)
    both = jnp.concatenate([high, low], axis=0)
    stack = [orient * part[d:d + 1] for d in range(3) for part in (plus, minus)]
    stack_high, stack_low = halves(jnp.concatenate(stack, axis=0))
    scale = 1.0 / count

    def product(left_high, left_low):
        wide = dot(left_high, both, (1, 1))
        return (wide[:, :rank] + wide[:, rank:] + dot(left_low, high, (1, 1))) * scale

    return product(high, low), product(stack_high, stack_low), jnp.sum(orient, axis=1, keepdims=True) * scale


def unit(rank):
    row = lax.broadcasted_iota(jnp.int32, (rank, rank), 0)
    col = lax.broadcasted_iota(jnp.int32, (rank, rank), 1)
    return jnp.where(row == col, 1.0, 0.0).astype(jnp.float32)


def stage_weights(gram, table, mean, into):
    rank = mean.shape[0]
    blocks = [table[d * rank:(d + 1) * rank] for d in range(6)]
    total = blocks[0] + blocks[1] + blocks[2] + blocks[3] + blocks[4] + blocks[5]
    spread = jnp.broadcast_to(mean, (rank, rank))
    first = (1.0 - tumble) * gram + tumble * spread * spread.T
    weights = mm(jnp.concatenate([first, -courant * total, courant * table], axis=0), into)
    weights = jnp.concatenate([weights[b * rank:(b + 1) * rank] for b in range(8)], axis=1)
    return weights, mm(into, spread, (0, 0))[:, :1]


def factor(gram, beside=None, meanwhile=()):
    rank = gram.shape[0]
    group = 8
    shape = (group, 2 * rank)
    eye = unit(rank)
    diag_row = jnp.sum(eye * gram, axis=0, keepdims=True)
    diag_column = jnp.sum(eye * gram, axis=1, keepdims=True)
    scale = lax.rsqrt(diag_row)
    scale_column = lax.rsqrt(diag_column)
    wide = jnp.concatenate([gram * scale_column * scale, eye], axis=1)
    blocks = rank // group
    fields = [wide] if beside is None else [wide, beside * scale_column]
    fields = [[f[b * group:(b + 1) * group] for b in range(blocks)] for f in fields]
    rows = fields[0]
    done = [list(f) for f in fields]
    place = lax.broadcasted_iota(jnp.int32, shape, 0)

    def spread(value, i):
        return jnp.broadcast_to(value[i:i + 1], value.shape)

    for b in range(blocks):
        start = b * group
        cols = {
            c: [jnp.broadcast_to(rows[c][:, start + j:start + j + 1], shape) for j in range(group)]
            for c in range(b, blocks)
        }
        for j in range(0, group, 2):
            first, second = cols[b][j], cols[b][j + 1]
            p, o, q = spread(first, j), spread(second, j), spread(second, j + 1)
            root = lax.rsqrt(p)
            along = o * root
            root_next = lax.rsqrt(q - along * along)
            for f, out in zip(fields, done):
                width = f[b].shape[1]
                upper = spread(f[b], j) * root[:, :width]
                lower = (spread(f[b], j + 1) - along[:, :width] * upper) * root_next[:, :width]
                at = place[:, :width]
                out[b] = jnp.where(at == j, upper, jnp.where(at == j + 1, lower, out[b]))
            over = 1.0 / (p * q - o * o)

            def solve(value):
                width = value.shape[1]
                upper, lower = spread(value, j), spread(value, j + 1)
                return (
                    q[:, :width] * upper - o[:, :width] * lower,
                    p[:, :width] * lower - o[:, :width] * upper,
                )

            def remove(value, left, right, up, low, scale):
                width = value.shape[1]
                part = left[:, :width] * up + right[:, :width] * low
                return value - (part if scale is None else part * scale[:, :width])

            later = [solve(cols[b][n]) for n in range(j + 2, group)]
            pivots = [solve(f[b]) for f in fields]
            if j < group - 2:
                left = jnp.where(place > j + 1, first, 0.0)
                right = jnp.where(place > j + 1, second, 0.0)
                for n, (up, low) in enumerate(later):
                    cols[b][j + 2 + n] = remove(cols[b][j + 2 + n], left, right, up, low, over)
                for f, (up, low) in zip(fields, pivots):
                    f[b] = remove(f[b], left, right, up, low, over)
            later = [(up * over, low * over) for up, low in later]
            pivots = [(up * over[:, :up.shape[1]], low * over[:, :up.shape[1]]) for up, low in pivots]
            for c in range(b + 1, blocks):
                left, right = cols[c][j], cols[c][j + 1]
                for n, (up, low) in enumerate(later):
                    cols[c][j + 2 + n] = remove(cols[c][j + 2 + n], left, right, up, low, None)
                for f, (up, low) in zip(fields, pivots):
                    f[c] = remove(f[c], left, right, up, low, None)
        if b < len(meanwhile):
            meanwhile[b]()
    done = [jnp.concatenate(d, axis=0) for d in done]
    both = done[0] * jnp.concatenate([diag_row * scale, scale], axis=1)
    return (both[:, :rank], both[:, rank:], *done[1:])


def call(body, outs, *args, far_out=(), scratch=(), cost=None):
    def space(n, far):
        return pl.BlockSpec(memory_space=pltpu.HBM if n in far else pltpu.VMEM)

    return pl.pallas_call(
        body,
        out_shape=[jax.ShapeDtypeStruct(shape, jnp.float32) for shape in outs],
        in_specs=[pl.BlockSpec(memory_space=pltpu.VMEM)] * len(args),
        out_specs=[space(n, far_out) for n in range(len(outs))],
        scratch_shapes=list(scratch),
        cost_estimate=cost,
        compiler_params=pltpu.CompilerParams(vmem_limit_bytes=VMEM_BYTES),
    )(*args)


def enter_kernel(dims, x_ref, field_ref, first_ref, last_ref, y_first_ref, y_last_ref):
    field = x_ref[...].T
    field_ref[...] = field
    slabs = slabs_of(field, dims)
    first_ref[...], last_ref[...] = slabs[0], slabs[-1]
    y_first_ref[...], y_last_ref[...] = y_layer(slabs, dims, 0), y_layer(slabs, dims, dims[1] - 1)


def table_kernel(orient_ref, e_ref, s_ref, table_ref, mean_ref, weight_ref, column_ref):
    _, table, mean = tables(orient_ref[...], e_ref[...])
    table_ref[...] = table
    mean_ref[...] = mean
    weight_ref[...], column_ref[...] = stage_weights(unit(mean.shape[0]), table, mean, s_ref[...].T)


CENTRE, X_BEHIND, X_AHEAD, Y_BEHIND, Y_AHEAD, Z_BEHIND, Z_AHEAD = range(7)


def triple(value):
    high, low = halves(value)
    return jnp.concatenate([high, low, high], axis=0)


class Weights:
    def __init__(self, weights, column):
        self.column = column
        self.rank = rank = column.shape[0]
        blocks = [weights[:, n * rank:(n + 1) * rank] for n in range(8)]
        high, low = halves(jnp.concatenate(blocks, axis=0))
        self.left = jnp.concatenate([high, high, low], axis=1)

    def times(self, value, start=CENTRE, stop=Z_AHEAD + 1):
        rank = self.rank
        flux = triple(speed_of(self.column, value) * value)
        wide = dot(self.left[(1 + start) * rank:(1 + stop) * rank], flux)
        return {n: wide[(n - start) * rank:(n - start + 1) * rank] for n in range(start, stop)}

    def one(self, value, n):
        return self.times(value, n, n + 1)[n]

    def whole(self, value, part, dims):
        return (
            dot(self.left[:self.rank], triple(value)) + part[CENTRE]
            + z_behind(part[Z_BEHIND], dims) + z_ahead(part[Z_AHEAD], dims)
        )


def k_edges(dims, field, weights, column, xb, xa, yb, ya):
    lx, ly, lz = dims
    width = lx * lz
    w = Weights(weights, column)
    slabs = slabs_of(field, dims)
    from_behind, from_ahead = w.one(xb, X_BEHIND), w.one(xa, X_AHEAD)
    before = w.one(yb, Y_BEHIND)
    part = w.times(slabs[0])
    first = (
        w.whole(slabs[0], part, dims) + from_behind + w.one(slabs[1], X_AHEAD)
        + y_behind(part[Y_BEHIND], before, dims)
        + y_ahead(part[Y_AHEAD], roll(w.one(ya, Y_AHEAD), -lz), dims)
    )
    layers = jnp.concatenate([y_layer(slabs, dims, 0), y_layer(slabs, dims, 1)], axis=1)
    part = w.times(layers)
    after = w.one(y_layer(slabs, dims, 2), Y_AHEAD)
    lane = lane_index(width)
    over_y = [before + part[Y_AHEAD][:, width:], part[Y_BEHIND][:, :width] + after]
    over_x = []
    for n in range(2):
        here = slice(n * width, (n + 1) * width)
        over_x.append(
            jnp.where(lane < lz, roll(from_behind[:, :width], -n * lz), roll(part[X_BEHIND][:, here], lz))
            + jnp.where(
                lane >= width - lz, roll(from_ahead[:, :width], -(n + 1) * lz), roll(part[X_AHEAD][:, here], -lz)
            )
        )
    return first, w.whole(layers, part, dims) + jnp.concatenate([x + y for x, y in zip(over_x, over_y)], axis=1)


def k_stage(dims, field, weights, column, xb, xa, yb, ya, further=None):
    lx, ly, lz = dims
    slab, width = ly * lz, lx * lz
    w = Weights(weights, column)
    fields = slabs_of(field, dims)
    if further is not None:
        fields.append(xa)
        second, corner_before, layer_next = further
        last = w.one(second[:, :slab], X_AHEAD)
    else:
        last = w.one(xa, X_AHEAD)
    parts = [w.times(f) for f in fields]
    from_behind = [w.one(xb, X_BEHIND)] + [p[X_BEHIND] for p in parts[:-1]]
    from_ahead = [p[X_AHEAD] for p in parts[1:]] + [last]
    layer_before = w.one(yb, Y_BEHIND)
    if further is None:
        layer = {Y_AHEAD: w.one(ya, Y_AHEAD)}
    else:
        layer = w.times(ya)
        corners = w.times(second[:, slab:], X_AHEAD, Y_AHEAD + 1)

    results = []
    for x, value in enumerate(fields):
        line_before = roll(layer_before, -lz * x) if x < lx else corners[Y_BEHIND]
        line_after = roll(layer[Y_AHEAD], -lz * (x + 1)) if x < lx else roll(corners[Y_AHEAD], -2 * lz)
        results.append(
            w.whole(value, parts[x], dims) + from_behind[x] + from_ahead[x]
            + y_behind(parts[x][Y_BEHIND], line_before, dims) + y_ahead(parts[x][Y_AHEAD], line_after, dims)
        )
    if further is None:
        return results
    lane = lane_index(width)
    side = (
        w.whole(ya, layer, dims)
        + jnp.where(lane < lz, roll(w.one(corner_before, X_BEHIND), lz), roll(layer[X_BEHIND], lz))
        + jnp.where(lane >= width - lz, roll(corners[X_AHEAD], -2 * lz), roll(layer[X_AHEAD], -lz))
        + y_layer([p[Y_BEHIND] for p in parts[:lx]], dims, ly - 1) + w.one(layer_next, Y_AHEAD)
    )
    return results, side


def pair_sums(left, right, q):
    return three(halves(left), stacked([halves(right), q]), (1, 1))


def inner_sums(dims, fields, layer, mean):
    lx, ly, lz = dims
    rank = mean.shape[0]
    speeds = [speed_of(mean, f) for f in fields]
    split = [halves(f) for f in fields]
    sums = [jnp.zeros((rank, 2 * rank), jnp.float32) for _ in range(4)]
    for x in range(lx):
        k = fields[x]
        q = halves(speeds[x] * k)
        pairs = [(0, split[x], split[x])]
        if x + 1 < len(fields):
            pairs.append((1, split[x + 1], halves(speeds[x + 1] * k)))
        for n, moved in ((2, y_ahead(k, roll(layer, -lz * (x + 1)), dims)), (3, z_ahead(k, dims))):
            pairs.append((n, halves(moved), halves(speed_of(mean, moved) * k)))
        for n, left, right in pairs:
            sums[n] = sums[n] + three(left, stacked([right, q]), (1, 1))
    return sums


def packed_sums(sums):
    rank = sums[0].shape[0]
    low = lane_index(2 * rank) < rank
    centre = jnp.where(low, -roll(sums[0], rank), sums[0])
    gram = sums[0][:, :rank]
    rows = [jnp.concatenate([gram[:rank // 2], gram[rank // 2:]], axis=1)]
    for part in sums[1:]:
        rows.append(centre + jnp.where(low, part, -part))
    return jnp.concatenate(rows, axis=0)


def write_slabs(ref, slabs):
    slab = slabs[0].shape[1]
    for x, value in enumerate(slabs):
        ref[:, x * slab:(x + 1) * slab] = value


def edge_kernel(dims, field_ref, xb, xa, yb, ya, weight_ref, column_ref, first_ref, y_first_ref):
    first_ref[...], y_first_ref[...] = k_edges(
        dims, field_ref[...], weight_ref[...], column_ref[...], xb[...], xa[...], yb[...], ya[...]
    )


def first_kernel(
    dims, field_ref, xb, xa, yb, ya, weight_ref, column_ref, mean_ref, out_ref, sums_ref, last_ref, y_last_ref
):
    slabs = k_stage(
        dims, field_ref[...], weight_ref[...], column_ref[...], xb[...], xa[...], yb[...], ya[...]
    )
    write_slabs(out_ref, slabs)
    last_ref[...], y_last_ref[...] = slabs[-1], y_layer(slabs, dims, dims[1] - 1)
    none = jnp.zeros(y_last_ref.shape, jnp.float32)
    sums_ref[...] = jnp.concatenate(inner_sums(dims, slabs, none, mean_ref[...]), axis=0)


def face_kernel(dims, sums_ref, last_ref, y_last_ref, xa, ya, mean_ref, part_ref, up_ref):
    slab, width = dims[1] * dims[2], dims[0] * dims[2]
    mean = mean_ref[...]
    rank = mean.shape[0]
    layer = ya[:, :width]
    sums = [sums_ref[n * rank:(n + 1) * rank] for n in range(4)]
    for n, moved, k in ((1, xa[...], last_ref[...]), (2, layer, y_last_ref[...])):
        sums[n] = sums[n] + pair_sums(moved, speed_of(mean, moved) * k, halves(speed_of(mean, k) * k))
    part_ref[...] = packed_sums(sums)
    up_ref[:, :slab] = last_ref[...]
    up_ref[:, slab:] = layer


def pack_kernel(dims, field_ref, ya, yb, down_ref):
    lx, ly, lz = dims
    slab, width = ly * lz, lx * lz
    down_ref[:, :slab] = field_ref[:, slab:2 * slab]
    down_ref[:, slab:] = jnp.where(lane_index(width) < lz, yb[...], roll(ya[:, :width], lz))


def apply(left, right):
    left_high, left_low = halves(left)
    high, low = halves(right)
    return dot(
        jnp.concatenate([left_high, left_high, left_low], axis=1), jnp.concatenate([high, low, high], axis=0)
    )


def orient_stage(cells, sums, orient, table, mean, directions, basis=None):
    rank = orient.shape[0]
    plus, minus = signs(directions)
    sums = sums * (1.0 / cells)
    gram = jnp.concatenate([sums[:rank // 2, :rank], sums[:rank // 2, rank:]], axis=0)
    inner = []
    for d in range(3):
        block = sums[rank // 2 + d * rank:rank // 2 + (d + 1) * rank]
        inner += [-block[:, rank:], block[:, :rank].T]
    drift = -mm(jnp.concatenate(inner, axis=1), table)
    upper, inverse, drift = factor(gram, drift)
    spread = jnp.broadcast_to(mean, (rank, rank))
    solved = (1.0 + tumble) * unit(rank) - tumble * spread * spread.T + courant * mm(inverse, drift, (0, 0))
    rows = [(1.0 - tumble) * upper] + [courant * mm(inverse, part) for part in inner]
    rows = mm(jnp.concatenate(rows, axis=0), solved)
    mid_mean = mm(rows[:rank], spread)[:, :1]
    moved = apply(rows if basis is None else mm(rows, basis), orient)
    new = moved[:rank] + mid_mean * (tumble / (1.0 - tumble))
    for d in range(3):
        new = new + plus[d:d + 1] * moved[(1 + 2 * d) * rank:(2 + 2 * d) * rank]
        new = new + minus[d:d + 1] * moved[(2 + 2 * d) * rank:(3 + 2 * d) * rank]
    return inverse, new


def turn_kernel(
    cells, sums_ref, orient_ref, table_ref, mean_ref, e_ref,
    weight_ref, column_ref, mean_out, new_ref, inverse_ref, table_out,
):
    directions = e_ref[...]
    rank = orient_ref.shape[0]
    inverse, new = orient_stage(cells, sums_ref[...], orient_ref[...], table_ref[...], mean_ref[...], directions)
    new_ref[...] = new
    gram, table, mean = tables(new, directions)
    weights, column_ref[...] = stage_weights(gram, table, mean, inverse)
    _, inverse_v = factor(gram)
    inverse_ref[...] = inverse_v
    weight_ref[...] = mm(inverse_v, weights)
    mean_out[...] = mm(inverse_v, jnp.broadcast_to(mean, (rank, rank)))[:, :1]
    right = mm(table, inverse_v, (1, 1))
    for n in range(6):
        table_out[n * rank:(n + 1) * rank] = mm(inverse_v, right[n * rank:(n + 1) * rank])


def second_kernel(
    dims, field_ref, xa, ya, yb, second, behind, weight_ref, column_ref, mean_ref, field_out, sums_out
):
    slab, width = dims[1] * dims[2], dims[0] * dims[2]
    slabs, side = k_stage(
        dims, field_ref[...], weight_ref[...], column_ref[...], behind[:, :slab], xa[...], yb[...], ya[:, :width],
        (second[...], behind[:, slab:], ya[:, width:]),
    )
    write_slabs(field_out, slabs[:-1])
    sums_out[...] = packed_sums(inner_sums(dims, slabs, side, mean_ref[...]))


def last_kernel(
    cells, sums_ref, orient_ref, basis_ref, table_ref, mean_ref, e_ref, field_ref, x_ref, s_ref, v_ref, x_buffer, v_buffer, sems
):
    inverse, new = orient_stage(
        cells, sums_ref[...], orient_ref[...], table_ref[...], mean_ref[...], e_ref[...], basis_ref[...]
    )
    count = new.shape[1]
    parts = v_buffer.shape[0]
    chunk = field_ref.shape[1] // parts

    copies = [
        pltpu.make_async_copy(
            x_buffer.at[pl.ds(n * chunk, chunk)], x_ref.at[pl.ds(n * chunk, chunk)], sems.at[n]
        )
        for n in range(parts)
    ]

    def x_part(n):
        def work():
            x_buffer[n * chunk:(n + 1) * chunk] = apply(inverse, field_ref[:, n * chunk:(n + 1) * chunk]).T
            copies[n].start()
        return work

    new_halves = halves(new)
    upper_v, inverse_v = factor(
        three(new_halves, new_halves, (1, 1)) * (1.0 / count), meanwhile=[x_part(n) for n in range(parts)]
    )
    s_ref[...] = upper_v.T
    wide = count // parts
    for n in range(parts):
        v_buffer[n] = apply(inverse_v, new[:, n * wide:(n + 1) * wide])
        copies.append(
            pltpu.make_async_copy(v_buffer.at[n], v_ref.at[:, pl.ds(n * wide, wide)], sems.at[parts + n])
        )
        copies[-1].start()
    for copy in copies:
        copy.wait()


def shifted(axis, up):
    count = lax.axis_size(axis)
    step = 1 if up else count - 1
    return [(i, (i + step) % count) for i in range(count)]


def scatter_gather_sum(part):
    count = lax.axis_size("gx") * lax.axis_size("gy")
    rows, width = part.shape
    padded = -(-rows // count) * count
    if padded != rows:
        part = jnp.pad(part, ((0, padded - rows), (0, 0)))
    split = part.reshape(count, padded // count, width)
    mine = lax.all_to_all(split, ("gx", "gy"), 0, 0).sum(axis=0)
    every = lax.all_to_all(jnp.broadcast_to(mine[None], split.shape), ("gx", "gy"), 0, 0)
    return every.reshape(padded, width)[:rows]


def swapped(value, bits):
    count = lax.axis_size("gx") * lax.axis_size("gy")
    return lax.ppermute(value, ("gx", "gy"), [(i, i ^ bits) for i in range(count)])


def sum_of_four(value, step):
    near, far, cross = [swapped(value, n * step) for n in (1, 2, 3)]
    return (value + near) + (far + cross)


def all_sum(part, meanwhile=(lambda value: value,) * 2):
    nx, ny = lax.axis_size("gx"), lax.axis_size("gy")
    rows = part.shape[0] // 2
    if nx != 4 or ny != 8 or rows % 8:
        for work in meanwhile:
            part = work(part)
        return scatter_gather_sum(part)
    first = lax.axis_index("gy") % 2 == 0
    total = part + swapped(part, 1)
    mine = jnp.where(first, total[:rows], total[rows:])
    for step, work in zip((ny, 2), meanwhile):
        mine = work(sum_of_four(mine, step))
    other = swapped(mine, 1)
    return jnp.concatenate([jnp.where(first, mine, other), jnp.where(first, other, mine)], axis=0)


def up(value, axis):
    return lax.ppermute(value, axis, shifted(axis, True))


def down(value, axis):
    return lax.ppermute(value, axis, shifted(axis, False))


def shards(spatial_factor, coupling, orient_factor, directions):
    dims = spatial_factor.shape[:3]
    lx, ly, lz = dims
    rank = spatial_factor.shape[-1]
    sites = lx * ly * lz
    count = orient_factor.shape[0]
    cells = sites * lax.axis_size("gx") * lax.axis_size("gy")
    whole, slab, layer = (rank, sites), (rank, ly * lz), (rank, lx * lz)
    two_layers, more = (rank, 2 * lx * lz), (rank, ly * lz + lx * lz)
    summed = (7 * rank // 2, 2 * rank)
    field, first, last, y_first, y_last = call(
        functools.partial(enter_kernel, dims), [whole, slab, slab, layer, layer], spatial_factor.reshape(sites, rank)
    )
    xb, xa, yb, ya = up(last, "gx"), down(first, "gx"), up(y_last, "gy"), down(y_first, "gy")
    basis = [(rank, count), (6 * rank, rank)]
    column_shape, weight_shape = (rank, 1), (rank, 8 * rank)
    orient = orient_factor.T
    table, mean, weights, column = call(
        table_kernel, [basis[1], column_shape, weight_shape, column_shape], orient, directions, coupling
    )
    near = (field, xb, xa, yb, ya, weights, column)
    first, y_first = call(functools.partial(edge_kernel, dims), [slab, two_layers], *near)
    xa, ya = down(first, "gx"), down(y_first, "gy")
    field, part, last, y_last = call(
        functools.partial(first_kernel, dims), [whole, (4 * rank, 2 * rank), slab, layer], *near, mean,
        cost=pl.CostEstimate(flops=10**9, bytes_accessed=8 * 10**6, transcendentals=0),
    )
    part, behind = call(
        functools.partial(face_kernel, dims), [summed, more], part, last, y_last, xa, ya, mean
    )
    yb, behind = up(y_last, "gy"), up(behind, "gx")
    halo = {"yb": yb, "behind": behind}

    def with_layer(value):
        value, halo["yb"] = lax.optimization_barrier((value, halo["yb"]))
        (packed,) = call(functools.partial(pack_kernel, dims), [more], field, ya, halo["yb"])
        halo["second"] = down(packed, "gx")
        return value

    sums = all_sum(part, (with_layer, lambda value: value))
    weights, column, mean, new, inverse, table = call(
        functools.partial(turn_kernel, cells),
        [weight_shape, column_shape, column_shape, basis[0], (rank, rank), basis[1]],
        sums, orient, table, mean, directions, cost=pl.CostEstimate(flops=1, bytes_accessed=1, transcendentals=0),
    )
    field, part = call(
        functools.partial(second_kernel, dims), [whole, summed],
        field, xa, ya, halo["yb"], halo["second"], halo["behind"], weights, column, mean,
    )
    new_spatial, new_coupling, new_orient = call(
        functools.partial(last_kernel, cells), [(sites, rank), (rank, rank), (rank, count)],
        all_sum(part), new, inverse, table, mean, directions, field, far_out=(0, 2),
        scratch=(
            pltpu.VMEM((sites, rank), jnp.float32),
            pltpu.VMEM((4, rank, count // 4), jnp.float32),
            pltpu.SemaphoreType.DMA((8,)),
        ),
    )
    return new_spatial.reshape(spatial_factor.shape), new_coupling, new_orient.T


def solution(mesh):
    return jax.shard_map(
        shards,
        mesh=mesh,
        in_specs=(P("gx", "gy", None, None), P(), P(), P()),
        out_specs=(P("gx", "gy", None, None), P(), P()),
        check_vma=False,
    )
```

```python
import functools

import jax
import jax.numpy as jnp
from jax import lax
from jax.experimental import pallas as pl
from jax.experimental.pallas import tpu as pltpu
from jax.sharding import PartitionSpec as P

courant = 0.3
tumble = 0.2
highest = lax.Precision.HIGHEST
half = jnp.bfloat16
LANES = 128
VMEM_BYTES = 32 * 1024 * 1024


def mm(left, right, contract=(1, 0)):
    return lax.dot_general(
        left, right, (((contract[0],), (contract[1],)), ((), ())),
        precision=highest, preferred_element_type=jnp.float32,
    )


def dot(left, right, contract=(1, 0)):
    return lax.dot_general(
        left, right, (((contract[0],), (contract[1],)), ((), ())),
        preferred_element_type=jnp.float32,
    )


def halves(value):
    high = value.astype(half)
    return high, (value - high.astype(jnp.float32)).astype(half)


def stacked(pairs, axis=0):
    return tuple(jnp.concatenate(part, axis=axis) for part in zip(*pairs))


def three(left, right, contract):
    left_high, left_low = left
    right_high, right_low = right
    rows = left_high.shape[0]
    both = dot(jnp.concatenate(left, axis=0), right_high, contract)
    return both[:rows] + both[rows:] + dot(left_high, right_low, contract)


def lane_index(width):
    return lax.broadcasted_iota(jnp.int32, (1, width), 1)


def roll(value, shift):
    width = value.shape[1]
    shift = shift % width
    return value if shift == 0 else pltpu.roll(value, shift, axis=1)


def slabs_of(value, dims):
    slab = dims[1] * dims[2]
    return [value[:, x * slab:(x + 1) * slab] for x in range(dims[0])]


def y_layer(slabs, dims, index):
    lx, ly, lz = dims
    width = lx * lz
    start = index * lz // width * width
    owner = lane_index(width) // lz
    layer = None
    for x in range(lx):
        line = roll(slabs[x][:, start:start + width], lz * x - (index * lz - start))
        layer = line if layer is None else jnp.where(owner == x, line, layer)
    return layer


def y_ahead(slab, edge, dims):
    lz, width = dims[2], edge.shape[1]
    moved = roll(slab, -lz)
    last = jnp.where(lane_index(width) >= width - lz, edge, moved[:, -width:])
    return jnp.concatenate([moved[:, :-width], last], axis=1)


def y_behind(slab, edge, dims):
    lz, width = dims[2], edge.shape[1]
    moved = roll(slab, lz)
    first = jnp.where(lane_index(width) < lz, edge, moved[:, :width])
    return jnp.concatenate([first, moved[:, width:]], axis=1)


def z_ahead(slab, dims):
    lz = dims[2]
    place = lane_index(slab.shape[1]) % lz
    return jnp.where(place == lz - 1, roll(slab, lz - 1), roll(slab, -1))


def z_behind(slab, dims):
    lz = dims[2]
    place = lane_index(slab.shape[1]) % lz
    return jnp.where(place == 0, roll(slab, 1 - lz), roll(slab, 1))


def motility(density):
    return 1.0 / (1.0 + density * density)


def speed_of(column, value):
    return motility(jnp.sum(column * value, axis=0, keepdims=True))


def signs(directions):
    return jnp.maximum(directions, 0.0), jnp.maximum(-directions, 0.0)


def tables(orient, directions):
    rank, count = orient.shape
    plus, minus = signs(directions)
    high, low = halves(orient)
    both = jnp.concatenate([high, low], axis=0)
    stack = [orient * part[d:d + 1] for d in range(3) for part in (plus, minus)]
    stack_high, stack_low = halves(jnp.concatenate(stack, axis=0))
    scale = 1.0 / count

    def product(left_high, left_low):
        wide = dot(left_high, both, (1, 1))
        return (wide[:, :rank] + wide[:, rank:] + dot(left_low, high, (1, 1))) * scale

    return product(high, low), product(stack_high, stack_low), jnp.sum(orient, axis=1, keepdims=True) * scale


def unit(rank):
    row = lax.broadcasted_iota(jnp.int32, (rank, rank), 0)
    col = lax.broadcasted_iota(jnp.int32, (rank, rank), 1)
    return jnp.where(row == col, 1.0, 0.0).astype(jnp.float32)


def stage_weights(gram, table, mean, into):
    rank = mean.shape[0]
    blocks = [table[d * rank:(d + 1) * rank] for d in range(6)]
    total = blocks[0] + blocks[1] + blocks[2] + blocks[3] + blocks[4] + blocks[5]
    spread = jnp.broadcast_to(mean, (rank, rank))
    first = (1.0 - tumble) * gram + tumble * spread * spread.T
    weights = apply(jnp.concatenate([first, -courant * total, courant * table], axis=0), into)
    weights = jnp.concatenate([weights[b * rank:(b + 1) * rank] for b in range(8)], axis=1)
    return weights, mm(into, spread, (0, 0))[:, :1]


def factor(gram, beside=None, meanwhile=()):
    rank = gram.shape[0]
    group = 8
    shape = (group, 2 * rank)
    eye = unit(rank)
    diag_row = jnp.sum(eye * gram, axis=0, keepdims=True)
    diag_column = jnp.sum(eye * gram, axis=1, keepdims=True)
    scale = lax.rsqrt(diag_row)
    scale_column = lax.rsqrt(diag_column)
    wide = jnp.concatenate([gram * scale_column * scale, eye], axis=1)
    blocks = rank // group
    fields = [wide] if beside is None else [wide, beside * scale_column]
    fields = [[f[b * group:(b + 1) * group] for b in range(blocks)] for f in fields]
    rows = fields[0]
    done = [list(f) for f in fields]
    place = lax.broadcasted_iota(jnp.int32, shape, 0)

    def spread(value, i):
        return jnp.broadcast_to(value[i:i + 1], value.shape)

    for b in range(blocks):
        start = b * group
        cols = {
            c: [jnp.broadcast_to(rows[c][:, start + j:start + j + 1], shape) for j in range(group)]
            for c in range(b, blocks)
        }
        for j in range(0, group, 2):
            first, second = cols[b][j], cols[b][j + 1]
            p, o, q = spread(first, j), spread(second, j), spread(second, j + 1)
            root = lax.rsqrt(p)
            along = o * root
            root_next = lax.rsqrt(q - along * along)
            for f, out in zip(fields, done):
                width = f[b].shape[1]
                upper = spread(f[b], j) * root[:, :width]
                lower = (spread(f[b], j + 1) - along[:, :width] * upper) * root_next[:, :width]
                at = place[:, :width]
                out[b] = jnp.where(at == j, upper, jnp.where(at == j + 1, lower, out[b]))
            over = 1.0 / (p * q - o * o)

            def solve(value):
                width = value.shape[1]
                upper, lower = spread(value, j), spread(value, j + 1)
                return (
                    q[:, :width] * upper - o[:, :width] * lower,
                    p[:, :width] * lower - o[:, :width] * upper,
                )

            def remove(value, left, right, up, low, scale):
                width = value.shape[1]
                part = left[:, :width] * up + right[:, :width] * low
                return value - (part if scale is None else part * scale[:, :width])

            later = [solve(cols[b][n]) for n in range(j + 2, group)]
            pivots = [solve(f[b]) for f in fields]
            if j < group - 2:
                left = jnp.where(place > j + 1, first, 0.0)
                right = jnp.where(place > j + 1, second, 0.0)
                for n, (up, low) in enumerate(later):
                    cols[b][j + 2 + n] = remove(cols[b][j + 2 + n], left, right, up, low, over)
                for f, (up, low) in zip(fields, pivots):
                    f[b] = remove(f[b], left, right, up, low, over)
            later = [(up * over, low * over) for up, low in later]
            pivots = [(up * over[:, :up.shape[1]], low * over[:, :up.shape[1]]) for up, low in pivots]
            for c in range(b + 1, blocks):
                left, right = cols[c][j], cols[c][j + 1]
                for n, (up, low) in enumerate(later):
                    cols[c][j + 2 + n] = remove(cols[c][j + 2 + n], left, right, up, low, None)
                for f, (up, low) in zip(fields, pivots):
                    f[c] = remove(f[c], left, right, up, low, None)
        if b < len(meanwhile):
            meanwhile[b]()
    done = [jnp.concatenate(d, axis=0) for d in done]
    both = done[0] * jnp.concatenate([diag_row * scale, scale], axis=1)
    return (both[:, :rank], both[:, rank:], *done[1:])


def call(body, outs, *args, far_out=(), scratch=(), cost=None):
    def space(n, far):
        return pl.BlockSpec(memory_space=pltpu.HBM if n in far else pltpu.VMEM)

    return pl.pallas_call(
        body,
        out_shape=[jax.ShapeDtypeStruct(shape, jnp.float32) for shape in outs],
        in_specs=[pl.BlockSpec(memory_space=pltpu.VMEM)] * len(args),
        out_specs=[space(n, far_out) for n in range(len(outs))],
        scratch_shapes=list(scratch),
        cost_estimate=cost,
        compiler_params=pltpu.CompilerParams(vmem_limit_bytes=VMEM_BYTES),
    )(*args)


def enter_kernel(dims, x_ref, field_ref, first_ref, last_ref, y_first_ref, y_last_ref):
    field = x_ref[...].T
    field_ref[...] = field
    slabs = slabs_of(field, dims)
    first_ref[...], last_ref[...] = slabs[0], slabs[-1]
    y_first_ref[...], y_last_ref[...] = y_layer(slabs, dims, 0), y_layer(slabs, dims, dims[1] - 1)


def table_kernel(orient_ref, e_ref, s_ref, table_ref, mean_ref, weight_ref, column_ref):
    _, table, mean = tables(orient_ref[...], e_ref[...])
    table_ref[...] = table
    mean_ref[...] = mean
    weight_ref[...], column_ref[...] = stage_weights(unit(mean.shape[0]), table, mean, s_ref[...].T)


CENTRE, X_BEHIND, X_AHEAD, Y_BEHIND, Y_AHEAD, Z_BEHIND, Z_AHEAD = range(7)


def triple(value):
    high, low = halves(value)
    return jnp.concatenate([high, low, high], axis=0)


class Weights:
    def __init__(self, weights, column):
        self.column = column
        self.rank = rank = column.shape[0]
        blocks = [weights[:, n * rank:(n + 1) * rank] for n in range(8)]
        high, low = halves(jnp.concatenate(blocks, axis=0))
        self.left = jnp.concatenate([high, high, low], axis=1)

    def times(self, value, start=CENTRE, stop=Z_AHEAD + 1):
        rank = self.rank
        flux = triple(speed_of(self.column, value) * value)
        wide = dot(self.left[(1 + start) * rank:(1 + stop) * rank], flux)
        return {n: wide[(n - start) * rank:(n - start + 1) * rank] for n in range(start, stop)}

    def one(self, value, n):
        return self.times(value, n, n + 1)[n]

    def whole(self, value, part, dims):
        return (
            dot(self.left[:self.rank], triple(value)) + part[CENTRE]
            + z_behind(part[Z_BEHIND], dims) + z_ahead(part[Z_AHEAD], dims)
        )


def k_edges(dims, field, weights, column, xb, xa, yb, ya):
    lx, ly, lz = dims
    width = lx * lz
    w = Weights(weights, column)
    slabs = slabs_of(field, dims)
    from_behind, from_ahead = w.one(xb, X_BEHIND), w.one(xa, X_AHEAD)
    before = w.one(yb, Y_BEHIND)
    part = w.times(slabs[0])
    first = (
        w.whole(slabs[0], part, dims) + from_behind + w.one(slabs[1], X_AHEAD)
        + y_behind(part[Y_BEHIND], before, dims)
        + y_ahead(part[Y_AHEAD], roll(w.one(ya, Y_AHEAD), -lz), dims)
    )
    layers = jnp.concatenate([y_layer(slabs, dims, 0), y_layer(slabs, dims, 1)], axis=1)
    part = w.times(layers)
    after = w.one(y_layer(slabs, dims, 2), Y_AHEAD)
    lane = lane_index(width)
    over_y = [before + part[Y_AHEAD][:, width:], part[Y_BEHIND][:, :width] + after]
    over_x = []
    for n in range(2):
        here = slice(n * width, (n + 1) * width)
        over_x.append(
            jnp.where(lane < lz, roll(from_behind[:, :width], -n * lz), roll(part[X_BEHIND][:, here], lz))
            + jnp.where(
                lane >= width - lz, roll(from_ahead[:, :width], -(n + 1) * lz), roll(part[X_AHEAD][:, here], -lz)
            )
        )
    return first, w.whole(layers, part, dims) + jnp.concatenate([x + y for x, y in zip(over_x, over_y)], axis=1)


def k_stage(dims, field, weights, column, xb, xa, yb, ya, further=None):
    lx, ly, lz = dims
    slab, width = ly * lz, lx * lz
    w = Weights(weights, column)
    fields = slabs_of(field, dims)
    if further is not None:
        fields.append(xa)
        second, corner_before, layer_next = further
        last = w.one(second[:, :slab], X_AHEAD)
    else:
        last = w.one(xa, X_AHEAD)
    parts = [w.times(f) for f in fields]
    from_behind = [w.one(xb, X_BEHIND)] + [p[X_BEHIND] for p in parts[:-1]]
    from_ahead = [p[X_AHEAD] for p in parts[1:]] + [last]
    layer_before = w.one(yb, Y_BEHIND)
    if further is None:
        layer = {Y_AHEAD: w.one(ya, Y_AHEAD)}
    else:
        layer = w.times(ya)
        corners = w.times(second[:, slab:], X_AHEAD, Y_AHEAD + 1)

    results = []
    for x, value in enumerate(fields):
        line_before = roll(layer_before, -lz * x) if x < lx else corners[Y_BEHIND]
        line_after = roll(layer[Y_AHEAD], -lz * (x + 1)) if x < lx else roll(corners[Y_AHEAD], -2 * lz)
        results.append(
            w.whole(value, parts[x], dims) + from_behind[x] + from_ahead[x]
            + y_behind(parts[x][Y_BEHIND], line_before, dims) + y_ahead(parts[x][Y_AHEAD], line_after, dims)
        )
    if further is None:
        return results
    lane = lane_index(width)
    side = (
        w.whole(ya, layer, dims)
        + jnp.where(lane < lz, roll(w.one(corner_before, X_BEHIND), lz), roll(layer[X_BEHIND], lz))
        + jnp.where(lane >= width - lz, roll(corners[X_AHEAD], -2 * lz), roll(layer[X_AHEAD], -lz))
        + y_layer([p[Y_BEHIND] for p in parts[:lx]], dims, ly - 1) + w.one(layer_next, Y_AHEAD)
    )
    return results, side


def pair_sums(left, right, q):
    return three(halves(left), stacked([halves(right), q]), (1, 1))


def inner_sums(dims, fields, layer, mean):
    lx, ly, lz = dims
    rank = mean.shape[0]
    speeds = [speed_of(mean, f) for f in fields]
    split = [halves(f) for f in fields]
    sums = [jnp.zeros((rank, 2 * rank), jnp.float32) for _ in range(4)]
    for x in range(lx):
        k = fields[x]
        q = halves(speeds[x] * k)
        pairs = [(0, split[x], split[x])]
        if x + 1 < len(fields):
            pairs.append((1, split[x + 1], halves(speeds[x + 1] * k)))
        for n, moved in ((2, y_ahead(k, roll(layer, -lz * (x + 1)), dims)), (3, z_ahead(k, dims))):
            pairs.append((n, halves(moved), halves(speed_of(mean, moved) * k)))
        for n, left, right in pairs:
            sums[n] = sums[n] + three(left, stacked([right, q]), (1, 1))
    return sums


def packed_sums(sums):
    rank = sums[0].shape[0]
    low = lane_index(2 * rank) < rank
    centre = jnp.where(low, -roll(sums[0], rank), sums[0])
    gram = sums[0][:, :rank]
    rows = [jnp.concatenate([gram[:rank // 2], gram[rank // 2:]], axis=1)]
    for part in sums[1:]:
        rows.append(centre + jnp.where(low, part, -part))
    return jnp.concatenate(rows, axis=0)


def write_slabs(ref, slabs):
    slab = slabs[0].shape[1]
    for x, value in enumerate(slabs):
        ref[:, x * slab:(x + 1) * slab] = value


def edge_kernel(dims, field_ref, xb, xa, yb, ya, weight_ref, column_ref, first_ref, y_first_ref):
    first_ref[...], y_first_ref[...] = k_edges(
        dims, field_ref[...], weight_ref[...], column_ref[...], xb[...], xa[...], yb[...], ya[...]
    )


def first_kernel(
    dims, field_ref, xb, xa, yb, ya, weight_ref, column_ref, mean_ref, out_ref, sums_ref, last_ref, y_last_ref
):
    slabs = k_stage(
        dims, field_ref[...], weight_ref[...], column_ref[...], xb[...], xa[...], yb[...], ya[...]
    )
    write_slabs(out_ref, slabs)
    last_ref[...], y_last_ref[...] = slabs[-1], y_layer(slabs, dims, dims[1] - 1)
    none = jnp.zeros(y_last_ref.shape, jnp.float32)
    sums_ref[...] = jnp.concatenate(inner_sums(dims, slabs, none, mean_ref[...]), axis=0)


def face_kernel(dims, sums_ref, last_ref, y_last_ref, xa, ya, mean_ref, part_ref, up_ref):
    slab, width = dims[1] * dims[2], dims[0] * dims[2]
    mean = mean_ref[...]
    rank = mean.shape[0]
    layer = ya[:, :width]
    sums = [sums_ref[n * rank:(n + 1) * rank] for n in range(4)]
    for n, moved, k in ((1, xa[...], last_ref[...]), (2, layer, y_last_ref[...])):
        sums[n] = sums[n] + pair_sums(moved, speed_of(mean, moved) * k, halves(speed_of(mean, k) * k))
    part_ref[...] = packed_sums(sums)
    up_ref[:, :slab] = last_ref[...]
    up_ref[:, slab:] = layer


def pack_kernel(dims, field_ref, ya, yb, down_ref):
    lx, ly, lz = dims
    slab, width = ly * lz, lx * lz
    down_ref[:, :slab] = field_ref[:, slab:2 * slab]
    down_ref[:, slab:] = jnp.where(lane_index(width) < lz, yb[...], roll(ya[:, :width], lz))


def apply(left, right):
    left_high, left_low = halves(left)
    high, low = halves(right)
    return dot(
        jnp.concatenate([left_high, left_high, left_low], axis=1), jnp.concatenate([high, low, high], axis=0)
    )


def orient_stage(cells, sums, orient, table, mean, directions, basis=None):
    rank = orient.shape[0]
    plus, minus = signs(directions)
    sums = sums * (1.0 / cells)
    gram = jnp.concatenate([sums[:rank // 2, :rank], sums[:rank // 2, rank:]], axis=0)
    inner = []
    for d in range(3):
        block = sums[rank // 2 + d * rank:rank // 2 + (d + 1) * rank]
        inner += [-block[:, rank:], block[:, :rank].T]
    drift = -mm(jnp.concatenate(inner, axis=1), table)
    upper, inverse, drift = factor(gram, drift)
    spread = jnp.broadcast_to(mean, (rank, rank))
    solved = (1.0 + tumble) * unit(rank) - tumble * spread * spread.T + courant * mm(inverse, drift, (0, 0))
    rows = [(1.0 - tumble) * upper] + [courant * mm(inverse, part) for part in inner]
    rows = apply(jnp.concatenate(rows, axis=0), solved)
    mid_mean = mm(rows[:rank], spread)[:, :1]
    moved = apply(rows if basis is None else apply(rows, basis), orient)
    new = moved[:rank] + mid_mean * (tumble / (1.0 - tumble))
    for d in range(3):
        new = new + plus[d:d + 1] * moved[(1 + 2 * d) * rank:(2 + 2 * d) * rank]
        new = new + minus[d:d + 1] * moved[(2 + 2 * d) * rank:(3 + 2 * d) * rank]
    return inverse, new


def turn_kernel(
    cells, sums_ref, orient_ref, table_ref, mean_ref, e_ref,
    weight_ref, column_ref, mean_out, new_ref, inverse_ref, table_out,
):
    directions = e_ref[...]
    rank = orient_ref.shape[0]
    inverse, new = orient_stage(cells, sums_ref[...], orient_ref[...], table_ref[...], mean_ref[...], directions)
    new_ref[...] = new
    gram, table, mean = tables(new, directions)
    weights, column_ref[...] = stage_weights(gram, table, mean, inverse)
    _, inverse_v = factor(gram)
    inverse_ref[...] = inverse_v
    weight_ref[...] = mm(inverse_v, weights)
    mean_out[...] = mm(inverse_v, jnp.broadcast_to(mean, (rank, rank)))[:, :1]
    right = mm(table, inverse_v, (1, 1))
    for n in range(6):
        table_out[n * rank:(n + 1) * rank] = mm(inverse_v, right[n * rank:(n + 1) * rank])


def second_kernel(
    dims, field_ref, xa, ya, yb, second, behind, weight_ref, column_ref, mean_ref, field_out, sums_out
):
    slab, width = dims[1] * dims[2], dims[0] * dims[2]
    slabs, side = k_stage(
        dims, field_ref[...], weight_ref[...], column_ref[...], behind[:, :slab], xa[...], yb[...], ya[:, :width],
        (second[...], behind[:, slab:], ya[:, width:]),
    )
    write_slabs(field_out, slabs[:-1])
    sums_out[...] = packed_sums(inner_sums(dims, slabs, side, mean_ref[...]))


def last_kernel(
    cells, sums_ref, orient_ref, basis_ref, table_ref, mean_ref, e_ref, field_ref, x_ref, s_ref, v_ref, x_buffer, v_buffer, sems
):
    inverse, new = orient_stage(
        cells, sums_ref[...], orient_ref[...], table_ref[...], mean_ref[...], e_ref[...], basis_ref[...]
    )
    count = new.shape[1]
    parts = v_buffer.shape[0]
    chunk = field_ref.shape[1] // parts

    copies = [
        pltpu.make_async_copy(
            x_buffer.at[pl.ds(n * chunk, chunk)], x_ref.at[pl.ds(n * chunk, chunk)], sems.at[n]
        )
        for n in range(parts)
    ]

    def x_part(n):
        def work():
            x_buffer[n * chunk:(n + 1) * chunk] = apply(inverse, field_ref[:, n * chunk:(n + 1) * chunk]).T
            copies[n].start()
        return work

    new_halves = halves(new)
    upper_v, inverse_v = factor(
        three(new_halves, new_halves, (1, 1)) * (1.0 / count), meanwhile=[x_part(n) for n in range(parts)]
    )
    s_ref[...] = upper_v.T
    wide = count // parts
    for n in range(parts):
        v_buffer[n] = apply(inverse_v, new[:, n * wide:(n + 1) * wide])
        copies.append(
            pltpu.make_async_copy(v_buffer.at[n], v_ref.at[:, pl.ds(n * wide, wide)], sems.at[parts + n])
        )
        copies[-1].start()
    for copy in copies:
        copy.wait()


def shifted(axis, up):
    count = lax.axis_size(axis)
    step = 1 if up else count - 1
    return [(i, (i + step) % count) for i in range(count)]


def scatter_gather_sum(part):
    count = lax.axis_size("gx") * lax.axis_size("gy")
    rows, width = part.shape
    padded = -(-rows // count) * count
    if padded != rows:
        part = jnp.pad(part, ((0, padded - rows), (0, 0)))
    split = part.reshape(count, padded // count, width)
    mine = lax.all_to_all(split, ("gx", "gy"), 0, 0).sum(axis=0)
    every = lax.all_to_all(jnp.broadcast_to(mine[None], split.shape), ("gx", "gy"), 0, 0)
    return every.reshape(padded, width)[:rows]


def swapped(value, bits):
    count = lax.axis_size("gx") * lax.axis_size("gy")
    return lax.ppermute(value, ("gx", "gy"), [(i, i ^ bits) for i in range(count)])


def sum_of_four(value, step):
    near, far, cross = [swapped(value, n * step) for n in (1, 2, 3)]
    return (value + near) + (far + cross)


def all_sum(part, meanwhile=(lambda value: value,) * 2):
    nx, ny = lax.axis_size("gx"), lax.axis_size("gy")
    rows = part.shape[0] // 2
    if nx != 4 or ny != 8 or rows % 8:
        for work in meanwhile:
            part = work(part)
        return scatter_gather_sum(part)
    first = lax.axis_index("gy") % 2 == 0
    total = part + swapped(part, 1)
    mine = jnp.where(first, total[:rows], total[rows:])
    for step, work in zip((ny, 2), meanwhile):
        mine = work(sum_of_four(mine, step))
    other = swapped(mine, 1)
    return jnp.concatenate([jnp.where(first, mine, other), jnp.where(first, other, mine)], axis=0)


def up(value, axis):
    return lax.ppermute(value, axis, shifted(axis, True))


def down(value, axis):
    return lax.ppermute(value, axis, shifted(axis, False))


def shards(spatial_factor, coupling, orient_factor, directions):
    dims = spatial_factor.shape[:3]
    lx, ly, lz = dims
    rank = spatial_factor.shape[-1]
    sites = lx * ly * lz
    count = orient_factor.shape[0]
    cells = sites * lax.axis_size("gx") * lax.axis_size("gy")
    whole, slab, layer = (rank, sites), (rank, ly * lz), (rank, lx * lz)
    two_layers, more = (rank, 2 * lx * lz), (rank, ly * lz + lx * lz)
    summed = (7 * rank // 2, 2 * rank)
    field, first, last, y_first, y_last = call(
        functools.partial(enter_kernel, dims), [whole, slab, slab, layer, layer], spatial_factor.reshape(sites, rank)
    )
    xb, xa, yb, ya = up(last, "gx"), down(first, "gx"), up(y_last, "gy"), down(y_first, "gy")
    basis = [(rank, count), (6 * rank, rank)]
    column_shape, weight_shape = (rank, 1), (rank, 8 * rank)
    orient = orient_factor.T
    table, mean, weights, column = call(
        table_kernel, [basis[1], column_shape, weight_shape, column_shape], orient, directions, coupling
    )
    near = (field, xb, xa, yb, ya, weights, column)
    first, y_first = call(functools.partial(edge_kernel, dims), [slab, two_layers], *near)
    xa, ya = down(first, "gx"), down(y_first, "gy")
    field, part, last, y_last = call(
        functools.partial(first_kernel, dims), [whole, (4 * rank, 2 * rank), slab, layer], *near, mean,
        cost=pl.CostEstimate(flops=10**9, bytes_accessed=8 * 10**6, transcendentals=0),
    )
    part, behind = call(
        functools.partial(face_kernel, dims), [summed, more], part, last, y_last, xa, ya, mean
    )
    yb, behind = up(y_last, "gy"), up(behind, "gx")
    halo = {"yb": yb, "behind": behind}

    def with_layer(value):
        value, halo["yb"] = lax.optimization_barrier((value, halo["yb"]))
        (packed,) = call(functools.partial(pack_kernel, dims), [more], field, ya, halo["yb"])
        halo["second"] = down(packed, "gx")
        return value

    sums = all_sum(part, (with_layer, lambda value: value))
    weights, column, mean, new, inverse, table = call(
        functools.partial(turn_kernel, cells),
        [weight_shape, column_shape, column_shape, basis[0], (rank, rank), basis[1]],
        sums, orient, table, mean, directions, cost=pl.CostEstimate(flops=1, bytes_accessed=1, transcendentals=0),
    )
    field, part = call(
        functools.partial(second_kernel, dims), [whole, summed],
        field, xa, ya, halo["yb"], halo["second"], halo["behind"], weights, column, mean,
    )
    new_spatial, new_coupling, new_orient = call(
        functools.partial(last_kernel, cells), [(sites, rank), (rank, rank), (rank, count)],
        all_sum(part), new, inverse, table, mean, directions, field, far_out=(0, 2),
        scratch=(
            pltpu.VMEM((sites, rank), jnp.float32),
            pltpu.VMEM((4, rank, count // 4), jnp.float32),
            pltpu.SemaphoreType.DMA((8,)),
        ),
    )
    return new_spatial.reshape(spatial_factor.shape), new_coupling, new_orient.T


def solution(mesh):
    return jax.shard_map(
        shards,
        mesh=mesh,
        in_specs=(P("gx", "gy", None, None), P(), P(), P()),
        out_specs=(P("gx", "gy", None, None), P(), P()),
        check_vma=False,
    )
```

```python
import functools

import jax
import jax.numpy as jnp
from jax import lax
from jax.experimental import pallas as pl
from jax.experimental.pallas import tpu as pltpu
from jax.sharding import PartitionSpec as P

courant = 0.3
tumble = 0.2
highest = lax.Precision.HIGHEST
half = jnp.bfloat16
LANES = 128
VMEM_BYTES = 32 * 1024 * 1024


def mm(left, right, contract=(1, 0)):
    return lax.dot_general(
        left, right, (((contract[0],), (contract[1],)), ((), ())),
        precision=highest, preferred_element_type=jnp.float32,
    )


def dot(left, right, contract=(1, 0)):
    return lax.dot_general(
        left, right, (((contract[0],), (contract[1],)), ((), ())),
        preferred_element_type=jnp.float32,
    )


def halves(value):
    high = value.astype(half)
    return high, (value - high.astype(jnp.float32)).astype(half)


def stacked(pairs, axis=0):
    return tuple(jnp.concatenate(part, axis=axis) for part in zip(*pairs))


def three(left, right, contract):
    left_high, left_low = left
    right_high, right_low = right
    rows = left_high.shape[0]
    both = dot(jnp.concatenate(left, axis=0), right_high, contract)
    return both[:rows] + both[rows:] + dot(left_high, right_low, contract)


def lane_index(width):
    return lax.broadcasted_iota(jnp.int32, (1, width), 1)


def roll(value, shift):
    width = value.shape[1]
    shift = shift % width
    return value if shift == 0 else pltpu.roll(value, shift, axis=1)


def slabs_of(value, dims):
    slab = dims[1] * dims[2]
    return [value[:, x * slab:(x + 1) * slab] for x in range(dims[0])]


def y_layer(slabs, dims, index):
    lx, ly, lz = dims
    width = lx * lz
    start = index * lz // width * width
    owner = lane_index(width) // lz
    layer = None
    for x in range(lx):
        line = roll(slabs[x][:, start:start + width], lz * x - (index * lz - start))
        layer = line if layer is None else jnp.where(owner == x, line, layer)
    return layer


def y_ahead(slab, edge, dims):
    lz, width = dims[2], edge.shape[1]
    moved = roll(slab, -lz)
    last = jnp.where(lane_index(width) >= width - lz, edge, moved[:, -width:])
    return jnp.concatenate([moved[:, :-width], last], axis=1)


def y_behind(slab, edge, dims):
    lz, width = dims[2], edge.shape[1]
    moved = roll(slab, lz)
    first = jnp.where(lane_index(width) < lz, edge, moved[:, :width])
    return jnp.concatenate([first, moved[:, width:]], axis=1)


def z_ahead(slab, dims):
    lz = dims[2]
    place = lane_index(slab.shape[1]) % lz
    return jnp.where(place == lz - 1, roll(slab, lz - 1), roll(slab, -1))


def z_behind(slab, dims):
    lz = dims[2]
    place = lane_index(slab.shape[1]) % lz
    return jnp.where(place == 0, roll(slab, 1 - lz), roll(slab, 1))


def motility(density):
    return 1.0 / (1.0 + density * density)


def speed_of(column, value):
    return motility(jnp.sum(column * value, axis=0, keepdims=True))


def signs(directions):
    return jnp.maximum(directions, 0.0), jnp.maximum(-directions, 0.0)


def tables(orient, directions):
    rank, count = orient.shape
    plus, minus = signs(directions)
    high, low = halves(orient)
    both = jnp.concatenate([high, low], axis=0)
    stack = [orient * part[d:d + 1] for d in range(3) for part in (plus, minus)]
    stack_high, stack_low = halves(jnp.concatenate(stack, axis=0))
    scale = 1.0 / count

    def product(left_high, left_low):
        wide = dot(left_high, both, (1, 1))
        return (wide[:, :rank] + wide[:, rank:] + dot(left_low, high, (1, 1))) * scale

    return product(high, low), product(stack_high, stack_low), jnp.sum(orient, axis=1, keepdims=True) * scale


def unit(rank):
    row = lax.broadcasted_iota(jnp.int32, (rank, rank), 0)
    col = lax.broadcasted_iota(jnp.int32, (rank, rank), 1)
    return jnp.where(row == col, 1.0, 0.0).astype(jnp.float32)


def stage_weights(gram, table, mean, into):
    rank = mean.shape[0]
    blocks = [table[d * rank:(d + 1) * rank] for d in range(6)]
    total = blocks[0] + blocks[1] + blocks[2] + blocks[3] + blocks[4] + blocks[5]
    spread = jnp.broadcast_to(mean, (rank, rank))
    first = (1.0 - tumble) * gram + tumble * spread * spread.T
    weights = apply(jnp.concatenate([first, -courant * total, courant * table], axis=0), into)
    weights = jnp.concatenate([weights[b * rank:(b + 1) * rank] for b in range(8)], axis=1)
    return weights, mm(into, spread, (0, 0))[:, :1]


def factor(gram, beside=None, meanwhile=()):
    rank = gram.shape[0]
    group = 8
    shape = (group, 2 * rank)
    eye = unit(rank)
    diag_row = jnp.sum(eye * gram, axis=0, keepdims=True)
    diag_column = jnp.sum(eye * gram, axis=1, keepdims=True)
    scale = lax.rsqrt(diag_row)
    scale_column = lax.rsqrt(diag_column)
    wide = jnp.concatenate([gram * scale_column * scale, eye], axis=1)
    blocks = rank // group
    fields = [wide] if beside is None else [wide, beside * scale_column]
    fields = [[f[b * group:(b + 1) * group] for b in range(blocks)] for f in fields]
    rows = fields[0]
    done = [list(f) for f in fields]
    place = lax.broadcasted_iota(jnp.int32, shape, 0)

    def spread(value, i):
        return jnp.broadcast_to(value[i:i + 1], value.shape)

    for b in range(blocks):
        start = b * group
        cols = {
            c: [jnp.broadcast_to(rows[c][:, start + j:start + j + 1], shape) for j in range(group)]
            for c in range(b, blocks)
        }
        for j in range(0, group, 2):
            first, second = cols[b][j], cols[b][j + 1]
            p, o, q = spread(first, j), spread(second, j), spread(second, j + 1)
            root = lax.rsqrt(p)
            along = o * root
            root_next = lax.rsqrt(q - along * along)
            for f, out in zip(fields, done):
                width = f[b].shape[1]
                upper = spread(f[b], j) * root[:, :width]
                lower = (spread(f[b], j + 1) - along[:, :width] * upper) * root_next[:, :width]
                at = place[:, :width]
                out[b] = jnp.where(at == j, upper, jnp.where(at == j + 1, lower, out[b]))
            over = 1.0 / (p * q - o * o)

            def solve(value):
                width = value.shape[1]
                upper, lower = spread(value, j), spread(value, j + 1)
                return (
                    q[:, :width] * upper - o[:, :width] * lower,
                    p[:, :width] * lower - o[:, :width] * upper,
                )

            def remove(value, left, right, up, low, scale):
                width = value.shape[1]
                part = left[:, :width] * up + right[:, :width] * low
                return value - (part if scale is None else part * scale[:, :width])

            later = [solve(cols[b][n]) for n in range(j + 2, group)]
            pivots = [solve(f[b]) for f in fields]
            if j < group - 2:
                left = jnp.where(place > j + 1, first, 0.0)
                right = jnp.where(place > j + 1, second, 0.0)
                for n, (up, low) in enumerate(later):
                    cols[b][j + 2 + n] = remove(cols[b][j + 2 + n], left, right, up, low, over)
                for f, (up, low) in zip(fields, pivots):
                    f[b] = remove(f[b], left, right, up, low, over)
            later = [(up * over, low * over) for up, low in later]
            pivots = [(up * over[:, :up.shape[1]], low * over[:, :up.shape[1]]) for up, low in pivots]
            for c in range(b + 1, blocks):
                left, right = cols[c][j], cols[c][j + 1]
                for n, (up, low) in enumerate(later):
                    cols[c][j + 2 + n] = remove(cols[c][j + 2 + n], left, right, up, low, None)
                for f, (up, low) in zip(fields, pivots):
                    f[c] = remove(f[c], left, right, up, low, None)
        if b < len(meanwhile):
            meanwhile[b]()
    done = [jnp.concatenate(d, axis=0) for d in done]
    both = done[0] * jnp.concatenate([diag_row * scale, scale], axis=1)
    return (both[:, :rank], both[:, rank:], *done[1:])


def call(body, outs, *args, far_out=(), scratch=(), cost=None):
    def space(n, far):
        return pl.BlockSpec(memory_space=pltpu.HBM if n in far else pltpu.VMEM)

    return pl.pallas_call(
        body,
        out_shape=[jax.ShapeDtypeStruct(shape, jnp.float32) for shape in outs],
        in_specs=[pl.BlockSpec(memory_space=pltpu.VMEM)] * len(args),
        out_specs=[space(n, far_out) for n in range(len(outs))],
        scratch_shapes=list(scratch),
        cost_estimate=cost,
        compiler_params=pltpu.CompilerParams(vmem_limit_bytes=VMEM_BYTES),
    )(*args)


def enter_kernel(dims, x_ref, field_ref, first_ref, last_ref, y_first_ref, y_last_ref):
    field = x_ref[...].T
    field_ref[...] = field
    slabs = slabs_of(field, dims)
    first_ref[...], last_ref[...] = slabs[0], slabs[-1]
    y_first_ref[...], y_last_ref[...] = y_layer(slabs, dims, 0), y_layer(slabs, dims, dims[1] - 1)


def table_kernel(
    dims, orient_ref, e_ref, s_ref, field_ref, table_ref, mean_ref, weight_ref, column_ref, first_ref, layers_ref
):
    _, table, mean = tables(orient_ref[...], e_ref[...])
    table_ref[...] = table
    mean_ref[...] = mean
    weights, column = stage_weights(unit(mean.shape[0]), table, mean, s_ref[...].T)
    weight_ref[...], column_ref[...] = weights, column
    first_ref[...], layers_ref[...] = k_edges_inside(dims, field_ref[...], weights, column)


CENTRE, X_BEHIND, X_AHEAD, Y_BEHIND, Y_AHEAD, Z_BEHIND, Z_AHEAD = range(7)


def triple(value):
    high, low = halves(value)
    return jnp.concatenate([high, low, high], axis=0)


class Weights:
    def __init__(self, weights, column):
        self.column = column
        self.rank = rank = column.shape[0]
        blocks = [weights[:, n * rank:(n + 1) * rank] for n in range(8)]
        high, low = halves(jnp.concatenate(blocks, axis=0))
        self.left = jnp.concatenate([high, high, low], axis=1)

    def times(self, value, start=CENTRE, stop=Z_AHEAD + 1):
        rank = self.rank
        flux = triple(speed_of(self.column, value) * value)
        wide = dot(self.left[(1 + start) * rank:(1 + stop) * rank], flux)
        return {n: wide[(n - start) * rank:(n - start + 1) * rank] for n in range(start, stop)}

    def one(self, value, n):
        return self.times(value, n, n + 1)[n]

    def whole(self, value, part, dims):
        return (
            dot(self.left[:self.rank], triple(value)) + part[CENTRE]
            + z_behind(part[Z_BEHIND], dims) + z_ahead(part[Z_AHEAD], dims)
        )


def k_edges_inside(dims, field, weights, column):
    lx, ly, lz = dims
    width = lx * lz
    w = Weights(weights, column)
    slabs = slabs_of(field, dims)
    none = jnp.zeros((field.shape[0], width), jnp.float32)
    part = w.times(slabs[0])
    first = (
        w.whole(slabs[0], part, dims) + w.one(slabs[1], X_AHEAD)
        + y_behind(part[Y_BEHIND], none, dims) + y_ahead(part[Y_AHEAD], none, dims)
    )
    layers = jnp.concatenate([y_layer(slabs, dims, 0), y_layer(slabs, dims, 1)], axis=1)
    part = w.times(layers)
    lane = lane_index(width)
    over_y = [
        part[Y_AHEAD][:, width:], part[Y_BEHIND][:, :width] + w.one(y_layer(slabs, dims, 2), Y_AHEAD)
    ]
    sums = []
    for n in range(2):
        here = slice(n * width, (n + 1) * width)
        sums.append(
            over_y[n] + jnp.where(lane < lz, 0.0, roll(part[X_BEHIND][:, here], lz))
            + jnp.where(lane >= width - lz, 0.0, roll(part[X_AHEAD][:, here], -lz))
        )
    return first, w.whole(layers, part, dims) + jnp.concatenate(sums, axis=1)


def k_edges(dims, first, layers, weights, column, xb, xa, yb, ya):
    lx, ly, lz = dims
    width = lx * lz
    w = Weights(weights, column)
    from_behind, from_ahead = w.one(xb, X_BEHIND), w.one(xa[:, :width], X_AHEAD)
    before, after = w.one(yb, Y_BEHIND), w.one(ya, Y_AHEAD)
    lane = lane_index(width)
    low, high = lane < lz, lane >= width - lz
    first = first + from_behind
    first = jnp.concatenate([
        first[:, :width] + jnp.where(low, before, 0.0),
        first[:, width:-width],
        first[:, -width:] + jnp.where(high, roll(after, -lz), 0.0),
    ], axis=1)
    sides = [
        jnp.where(low, roll(from_behind[:, :width], -n * lz), 0.0)
        + jnp.where(high, roll(from_ahead, -(n + 1) * lz), 0.0)
        for n in range(2)
    ]
    return first, layers + jnp.concatenate([sides[0] + before, sides[1]], axis=1)


def k_stage(dims, field, weights, column, xb, xa, yb, ya, further=None):
    lx, ly, lz = dims
    slab, width = ly * lz, lx * lz
    w = Weights(weights, column)
    fields = slabs_of(field, dims)
    if further is not None:
        fields.append(xa)
        second, corner_before, layer_next = further
        last = w.one(second[:, :slab], X_AHEAD)
    else:
        last = w.one(xa, X_AHEAD)
    parts = [w.times(f) for f in fields]
    from_behind = [w.one(xb, X_BEHIND)] + [p[X_BEHIND] for p in parts[:-1]]
    from_ahead = [p[X_AHEAD] for p in parts[1:]] + [last]
    layer_before = w.one(yb, Y_BEHIND)
    if further is None:
        layer = {Y_AHEAD: w.one(ya, Y_AHEAD)}
    else:
        layer = w.times(ya)
        corners = w.times(second[:, slab:], X_AHEAD, Y_AHEAD + 1)

    results = []
    for x, value in enumerate(fields):
        line_before = roll(layer_before, -lz * x) if x < lx else corners[Y_BEHIND]
        line_after = roll(layer[Y_AHEAD], -lz * (x + 1)) if x < lx else roll(corners[Y_AHEAD], -2 * lz)
        results.append(
            w.whole(value, parts[x], dims) + from_behind[x] + from_ahead[x]
            + y_behind(parts[x][Y_BEHIND], line_before, dims) + y_ahead(parts[x][Y_AHEAD], line_after, dims)
        )
    if further is None:
        return results
    lane = lane_index(width)
    side = (
        w.whole(ya, layer, dims)
        + jnp.where(lane < lz, roll(w.one(corner_before, X_BEHIND), lz), roll(layer[X_BEHIND], lz))
        + jnp.where(lane >= width - lz, roll(corners[X_AHEAD], -2 * lz), roll(layer[X_AHEAD], -lz))
        + y_layer([p[Y_BEHIND] for p in parts[:lx]], dims, ly - 1) + w.one(layer_next, Y_AHEAD)
    )
    return results, side


def pair_sums(left, right, q):
    return three(halves(left), stacked([halves(right), q]), (1, 1))


def inner_sums(dims, fields, layer, mean):
    lx, ly, lz = dims
    rank = mean.shape[0]
    speeds = [speed_of(mean, f) for f in fields]
    split = [halves(f) for f in fields]
    sums = [jnp.zeros((rank, 2 * rank), jnp.float32) for _ in range(4)]
    for x in range(lx):
        k = fields[x]
        q = halves(speeds[x] * k)
        pairs = [(0, split[x], split[x])]
        if x + 1 < len(fields):
            pairs.append((1, split[x + 1], halves(speeds[x + 1] * k)))
        for n, moved in ((2, y_ahead(k, roll(layer, -lz * (x + 1)), dims)), (3, z_ahead(k, dims))):
            pairs.append((n, halves(moved), halves(speed_of(mean, moved) * k)))
        for n, left, right in pairs:
            sums[n] = sums[n] + three(left, stacked([right, q]), (1, 1))
    return sums


def packed_sums(sums):
    rank = sums[0].shape[0]
    low = lane_index(2 * rank) < rank
    centre = jnp.where(low, -roll(sums[0], rank), sums[0])
    gram = sums[0][:, :rank]
    rows = [jnp.concatenate([gram[:rank // 2], gram[rank // 2:]], axis=1)]
    for part in sums[1:]:
        rows.append(centre + jnp.where(low, part, -part))
    return jnp.concatenate(rows, axis=0)


def write_slabs(ref, slabs):
    slab = slabs[0].shape[1]
    for x, value in enumerate(slabs):
        ref[:, x * slab:(x + 1) * slab] = value


def edge_kernel(dims, first, layers, xb, xa, yb, ya, weight_ref, column_ref, first_ref, y_first_ref):
    first_ref[...], y_first_ref[...] = k_edges(
        dims, first[...], layers[...], weight_ref[...], column_ref[...], xb[...], xa[...], yb[...], ya[...]
    )


def first_kernel(
    dims, field_ref, xb, xa, yb, ya, weight_ref, column_ref, mean_ref, out_ref, sums_ref, last_ref, y_last_ref
):
    slabs = k_stage(
        dims, field_ref[...], weight_ref[...], column_ref[...], xb[...], xa[...], yb[...], ya[...]
    )
    write_slabs(out_ref, slabs)
    last_ref[...], y_last_ref[...] = slabs[-1], y_layer(slabs, dims, dims[1] - 1)
    none = jnp.zeros(y_last_ref.shape, jnp.float32)
    sums_ref[...] = jnp.concatenate(inner_sums(dims, slabs, none, mean_ref[...]), axis=0)


def face_kernel(dims, sums_ref, last_ref, y_last_ref, xa, ya, mean_ref, part_ref, up_ref):
    slab, width = dims[1] * dims[2], dims[0] * dims[2]
    mean = mean_ref[...]
    rank = mean.shape[0]
    layer = ya[:, :width]
    sums = [sums_ref[n * rank:(n + 1) * rank] for n in range(4)]
    for n, moved, k in ((1, xa[...], last_ref[...]), (2, layer, y_last_ref[...])):
        sums[n] = sums[n] + pair_sums(moved, speed_of(mean, moved) * k, halves(speed_of(mean, k) * k))
    part_ref[...] = packed_sums(sums)
    up_ref[:, :slab] = last_ref[...]
    up_ref[:, slab:] = layer


def pack_kernel(dims, field_ref, ya, yb, down_ref):
    lx, ly, lz = dims
    slab, width = ly * lz, lx * lz
    down_ref[:, :slab] = field_ref[:, slab:2 * slab]
    down_ref[:, slab:] = jnp.where(lane_index(width) < lz, yb[...], roll(ya[:, :width], lz))


def apply(left, right):
    left_high, left_low = halves(left)
    high, low = halves(right)
    return dot(
        jnp.concatenate([left_high, left_high, left_low], axis=1), jnp.concatenate([high, low, high], axis=0)
    )


def orient_stage(cells, sums, orient, table, mean, directions, basis=None):
    rank = orient.shape[0]
    plus, minus = signs(directions)
    sums = sums * (1.0 / cells)
    gram = jnp.concatenate([sums[:rank // 2, :rank], sums[:rank // 2, rank:]], axis=0)
    inner = []
    for d in range(3):
        block = sums[rank // 2 + d * rank:rank // 2 + (d + 1) * rank]
        inner += [-block[:, rank:], block[:, :rank].T]
    drift = -mm(jnp.concatenate(inner, axis=1), table)
    upper, inverse, drift = factor(gram, drift)
    spread = jnp.broadcast_to(mean, (rank, rank))
    solved = (1.0 + tumble) * unit(rank) - tumble * spread * spread.T + courant * mm(inverse, drift, (0, 0))
    rows = [(1.0 - tumble) * upper] + [courant * mm(inverse, part) for part in inner]
    rows = apply(jnp.concatenate(rows, axis=0), solved)
    mid_mean = mm(rows[:rank], spread)[:, :1]
    moved = apply(rows if basis is None else apply(rows, basis), orient)
    new = moved[:rank] + mid_mean * (tumble / (1.0 - tumble))
    for d in range(3):
        new = new + plus[d:d + 1] * moved[(1 + 2 * d) * rank:(2 + 2 * d) * rank]
        new = new + minus[d:d + 1] * moved[(2 + 2 * d) * rank:(3 + 2 * d) * rank]
    return inverse, new


def turn_kernel(
    cells, sums_ref, orient_ref, table_ref, mean_ref, e_ref,
    weight_ref, column_ref, mean_out, new_ref, inverse_ref, table_out,
):
    directions = e_ref[...]
    rank = orient_ref.shape[0]
    inverse, new = orient_stage(cells, sums_ref[...], orient_ref[...], table_ref[...], mean_ref[...], directions)
    new_ref[...] = new
    gram, table, mean = tables(new, directions)
    weights, column_ref[...] = stage_weights(gram, table, mean, inverse)
    _, inverse_v = factor(gram)
    inverse_ref[...] = inverse_v
    weight_ref[...] = mm(inverse_v, weights)
    mean_out[...] = mm(inverse_v, jnp.broadcast_to(mean, (rank, rank)))[:, :1]
    right = mm(table, inverse_v, (1, 1))
    for n in range(6):
        table_out[n * rank:(n + 1) * rank] = mm(inverse_v, right[n * rank:(n + 1) * rank])


def second_kernel(
    dims, field_ref, xa, ya, yb, second, behind, weight_ref, column_ref, mean_ref, field_out, sums_out
):
    slab, width = dims[1] * dims[2], dims[0] * dims[2]
    slabs, side = k_stage(
        dims, field_ref[...], weight_ref[...], column_ref[...], behind[:, :slab], xa[...], yb[...], ya[:, :width],
        (second[...], behind[:, slab:], ya[:, width:]),
    )
    write_slabs(field_out, slabs[:-1])
    sums_out[...] = packed_sums(inner_sums(dims, slabs, side, mean_ref[...]))


def last_kernel(
    cells, sums_ref, orient_ref, basis_ref, table_ref, mean_ref, e_ref, field_ref, x_ref, s_ref, v_ref, x_buffer, v_buffer, sems
):
    inverse, new = orient_stage(
        cells, sums_ref[...], orient_ref[...], table_ref[...], mean_ref[...], e_ref[...], basis_ref[...]
    )
    count = new.shape[1]
    parts = v_buffer.shape[0]
    chunk = field_ref.shape[1] // parts

    copies = [
        pltpu.make_async_copy(
            x_buffer.at[pl.ds(n * chunk, chunk)], x_ref.at[pl.ds(n * chunk, chunk)], sems.at[n]
        )
        for n in range(parts)
    ]

    def x_part(n):
        def work():
            x_buffer[n * chunk:(n + 1) * chunk] = apply(inverse, field_ref[:, n * chunk:(n + 1) * chunk]).T
            copies[n].start()
        return work

    new_halves = halves(new)
    upper_v, inverse_v = factor(
        three(new_halves, new_halves, (1, 1)) * (1.0 / count), meanwhile=[x_part(n) for n in range(parts)]
    )
    s_ref[...] = upper_v.T
    wide = count // parts
    for n in range(parts):
        v_buffer[n] = apply(inverse_v, new[:, n * wide:(n + 1) * wide])
        copies.append(
            pltpu.make_async_copy(v_buffer.at[n], v_ref.at[:, pl.ds(n * wide, wide)], sems.at[parts + n])
        )
        copies[-1].start()
    for copy in copies:
        copy.wait()


def shifted(axis, up):
    count = lax.axis_size(axis)
    step = 1 if up else count - 1
    return [(i, (i + step) % count) for i in range(count)]


def scatter_gather_sum(part):
    count = lax.axis_size("gx") * lax.axis_size("gy")
    rows, width = part.shape
    padded = -(-rows // count) * count
    if padded != rows:
        part = jnp.pad(part, ((0, padded - rows), (0, 0)))
    split = part.reshape(count, padded // count, width)
    mine = lax.all_to_all(split, ("gx", "gy"), 0, 0).sum(axis=0)
    every = lax.all_to_all(jnp.broadcast_to(mine[None], split.shape), ("gx", "gy"), 0, 0)
    return every.reshape(padded, width)[:rows]


def swapped(value, bits):
    count = lax.axis_size("gx") * lax.axis_size("gy")
    return lax.ppermute(value, ("gx", "gy"), [(i, i ^ bits) for i in range(count)])


def sum_of_four(value, step):
    near, far, cross = [swapped(value, n * step) for n in (1, 2, 3)]
    return (value + near) + (far + cross)


def all_sum(part, meanwhile=(lambda value: value,) * 2):
    nx, ny = lax.axis_size("gx"), lax.axis_size("gy")
    rows = part.shape[0] // 2
    if nx != 4 or ny != 8 or rows % 8:
        for work in meanwhile:
            part = work(part)
        return scatter_gather_sum(part)
    first = lax.axis_index("gy") % 2 == 0
    total = part + swapped(part, 1)
    mine = jnp.where(first, total[:rows], total[rows:])
    for step, work in zip((ny, 2), meanwhile):
        mine = work(sum_of_four(mine, step))
    other = swapped(mine, 1)
    return jnp.concatenate([jnp.where(first, mine, other), jnp.where(first, other, mine)], axis=0)


def up(value, axis):
    return lax.ppermute(value, axis, shifted(axis, True))


def down(value, axis):
    return lax.ppermute(value, axis, shifted(axis, False))


def shards(spatial_factor, coupling, orient_factor, directions):
    dims = spatial_factor.shape[:3]
    lx, ly, lz = dims
    rank = spatial_factor.shape[-1]
    sites = lx * ly * lz
    count = orient_factor.shape[0]
    cells = sites * lax.axis_size("gx") * lax.axis_size("gy")
    whole, slab, layer = (rank, sites), (rank, ly * lz), (rank, lx * lz)
    two_layers, more = (rank, 2 * lx * lz), (rank, ly * lz + lx * lz)
    summed = (7 * rank // 2, 2 * rank)
    field, first, last, y_first, y_last = call(
        functools.partial(enter_kernel, dims), [whole, slab, slab, layer, layer], spatial_factor.reshape(sites, rank)
    )
    xb, xa, yb, ya = up(last, "gx"), down(first, "gx"), up(y_last, "gy"), down(y_first, "gy")
    basis = [(rank, count), (6 * rank, rank)]
    column_shape, weight_shape = (rank, 1), (rank, 8 * rank)
    orient = orient_factor.T
    table, mean, weights, column, first, y_first = call(
        functools.partial(table_kernel, dims), [basis[1], column_shape, weight_shape, column_shape, slab, two_layers],
        orient, directions, coupling, field,
    )
    near = (field, xb, xa, yb, ya, weights, column)
    first, y_first = call(
        functools.partial(edge_kernel, dims), [slab, two_layers], first, y_first, *near[1:]
    )
    xa, ya = down(first, "gx"), down(y_first, "gy")
    field, part, last, y_last = call(
        functools.partial(first_kernel, dims), [whole, (4 * rank, 2 * rank), slab, layer], *near, mean,
        cost=pl.CostEstimate(flops=10**9, bytes_accessed=8 * 10**6, transcendentals=0),
    )
    part, behind = call(
        functools.partial(face_kernel, dims), [summed, more], part, last, y_last, xa, ya, mean
    )
    yb, behind = up(y_last, "gy"), up(behind, "gx")
    halo = {"yb": yb, "behind": behind}

    def with_layer(value):
        value, halo["yb"] = lax.optimization_barrier((value, halo["yb"]))
        (packed,) = call(functools.partial(pack_kernel, dims), [more], field, ya, halo["yb"])
        halo["second"] = down(packed, "gx")
        return value

    sums = all_sum(part, (with_layer, lambda value: value))
    weights, column, mean, new, inverse, table = call(
        functools.partial(turn_kernel, cells),
        [weight_shape, column_shape, column_shape, basis[0], (rank, rank), basis[1]],
        sums, orient, table, mean, directions, cost=pl.CostEstimate(flops=1, bytes_accessed=1, transcendentals=0),
    )
    field, part = call(
        functools.partial(second_kernel, dims), [whole, summed],
        field, xa, ya, halo["yb"], halo["second"], halo["behind"], weights, column, mean,
    )
    new_spatial, new_coupling, new_orient = call(
        functools.partial(last_kernel, cells), [(sites, rank), (rank, rank), (rank, count)],
        all_sum(part), new, inverse, table, mean, directions, field, far_out=(0, 2),
        scratch=(
            pltpu.VMEM((sites, rank), jnp.float32),
            pltpu.VMEM((4, rank, count // 4), jnp.float32),
            pltpu.SemaphoreType.DMA((8,)),
        ),
    )
    return new_spatial.reshape(spatial_factor.shape), new_coupling, new_orient.T


def solution(mesh):
    return jax.shard_map(
        shards,
        mesh=mesh,
        in_specs=(P("gx", "gy", None, None), P(), P(), P()),
        out_specs=(P("gx", "gy", None, None), P(), P()),
        check_vma=False,
    )
```
